128 devices in a mesh: row: 8 (over y, z_lo), col: 16 (over z_hi, x, core).
Axes of the slice: x: 4, y: 4, z: 4 (z_hi: 2, z_lo: 2; z = z_hi * 2 + z_lo), core: 2. Of those that a mesh axis runs over, the one named last changes fastest.
Arguments:
- initial_kelvin_state: float32 [8, 1024, 2048], P(None, 'row', 'col'), may hold values from -6 to 6
- substance_region: int32 [8, 1024, 2048], P(None, 'row', 'col'), may hold values from 0 to 2, as said below
- source_energy: float32 [8, 1024, 2048], P(None, 'row', 'col'), may hold values from 0.2 to 5
- substance_transfer_magnitude: float32 [3], replicated, may hold values from 0.02 to 6, as said below
- substance_softening_rate: float32 [3], replicated, may hold values from 0.05 to 0.25
Outputs:
- new_temperature: float32 [8, 1024, 2048], P(None, 'row', 'col')
The draws below stay inside these ranges and needn't reach their ends.
Inputs may be any that keep to these rules, and one draw needn't show every extreme that they name: `substance_region`: 0 die, 1 thermal interface material, 2 spreader. `substance_transfer_magnitude`: positive conductivity scales of die, interface material and spreader, in that order.
All inputs are finite; a program needn't handle non-finite values.
Results may differ from the reference program's by a relative error of at most 0.0027.
Values sent between devices are 32-bit elements; how exact they have to be, the bound alone decides.
No kernel may reach another device: no remote copies, remote signals or barrier semaphores. Data moves between devices by JAX's collectives and lax.ppermute only.
A program may use at most 192 MiB of HBM per device.

```python
import math
import jax
import jax.numpy as jnp
from jax import lax

NODES_THROUGH = 8
NODES_ACROSS = 2048
NODES_DOWNWARD = 1024


def draw_substance_region(key, part):
    rolled = jax.random.randint(key, (NODES_THROUGH, NODES_DOWNWARD, NODES_ACROSS), 0, 10)
    layer = lax.broadcasted_iota(jnp.int32, (NODES_THROUGH, NODES_DOWNWARD, NODES_ACROSS), 0)
    spreader_cells = jnp.where(rolled < 2, 0, 2)
    interface_cells = jnp.where(rolled < 1, 0, 1)
    die_cells = jnp.where(rolled < 2, 2, 0)
    middle = NODES_THROUGH // 2
    return jnp.where(layer < middle, spreader_cells, jnp.where(layer == middle, interface_cells, die_cells)).astype(jnp.int32)


def draw_substance_transfer_magnitude(key, part):
    lowest = jnp.array([0.8, 0.02, 2.0], jnp.float32)
    highest = jnp.array([2.5, 0.08, 6.0], jnp.float32)
    fraction = jax.random.uniform(key, (3,), jnp.float32)
    return lowest * jnp.exp(fraction * jnp.log(highest / lowest))


def levels(own_key, shape, cuts, smallest, largest):
    gain = 1.0
    for dim, shards_of in cuts:
        steps = jax.random.uniform(jax.random.fold_in(jax.random.fold_in(own_key, 6), dim), (shards_of,), jnp.float32, smallest / len(cuts), largest / len(cuts))
        gain = gain * jnp.repeat(jnp.exp(steps), shape[dim] // shards_of).reshape((-1,) + (1,) * (len(shape) - 1 - dim))
    return gain


def gaussian(own_key, dims, scale, bound, shards=(), kind=jnp.bfloat16):
    entries = jax.random.normal(own_key, dims, jnp.float32) * scale
    if len(shards) > 0:
        entries = levels(own_key, dims, shards, -0.22, 0.18) * entries
    return jnp.clip(entries, min=-bound, max=bound).astype(kind)


def setup_inputs(seed: int = 0) -> dict:
    keys = jax.random.split(jax.random.key(seed), 6)
    initial_kelvin_state = gaussian(keys[0], (NODES_THROUGH, NODES_DOWNWARD, NODES_ACROSS), 1.0, 6.0, ((1, 8), (2, 16)), jnp.float32)
    substance_region = draw_substance_region(jax.random.fold_in(keys[5], 71), 0)
    source_energy = jnp.clip(jnp.exp(math.log(5.0) - 3.218876 * jax.random.uniform(keys[2], (NODES_THROUGH, NODES_DOWNWARD, NODES_ACROSS), jnp.float32) ** levels(keys[2], (NODES_THROUGH, NODES_DOWNWARD, NODES_ACROSS), ((1, 8), (2, 16)), -0.2, 0.2)), 0.2, 5.0)
    substance_transfer_magnitude = draw_substance_transfer_magnitude(jax.random.fold_in(keys[5], 71), 0)
    substance_softening_rate = jnp.clip(jax.random.uniform(keys[4], (3,), jnp.float32, 0.05, 0.25), 0.05, 0.25)
    return dict(initial_kelvin_state=initial_kelvin_state, substance_region=substance_region, source_energy=source_energy, substance_transfer_magnitude=substance_transfer_magnitude, substance_softening_rate=substance_softening_rate)


inplane_ratio = 1000.0
depth_ratio = 0.08


def transfer_coefficient_array(initial_kelvin_state, substance_region, substance_transfer_magnitude, substance_softening_rate):
    nodal_transfer_coefficient = jnp.where(substance_region == 0, substance_transfer_magnitude[0], jnp.where(substance_region == 1, substance_transfer_magnitude[1], substance_transfer_magnitude[2]))
    nodal_thermal_softening = jnp.where(substance_region == 0, substance_softening_rate[0], jnp.where(substance_region == 1, substance_softening_rate[1], substance_softening_rate[2]))
    return nodal_transfer_coefficient * jnp.exp(-nodal_thermal_softening * initial_kelvin_state)


def face_conductance(center, beside):
    return 2.0 * center * beside / (center + beside)


def forward_diffusion_parts(field_padded, cond_padded):
    field_center = field_padded[:, 1:-1, 1:-1]
    cond_center = cond_padded[:, 1:-1, 1:-1]

    def flux(field_beside, cond_beside):
        return face_conductance(cond_center, cond_beside) * (field_beside - field_center)

    implicit_pass_first_axis = inplane_ratio * (flux(field_padded[:, 1:-1, 2:], cond_padded[:, 1:-1, 2:]) + flux(field_padded[:, 1:-1, :-2], cond_padded[:, 1:-1, :-2]))
    implicit_pass_second_axis = inplane_ratio * (flux(field_padded[:, 2:, 1:-1], cond_padded[:, 2:, 1:-1]) + flux(field_padded[:, :-2, 1:-1], cond_padded[:, :-2, 1:-1]))
    field_layers = jnp.pad(field_center, ((1, 1), (0, 0), (0, 0)))
    cond_layers = jnp.pad(cond_center, ((1, 1), (0, 0), (0, 0)))
    implicit_pass_third_axis = depth_ratio * (flux(field_layers[2:], cond_layers[2:]) + flux(field_layers[:-2], cond_layers[:-2]))
    bottom = (lax.broadcasted_iota(jnp.int32, field_center.shape, 0) == 0).astype(field_center.dtype)
    implicit_pass_third_axis = implicit_pass_third_axis - depth_ratio * bottom * cond_center * field_center
    return implicit_pass_first_axis, implicit_pass_second_axis, implicit_pass_third_axis


def line_system(cond_lines, line_axis, ratio):
    length = cond_lines.shape[line_axis]
    plate_thicknesses = [(0, 0)] * cond_lines.ndim
    plate_thicknesses[line_axis] = (1, 1)
    cond_padded = jnp.pad(cond_lines, plate_thicknesses)
    before = lax.slice_in_dim(cond_padded, 0, length, axis=line_axis)
    after = lax.slice_in_dim(cond_padded, 2, length + 2, axis=line_axis)
    lower_band = -0.5 * ratio * face_conductance(cond_lines, before)
    upper_band = -0.5 * ratio * face_conductance(cond_lines, after)
    main_band = 1.0 - lower_band - upper_band
    return lower_band, main_band, upper_band


def append_slab(values, filler, line_axis):
    slab_shape = list(values.shape)
    slab_shape[line_axis] = 1
    return jnp.concatenate([values, jnp.full(slab_shape, filler, values.dtype)], line_axis)


def prepend_slab(values, filler, line_axis):
    slab_shape = list(values.shape)
    slab_shape[line_axis] = 1
    return jnp.concatenate([jnp.full(slab_shape, filler, values.dtype), values], line_axis)


def reduce_solve(lower_band, main_band, upper_band, right_side, line_axis):
    length = right_side.shape[line_axis]
    if length == 1:
        return right_side / main_band
    if length % 2 == 1:
        lower_band = append_slab(lower_band, 0.0, line_axis)
        main_band = append_slab(main_band, 1.0, line_axis)
        upper_band = append_slab(upper_band, 0.0, line_axis)
        right_side = append_slab(right_side, 0.0, line_axis)
    padded_length = right_side.shape[line_axis]
    half_length = padded_length // 2

    def evens(values):
        return lax.slice_in_dim(values, 0, padded_length, 2, line_axis)

    def odds(values):
        return lax.slice_in_dim(values, 1, padded_length, 2, line_axis)

    def following(values, filler):
        return append_slab(lax.slice_in_dim(evens(values), 1, half_length, axis=line_axis), filler, line_axis)

    left_factor = -odds(lower_band) / evens(main_band)
    right_factor = -odds(upper_band) / following(main_band, 1.0)
    new_lower = left_factor * evens(lower_band)
    new_upper = right_factor * following(upper_band, 0.0)
    new_main = odds(main_band) + left_factor * evens(upper_band) + right_factor * following(lower_band, 0.0)
    new_right = odds(right_side) + left_factor * evens(right_side) + right_factor * following(right_side, 0.0)
    odd_values = reduce_solve(new_lower, new_main, new_upper, new_right, line_axis)
    earlier = prepend_slab(lax.slice_in_dim(odd_values, 0, half_length - 1, axis=line_axis), 0.0, line_axis)
    even_values = (evens(right_side) - evens(lower_band) * earlier - evens(upper_band) * odd_values) / evens(main_band)
    joined_shape = list(right_side.shape)
    joined = jnp.stack([even_values, odd_values], line_axis + 1).reshape(joined_shape)
    return lax.slice_in_dim(joined, 0, length, axis=line_axis)


def reference(initial_kelvin_state, substance_region, source_energy, substance_transfer_magnitude, substance_softening_rate):
    transfer_coefficient_volume = transfer_coefficient_array(initial_kelvin_state, substance_region, substance_transfer_magnitude, substance_softening_rate)
    plate_thicknesses = ((0, 0), (1, 1), (1, 1))
    implicit_pass_first_axis, implicit_pass_second_axis, implicit_pass_third_axis = forward_diffusion_parts(jnp.pad(initial_kelvin_state, plate_thicknesses), jnp.pad(transfer_coefficient_volume, plate_thicknesses))
    first_boundary_face = initial_kelvin_state + 0.5 * implicit_pass_first_axis + implicit_pass_second_axis + implicit_pass_third_axis + source_energy

    def solve_rows(pieces):
        cond_layer, side_layer = pieces
        lower_band, main_band, upper_band = line_system(cond_layer, 1, inplane_ratio)
        return reduce_solve(lower_band, main_band, upper_band, side_layer, 1)

    def solve_columns(pieces):
        cond_layer, side_layer = pieces
        lower_band, main_band, upper_band = line_system(cond_layer, 0, inplane_ratio)
        return reduce_solve(lower_band, main_band, upper_band, side_layer, 0)

    half_step = lax.map(solve_rows, (transfer_coefficient_volume, first_boundary_face))
    second_side = half_step - 0.5 * implicit_pass_second_axis
    return lax.map(solve_columns, (transfer_coefficient_volume, second_side))
```

```python
import jax
import jax.numpy as jnp
from jax import lax
from jax.experimental import pallas as pl
from jax.experimental.pallas import tpu as pltpu
from jax.sharding import PartitionSpec as P

Z, N = 8, 128
ROWS = Z * N
CHUNKS, STEP = 8, 16
F32 = jnp.float32
VM = pltpu.VMEM


def rcp(x):
    r = pl.reciprocal(x, approx=True)
    return r * (2.0 - x * r)


def link(a, b):
    return a * b * rcp(a + b)


def at(i):
    return pl.ds(pl.multiple_of(i * Z, Z), Z)


def strided(i):
    return pl.ds(i, Z, stride=N)


def conductivity(t, reg, mag, soft):
    m = jnp.where(reg == 0, mag[0] * 1000.0, jnp.where(reg == 1, mag[1] * 1000.0, mag[2] * 1000.0))
    b = jnp.where(reg == 0, soft[0], jnp.where(reg == 1, soft[1], soft[2]))
    return m * jnp.exp(-(b * t))


def turn(src, dst):
    def body(z, _):
        lines = pl.ds(z, N, stride=Z)
        dst[lines, :] = src[lines, :].T
        return 0

    lax.fori_loop(0, Z, body, 0, unroll=2)


def factor(c_ref, pr_ref, gr_ref, rr_ref, sep_ref, net_ref):
    one = jnp.ones((Z, N), F32)
    zero = jnp.zeros((Z, N), F32)

    def cell(c, j, p, t, s, here):
        i = c * STEP + j
        beyond = c_ref[at(i + 1), :]
        g = link(here, beyond)
        r = rcp(p + g + t)
        pr, gr = p * r, g * r
        pr_ref[at(i), :] = pr
        gr_ref[at(i), :] = gr
        rr_ref[at(i), :] = r
        return pr * g, 1.0 + gr * t, s + pr * t, beyond

    start = []
    for c in range(CHUNKS):
        here = c_ref[at(c * STEP + 1), :]
        start.append((link(c_ref[at(c * STEP), :], here), one, zero, here))

    def body(j, state):
        return [cell(c, j, *state[c]) for c in range(CHUNKS)]

    state = lax.fori_loop(1, STEP - 1, body, start)
    state = [cell(c, STEP - 1, *state[c]) for c in range(CHUNKS - 1)] + [state[-1]]
    q = state[0][0]
    left = 1.0 + state[0][2]
    t = state[0][1] + state[1][2]
    for c in range(1, CHUNKS):
        g = state[c][0]
        r = rcp(q + g + t)
        qr, gr = q * r, g * r
        sep_ref[0, c] = qr
        sep_ref[1, c] = gr
        sep_ref[2, c] = r
        left = left + qr * t
        t = state[c][1] + gr * t
        if c + 1 < CHUNKS:
            t = t + state[c + 1][2]
        q = qr * g
    net_ref[0] = q
    net_ref[1] = left
    net_ref[2] = t
    net_ref[3] = c_ref[at(0), :]
    net_ref[4] = c_ref[at(N - 1), :]


def sweep(rhs, pr_ref, gr_ref, rr_ref, sep_ref, net_ref, rd_ref, srd_ref, out_ref):
    def cell(c, j, d, s):
        i = c * STEP + j
        rd_ref[at(i), :] = rr_ref[at(i), :] * d
        return rhs(i + 1) + gr_ref[at(i), :] * d, s + pr_ref[at(i), :] * d

    def body(j, state):
        return [cell(c, j, *state[c]) for c in range(CHUNKS)]

    start = [(rhs(c * STEP + 1), jnp.zeros((Z, N), F32)) for c in range(CHUNKS)]
    state = lax.fori_loop(1, STEP - 1, body, start)
    state = [cell(c, STEP - 1, *state[c]) for c in range(CHUNKS - 1)] + [state[-1]]
    left = rhs(0) + state[0][1]
    d = state[0][0] + state[1][1]
    for c in range(1, CHUNKS):
        left = left + sep_ref[0, c] * d
        srd_ref[c] = sep_ref[2, c] * d
        d = state[c][0] + sep_ref[1, c] * d
        if c + 1 < CHUNKS:
            d = d + state[c + 1][1]
    out_ref[0] = net_ref[0]
    out_ref[1] = net_ref[1]
    out_ref[2] = net_ref[2]
    out_ref[3] = left
    out_ref[4] = d
    out_ref[5] = net_ref[3]
    out_ref[6] = net_ref[4]


def back(ul, ur, pr_ref, gr_ref, rd_ref, sep_ref, srd_ref, put):
    seps = [None] * CHUNKS + [ur]
    for c in range(CHUNKS - 1, 0, -1):
        seps[c] = srd_ref[c] + sep_ref[0, c] * ul + sep_ref[1, c] * seps[c + 1]
    seps[0] = ul
    for c in range(CHUNKS):
        put(c * STEP, seps[c])
    put(N - 1, ur)

    def cell(c, j, u):
        i = c * STEP + j
        v = rd_ref[at(i), :] + pr_ref[at(i), :] * seps[c] + gr_ref[at(i), :] * u
        put(i, v)
        return v

    state = [cell(c, STEP - 1, seps[c + 1]) for c in range(CHUNKS - 1)] + [ur]

    def body(k, state):
        return [cell(c, STEP - 2 - k, state[c]) for c in range(CHUNKS)]

    lax.fori_loop(0, STEP - 2, body, state)


def joined(own, other, left):
    a = [jnp.where(left, own[k], other[k]) for k in range(7)]
    b = [jnp.where(left, other[k], own[k]) for k in range(7)]
    between = link(a[6], b[5])
    r = rcp(a[0] + between + a[2])
    f, h = a[0] * r, between * r
    g1 = f * between
    s1 = b[1] + h * a[2]
    d1 = b[3] + h * a[4]
    left_s = a[1] + f * a[2]
    left_d = a[3] + f * a[4]
    r = rcp(g1 + b[0] + s1)
    f, h = g1 * r, b[0] * r
    return [f * b[0], left_s + f * s1, b[2] + h * s1, left_d + f * d1, b[4] + h * d1, a[5], b[6]]


def ends(me, levels, owns, others):
    zero = jnp.zeros((Z, N), F32)
    yl = il = yr = ir = zero
    for k in reversed(range(levels)):
        p, m = others[k], owns[k]
        left = (me >> k) % 2 == 1
        far_s = jnp.where(left, p[1] + yl, p[2] + yr)
        far_d = jnp.where(left, p[3] + il, p[4] + ir)
        near_s = jnp.where(left, p[2], p[1])
        near_d = jnp.where(left, p[4], p[3])
        between = jnp.where(left, link(p[6], m[5]), link(p[5], m[6]))
        f = p[0] * rcp(p[0] + far_s)
        s, d = near_s + f * far_s, near_d + f * far_d
        f = between * rcp(between + s)
        y, i = f * s, f * d
        yl, il = jnp.where(left, y, yl), jnp.where(left, i, il)
        yr, ir = jnp.where(left, yr, y), jnp.where(left, ir, i)
    m = owns[0]
    sl, dl, sr, dr = m[1] + yl, m[3] + il, m[2] + yr, m[4] + ir
    r = rcp(m[0] + sl)
    f = m[0] * r
    ur = (dr + f * dl) * rcp(sr + f * sl)
    ul = (dl + m[0] * ur) * r
    return ul, ur


def edge_kernel(t_ref, reg_ref, mag, soft, up_ref, down_ref):
    for row, out in ((0, up_ref), (N - 1, down_ref)):
        t = t_ref[strided(row), :]
        out[0] = t
        out[1] = conductivity(t, reg_ref[strided(row), :], mag, soft)


def first_kernel(
    t_ref, reg_ref, s_ref, mag, soft,
    ty_ref, cy_ref, r_ref, pr_ref, gr_ref, rr_ref, sep_ref, net_ref, cx_ref,
):
    z = lax.broadcasted_iota(jnp.int32, (Z, N), 0)
    inner = jnp.where(z < Z - 1, 1.6e-4, 0.0)
    ground = jnp.where(z == 0, 8e-5, 0.0)

    def load(y):
        t = t_ref[strided(y), :]
        c = conductivity(t, reg_ref[strided(y), :], mag, soft)
        ty_ref[at(y), :] = t
        cy_ref[at(y), :] = c
        return t, c

    def row(y, t, c, before, after):
        flux = link(c, pltpu.roll(c, Z - 1, 0)) * (pltpu.roll(t, Z - 1, 0) - t) * inner
        up = flux - pltpu.roll(flux, 1, 0) - ground * (c * t)
        r_ref[at(y), :] = 2.0 * t + s_ref[strided(y), :] + 2.0 * (after - before) + up

    def body(k, state):
        t, c, before = state
        for j in range(8):
            y = k * 8 + j
            tn, cn = load(y + 1)
            after = link(c, cn) * (tn - t)
            row(y, t, c, before, after)
            t, c, before = tn, cn, after
        return t, c, before

    t, c = load(0)
    state = lax.fori_loop(0, N // 8 - 1, body, (t, c, jnp.zeros((Z, N), F32)))
    t, c, before = state
    for y in range(N - 8, N - 1):
        tn, cn = load(y + 1)
        after = link(c, cn) * (tn - t)
        row(y, t, c, before, after)
        t, c, before = tn, cn, after
    row(N - 1, t, c, before, jnp.zeros((Z, N), F32))
    turn(cy_ref, cx_ref)
    factor(cx_ref, pr_ref, gr_ref, rr_ref, sep_ref, net_ref)


def side_call(
    r_ref, ty_ref, cy_ref, north_ref, south_ref, pr_ref, gr_ref, rr_ref, sep_ref, net_ref,
    rd_ref, srd_ref, out_ref, rx_ref, ry_ref,
):
    me = lax.axis_index("row")
    ry_ref[...] = r_ref[...]
    for row, halo, there in ((0, north_ref, me > 0), (N - 1, south_ref, me < lax.axis_size("row") - 1)):
        i = slice(row * Z, row * Z + Z)
        flux = link(cy_ref[i, :], halo[1]) * (halo[0] - ty_ref[i, :])
        ry_ref[i, :] = r_ref[i, :] + jnp.where(there, 2.0 * flux, 0.0)
    turn(ry_ref, rx_ref)
    sweep(
        lambda i: rx_ref[at(i), :],
        pr_ref, gr_ref, rr_ref, sep_ref, net_ref, rd_ref, srd_ref, out_ref,
    )


def merge_kernel(axis, level, own_ref, other_ref, out_ref):
    left = (lax.axis_index(axis) >> level) % 2 == 0
    new = joined([own_ref[k] for k in range(7)], [other_ref[k] for k in range(7)], left)
    for k in range(7):
        out_ref[k] = new[k]


def middle_kernel(
    levels, *refs,
):
    owns, others, refs = refs[:levels], refs[levels : 2 * levels], refs[2 * levels :]
    (
        pr_ref, gr_ref, rd_ref, sep_ref, srd_ref, ty_ref,
        ypr_ref, ygr_ref, yrr_ref, ysep_ref, ynet_ref,
        yrd_ref, ysrd_ref, out_ref, wx_ref, wy_ref,
    ) = refs
    ul, ur = ends(lax.axis_index("col"), levels, owns, others)

    def put(i, v):
        wx_ref[at(i), :] = v

    back(ul, ur, pr_ref, gr_ref, rd_ref, sep_ref, srd_ref, put)
    turn(wx_ref, wy_ref)
    sweep(
        lambda i: wy_ref[at(i), :] - 2.0 * ty_ref[at(i), :],
        ypr_ref, ygr_ref, yrr_ref, ysep_ref, ynet_ref, yrd_ref, ysrd_ref, out_ref,
    )


def last_kernel(levels, *refs):
    owns, others, refs = refs[:levels], refs[levels : 2 * levels], refs[2 * levels :]
    pr_ref, gr_ref, rd_ref, sep_ref, srd_ref, ty_ref, out_ref = refs
    ul, ur = ends(lax.axis_index("row"), levels, owns, others)

    def put(i, v):
        out_ref[strided(i), :] = v + ty_ref[at(i), :]

    back(ul, ur, pr_ref, gr_ref, rd_ref, sep_ref, srd_ref, put)


FIELD = (ROWS, N)
NET = (7, Z, N)
PART = (5, Z, N)
SEPS = (3, CHUNKS, Z, N)
SEPD = (CHUNKS, Z, N)


def vm(shape):
    return VM(shape, F32)


def call(kernel, args, outs, scratch=(), scalars=(), flops=0, inplace=None):
    args = [pltpu.with_memory_space_constraint(a, VM) for a in args]
    whole = pl.BlockSpec(memory_space=VM)
    small = pl.BlockSpec(memory_space=pltpu.SMEM)
    many = isinstance(outs, tuple)
    return pl.pallas_call(
        kernel,
        in_specs=[whole] * len(args) + [small] * len(scalars),
        out_specs=(whole,) * len(outs) if many else whole,
        out_shape=outs,
        scratch_shapes=list(scratch),
        cost_estimate=pl.CostEstimate(flops=flops, bytes_accessed=flops, transcendentals=0),
        compiler_params=pltpu.CompilerParams(vmem_limit_bytes=16 * 1024 * 1024),
    )(*args, *scalars)


def partner(x, axis, mask):
    return lax.ppermute(x, axis, [(i, i ^ mask) for i in range(lax.axis_size(axis))])


def spread(net, axis, masks):
    owns, others = [net], []
    for level, mask in enumerate(masks):
        others.append(partner(owns[-1], axis, mask))
        if level + 1 < len(masks):
            owns.append(
                call(
                    lambda *refs, level=level: merge_kernel(axis, level, *refs),
                    [owns[-1], others[-1]],
                    vm(NET),
                )
            )
    return owns, others


def local(t, region, source, mag, soft):
    t, region, source = (a.reshape(FIELD) for a in (t, region, source))
    n = lax.axis_size("row")
    up, down = call(edge_kernel, [t, region], (vm((2, Z, N)), vm((2, Z, N))), scalars=(mag, soft))
    south = lax.ppermute(up, "row", [((i + 1) % n, i) for i in range(n)])
    north = lax.ppermute(down, "row", [(i, (i + 1) % n) for i in range(n)])
    ty, cy, r, pr, gr, rr, sep, net = call(
        first_kernel,
        [t, region, source],
        (vm(FIELD),) * 6 + (vm(SEPS), vm(PART)),
        scratch=[vm(FIELD)],
        scalars=(mag, soft),
        flops=20_000_000,
    )
    rd, srd, own = call(
        side_call,
        [r, ty, cy, north, south, pr, gr, rr, sep, net],
        (vm(FIELD), vm(SEPD), vm(NET)),
        scratch=[vm(FIELD), vm(FIELD)],
    )
    ypr, ygr, yrr, ysep, ynet = call(
        factor, [cy], (vm(FIELD),) * 3 + (vm(SEPS), vm(PART)), flops=5_000_000
    )
    owns, others = spread(own, "col", (1, 2, 6, 8))
    yrd, ysrd, own = call(
        lambda *refs: middle_kernel(4, *refs),
        owns + others + [pr, gr, rd, sep, srd, ty, ypr, ygr, yrr, ysep, ynet],
        (vm(FIELD), vm(SEPD), vm(NET)),
        scratch=[vm(FIELD), vm(FIELD)],
    )
    owns, others = spread(own, "row", (1, 2, 6))
    out = call(
        lambda *refs: last_kernel(3, *refs),
        owns + others + [ypr, ygr, yrd, ysep, ysrd, ty],
        jax.ShapeDtypeStruct(FIELD, F32),
    )
    return out.reshape((Z, N, N))


def solution(mesh):
    specs = (P(None, "row", "col"),) * 3 + (P(), P())
    return jax.shard_map(
        local, mesh=mesh, in_specs=specs, out_specs=P(None, "row", "col"), check_vma=False
    )
```

```python
import jax
import jax.numpy as jnp
from jax import lax
from jax.experimental import pallas as pl
from jax.experimental.pallas import tpu as pltpu
from jax.sharding import PartitionSpec as P

Z, N = 8, 128
ROWS = Z * N
CHUNKS, STEP = 8, 16
F32 = jnp.float32
VM = pltpu.VMEM


def rcp(x):
    r = pl.reciprocal(x, approx=True)
    return r * (2.0 - x * r)


def link(a, b):
    return a * b * rcp(a + b)


def at(i):
    return pl.ds(pl.multiple_of(i * Z, Z), Z)


def strided(i):
    return pl.ds(i, Z, stride=N)


def conductivity(t, reg, mag, soft):
    m = jnp.where(reg == 0, mag[0], jnp.where(reg == 1, mag[1], mag[2]))
    b = jnp.where(reg == 0, soft[0], jnp.where(reg == 1, soft[1], soft[2]))
    return m * jnp.exp(b * t)


def turn(src, dst):
    def body(z, _):
        lines = pl.ds(z, N, stride=Z)
        dst[lines, :] = src[lines, :].T
        return 0

    lax.fori_loop(0, Z, body, 0, unroll=2)


def factor(c_ref, pr_ref, gr_ref, rr_ref, sep_ref, net_ref):
    one = jnp.ones((Z, N), F32)
    zero = jnp.zeros((Z, N), F32)

    def cell(c, j, p, t, s, here):
        i = c * STEP + j
        beyond = c_ref[at(i + 1), :]
        g = link(here, beyond)
        r = rcp(p + g + t)
        pr, gr = p * r, g * r
        pr_ref[at(i), :] = pr
        gr_ref[at(i), :] = gr
        rr_ref[at(i), :] = r
        return pr * g, 1.0 + gr * t, s + pr * t, beyond

    start = []
    for c in range(CHUNKS):
        here = c_ref[at(c * STEP + 1), :]
        start.append((link(c_ref[at(c * STEP), :], here), one, zero, here))

    def body(j, state):
        return [cell(c, j, *state[c]) for c in range(CHUNKS)]

    state = lax.fori_loop(1, STEP - 1, body, start)
    state = [cell(c, STEP - 1, *state[c]) for c in range(CHUNKS - 1)] + [state[-1]]
    q = state[0][0]
    left = 1.0 + state[0][2]
    t = state[0][1] + state[1][2]
    for c in range(1, CHUNKS):
        g = state[c][0]
        r = rcp(q + g + t)
        qr, gr = q * r, g * r
        sep_ref[0, c] = qr
        sep_ref[1, c] = gr
        sep_ref[2, c] = r
        left = left + qr * t
        t = state[c][1] + gr * t
        if c + 1 < CHUNKS:
            t = t + state[c + 1][2]
        q = qr * g
    net_ref[0] = q
    net_ref[1] = left
    net_ref[2] = t
    net_ref[3] = c_ref[at(0), :]
    net_ref[4] = c_ref[at(N - 1), :]


def sweep(rhs, pr_ref, gr_ref, rr_ref, sep_ref, net_ref, rd_ref, srd_ref, out_ref):
    def cell(c, j, d, s):
        i = c * STEP + j
        rd_ref[at(i), :] = rr_ref[at(i), :] * d
        return rhs(i + 1) + gr_ref[at(i), :] * d, s + pr_ref[at(i), :] * d

    def body(j, state):
        return [cell(c, j, *state[c]) for c in range(CHUNKS)]

    start = [(rhs(c * STEP + 1), jnp.zeros((Z, N), F32)) for c in range(CHUNKS)]
    state = lax.fori_loop(1, STEP - 1, body, start)
    state = [cell(c, STEP - 1, *state[c]) for c in range(CHUNKS - 1)] + [state[-1]]
    left = rhs(0) + state[0][1]
    d = state[0][0] + state[1][1]
    for c in range(1, CHUNKS):
        left = left + sep_ref[0, c] * d
        srd_ref[c] = sep_ref[2, c] * d
        d = state[c][0] + sep_ref[1, c] * d
        if c + 1 < CHUNKS:
            d = d + state[c + 1][1]
    out_ref[0] = net_ref[0]
    out_ref[1] = net_ref[1]
    out_ref[2] = net_ref[2]
    out_ref[3] = left
    out_ref[4] = d
    out_ref[5] = net_ref[3]
    out_ref[6] = net_ref[4]


def back(ul, ur, pr_ref, gr_ref, rd_ref, sep_ref, srd_ref, put):
    seps = [None] * CHUNKS + [ur]
    for c in range(CHUNKS - 1, 0, -1):
        seps[c] = srd_ref[c] + sep_ref[0, c] * ul + sep_ref[1, c] * seps[c + 1]
    seps[0] = ul
    for c in range(CHUNKS):
        put(c * STEP, seps[c])
    put(N - 1, ur)

    def cell(c, j, u):
        i = c * STEP + j
        v = rd_ref[at(i), :] + pr_ref[at(i), :] * seps[c] + gr_ref[at(i), :] * u
        put(i, v)
        return v

    state = [cell(c, STEP - 1, seps[c + 1]) for c in range(CHUNKS - 1)] + [ur]

    def body(k, state):
        return [cell(c, STEP - 2 - k, state[c]) for c in range(CHUNKS)]

    lax.fori_loop(0, STEP - 2, body, state)


def joined(own, other, left):
    a = [jnp.where(left, own[k], other[k]) for k in range(7)]
    b = [jnp.where(left, other[k], own[k]) for k in range(7)]
    between = link(a[6], b[5])
    r = rcp(a[0] + between + a[2])
    f, h = a[0] * r, between * r
    g1 = f * between
    s1 = b[1] + h * a[2]
    d1 = b[3] + h * a[4]
    left_s = a[1] + f * a[2]
    left_d = a[3] + f * a[4]
    r = rcp(g1 + b[0] + s1)
    f, h = g1 * r, b[0] * r
    return [f * b[0], left_s + f * s1, b[2] + h * s1, left_d + f * d1, b[4] + h * d1, a[5], b[6]]


def ends(me, levels, owns, others):
    zero = jnp.zeros((Z, N), F32)
    yl = il = yr = ir = zero
    for k in reversed(range(levels)):
        p, m = others[k], owns[k]
        left = (me >> k) % 2 == 1
        far_s = jnp.where(left, p[1] + yl, p[2] + yr)
        far_d = jnp.where(left, p[3] + il, p[4] + ir)
        near_s = jnp.where(left, p[2], p[1])
        near_d = jnp.where(left, p[4], p[3])
        between = jnp.where(left, link(p[6], m[5]), link(p[5], m[6]))
        f = p[0] * rcp(p[0] + far_s)
        s, d = near_s + f * far_s, near_d + f * far_d
        f = between * rcp(between + s)
        y, i = f * s, f * d
        yl, il = jnp.where(left, y, yl), jnp.where(left, i, il)
        yr, ir = jnp.where(left, yr, y), jnp.where(left, ir, i)
    m = owns[0]
    sl, dl, sr, dr = m[1] + yl, m[3] + il, m[2] + yr, m[4] + ir
    r = rcp(m[0] + sl)
    f = m[0] * r
    ur = (dr + f * dl) * rcp(sr + f * sl)
    ul = (dl + m[0] * ur) * r
    return ul, ur


def edge_kernel(
    t_hbm, reg_hbm, s_hbm, mag_hbm, soft_hbm,
    t_ref, reg_ref, s_ref, up_ref, down_ref, par_ref, mag_ref, soft_ref, sem,
):
    pairs = (
        (mag_hbm, mag_ref), (soft_hbm, soft_ref), (t_hbm, t_ref), (reg_hbm, reg_ref), (s_hbm, s_ref),
    )
    copies = [pltpu.make_async_copy(a, b, sem.at[k]) for k, (a, b) in enumerate(pairs)]
    for copy in copies:
        copy.start()
    copies[0].wait()
    copies[1].wait()
    mag = [jnp.full((Z, N), mag_ref[k] * 1000.0) for k in range(3)]
    soft = [jnp.full((Z, N), -soft_ref[k]) for k in range(3)]
    for k in range(3):
        par_ref[k] = mag[k]
        par_ref[3 + k] = soft[k]
    copies[2].wait()
    copies[3].wait()
    for row, out in ((0, up_ref), (N - 1, down_ref)):
        t = t_ref[strided(row), :]
        out[0] = t
        out[1] = conductivity(t, reg_ref[strided(row), :], mag, soft)
    copies[4].wait()


def first_kernel(
    t_ref, reg_ref, s_ref, par_ref,
    ty_ref, cy_ref, r_ref, pr_ref, gr_ref, rr_ref, sep_ref, net_ref, cx_ref,
):
    mag = [par_ref[k] for k in range(3)]
    soft = [par_ref[3 + k] for k in range(3)]
    z = lax.broadcasted_iota(jnp.int32, (Z, N), 0)
    inner = jnp.where(z < Z - 1, 1.6e-4, 0.0)
    ground = jnp.where(z == 0, 8e-5, 0.0)

    def load(y):
        t = t_ref[strided(y), :]
        c = conductivity(t, reg_ref[strided(y), :], mag, soft)
        ty_ref[at(y), :] = t
        cy_ref[at(y), :] = c
        return t, c

    def row(y, t, c, before, after):
        flux = link(c, pltpu.roll(c, Z - 1, 0)) * (pltpu.roll(t, Z - 1, 0) - t) * inner
        up = flux - pltpu.roll(flux, 1, 0) - ground * (c * t)
        r_ref[at(y), :] = 2.0 * t + s_ref[strided(y), :] + 2.0 * (after - before) + up

    def body(k, state):
        t, c, before = state
        for j in range(8):
            y = k * 8 + j
            tn, cn = load(y + 1)
            after = link(c, cn) * (tn - t)
            row(y, t, c, before, after)
            t, c, before = tn, cn, after
        return t, c, before

    t, c = load(0)
    state = lax.fori_loop(0, N // 8 - 1, body, (t, c, jnp.zeros((Z, N), F32)))
    t, c, before = state
    for y in range(N - 8, N - 1):
        tn, cn = load(y + 1)
        after = link(c, cn) * (tn - t)
        row(y, t, c, before, after)
        t, c, before = tn, cn, after
    row(N - 1, t, c, before, jnp.zeros((Z, N), F32))
    turn(cy_ref, cx_ref)
    factor(cx_ref, pr_ref, gr_ref, rr_ref, sep_ref, net_ref)


def side_call(
    r_ref, ty_ref, cy_ref, north_ref, south_ref, pr_ref, gr_ref, rr_ref, sep_ref, net_ref,
    rd_ref, srd_ref, out_ref, rx_ref, ry_ref,
):
    me = lax.axis_index("row")
    ry_ref[...] = r_ref[...]
    for row, halo, there in ((0, north_ref, me > 0), (N - 1, south_ref, me < lax.axis_size("row") - 1)):
        i = slice(row * Z, row * Z + Z)
        flux = link(cy_ref[i, :], halo[1]) * (halo[0] - ty_ref[i, :])
        ry_ref[i, :] = r_ref[i, :] + jnp.where(there, 2.0 * flux, 0.0)
    turn(ry_ref, rx_ref)
    sweep(
        lambda i: rx_ref[at(i), :],
        pr_ref, gr_ref, rr_ref, sep_ref, net_ref, rd_ref, srd_ref, out_ref,
    )


def merge_kernel(axis, own_ref, other_ref, out_ref):
    left = lax.axis_index(axis) % 2 == 0
    new = joined([own_ref[k] for k in range(7)], [other_ref[k] for k in range(7)], left)
    for k in range(7):
        out_ref[k] = new[k]


def ring_kernel(axis, own_ref, before_ref, after_ref, across_ref, *outs):
    place = lax.axis_index(axis) // 2 % 4
    even = place % 2 == 0
    own, before, after, across = (
        [r[k] for k in range(7)] for r in (own_ref, before_ref, after_ref, across_ref)
    )
    near = [jnp.where(even, a, b) for a, b in zip(after, before)]
    far = [jnp.where(even, b, a) for a, b in zip(after, before)]
    pair = joined(own, near, even)
    rest = joined(across, far, even)
    every = joined(pair, rest, place < 2)
    for out, net in zip(outs, (near, pair, rest, every)):
        for k in range(7):
            out[k] = net[k]


def gather_kernel(net_ref, out_ref):
    for b in range(8):
        out_ref[b] = net_ref[...]


def tree_kernel(axis, all_ref, *outs):
    me = lax.axis_index(axis)
    own = [all_ref[me, k] for k in range(7)]
    place = lambda m: [all_ref[me ^ m, k] for k in range(7)]
    l0, l1, l2 = (me >> 0) % 2 == 0, (me >> 1) % 2 == 0, (me >> 2) % 2 == 0
    own1 = joined(own, place(1), l0)
    far1 = joined(place(2), place(3), l0)
    own2 = joined(own1, far1, l1)
    far2 = joined(joined(place(4), place(5), l0), joined(place(6), place(7), l0), l1)
    for out, net in zip(outs, (place(1), own1, far1, own2, far2)):
        for k in range(7):
            out[k] = net[k]


def middle_kernel(
    levels, *refs,
):
    owns, others, refs = refs[:levels], refs[levels : 2 * levels], refs[2 * levels :]
    (
        pr_ref, gr_ref, rd_ref, sep_ref, srd_ref, ty_ref,
        ypr_ref, ygr_ref, yrr_ref, ysep_ref, ynet_ref,
        yrd_ref, ysrd_ref, out_ref, wx_ref, wy_ref,
    ) = refs
    ul, ur = ends(lax.axis_index("col"), levels, owns, others)

    def put(i, v):
        wx_ref[at(i), :] = v

    back(ul, ur, pr_ref, gr_ref, rd_ref, sep_ref, srd_ref, put)
    turn(wx_ref, wy_ref)
    sweep(
        lambda i: wy_ref[at(i), :] - 2.0 * ty_ref[at(i), :],
        ypr_ref, ygr_ref, yrr_ref, ysep_ref, ynet_ref, yrd_ref, ysrd_ref, out_ref,
    )


def last_kernel(levels, *refs):
    owns, others, refs = refs[:levels], refs[levels : 2 * levels], refs[2 * levels :]
    pr_ref, gr_ref, rd_ref, sep_ref, srd_ref, ty_ref, out_ref = refs
    ul, ur = ends(lax.axis_index("row"), levels, owns, others)

    def put(i, v):
        out_ref[strided(i), :] = v + ty_ref[at(i), :]

    back(ul, ur, pr_ref, gr_ref, rd_ref, sep_ref, srd_ref, put)


FIELD = (ROWS, N)
NET = (7, Z, N)
PART = (5, Z, N)
SEPS = (3, CHUNKS, Z, N)
SEPD = (CHUNKS, Z, N)


def vm(shape):
    return VM(shape, F32)


def call(kernel, args, outs, scratch=(), flops=0):
    args = [pltpu.with_memory_space_constraint(a, VM) for a in args]
    whole = pl.BlockSpec(memory_space=VM)
    many = isinstance(outs, tuple)
    return pl.pallas_call(
        kernel,
        in_specs=[whole] * len(args),
        out_specs=(whole,) * len(outs) if many else whole,
        out_shape=outs,
        scratch_shapes=list(scratch),
        cost_estimate=pl.CostEstimate(flops=flops, bytes_accessed=flops, transcendentals=0),
        compiler_params=pltpu.CompilerParams(vmem_limit_bytes=16 * 1024 * 1024),
    )(*args)


def partner(x, axis, mask):
    return lax.ppermute(x, axis, [(i, i ^ mask) for i in range(lax.axis_size(axis))])


def around(x, axis, shift):
    n = lax.axis_size(axis)
    to = lambda i: i // 8 * 8 + (i // 2 + shift) % 4 * 2 + i % 2
    return lax.ppermute(x, axis, [(i, to(i)) for i in range(n)])


def spread_col(net, axis):
    owns, others = [net], [partner(net, axis, 1)]
    own = call(lambda *refs: merge_kernel(axis, *refs), [net, others[0]], vm(NET))
    near, pair, rest, every = call(
        lambda *refs: ring_kernel(axis, *refs),
        [own, around(own, axis, 1), around(own, axis, 3), around(own, axis, 2)],
        (vm(NET),) * 4,
    )
    return [net, own, pair, every], others + [near, rest, partner(every, axis, 8)]


def spread_row(net, axis):
    send = call(gather_kernel, [net], vm((8,) + NET))
    got = lax.all_to_all(send, axis, 0, 0, tiled=True)
    near, own1, far1, own2, far2 = call(lambda *refs: tree_kernel(axis, *refs), [got], (vm(NET),) * 5)
    return [net, own1, own2], [near, far1, far2]


def local(t, region, source, mag, soft):
    t, region, source = (a.reshape(FIELD) for a in (t, region, source))
    n = lax.axis_size("row")
    t, region, source, up, down, par = pl.pallas_call(
        edge_kernel,
        in_specs=[pl.BlockSpec(memory_space=pl.ANY)] * 5,
        out_specs=(pl.BlockSpec(memory_space=VM),) * 6,
        out_shape=(vm(FIELD), VM(FIELD, jnp.int32), vm(FIELD), vm((2, Z, N)), vm((2, Z, N)), vm((6, Z, N))),
        scratch_shapes=[
            pltpu.SMEM((3,), F32), pltpu.SMEM((3,), F32), pltpu.SemaphoreType.DMA((5,)),
        ],
    )(t, region, source, mag, soft)
    south = lax.ppermute(up, "row", [((i + 1) % n, i) for i in range(n)])
    north = lax.ppermute(down, "row", [(i, (i + 1) % n) for i in range(n)])
    ty, cy, r, pr, gr, rr, sep, net = call(
        first_kernel,
        [t, region, source, par],
        (vm(FIELD),) * 6 + (vm(SEPS), vm(PART)),
        scratch=[vm(FIELD)],
        flops=20_000_000,
    )
    rd, srd, own = call(
        side_call,
        [r, ty, cy, north, south, pr, gr, rr, sep, net],
        (vm(FIELD), vm(SEPD), vm(NET)),
        scratch=[vm(FIELD), vm(FIELD)],
    )
    ypr, ygr, yrr, ysep, ynet = call(
        factor, [cy], (vm(FIELD),) * 3 + (vm(SEPS), vm(PART)), flops=5_000_000
    )
    owns, others = spread_col(own, "col")
    yrd, ysrd, own = call(
        lambda *refs: middle_kernel(4, *refs),
        owns + others + [pr, gr, rd, sep, srd, ty, ypr, ygr, yrr, ysep, ynet],
        (vm(FIELD), vm(SEPD), vm(NET)),
        scratch=[vm(FIELD), vm(FIELD)],
    )
    owns, others = spread_row(own, "row")
    out = call(
        lambda *refs: last_kernel(3, *refs),
        owns + others + [ypr, ygr, yrd, ysep, ysrd, ty],
        jax.ShapeDtypeStruct(FIELD, F32),
    )
    return out.reshape((Z, N, N))


def solution(mesh):
    specs = (P(None, "row", "col"),) * 3 + (P(), P())
    return jax.shard_map(
        local, mesh=mesh, in_specs=specs, out_specs=P(None, "row", "col"), check_vma=False
    )
```

```python
import jax
import jax.numpy as jnp
from jax import lax
from jax.experimental import pallas as pl
from jax.experimental.pallas import tpu as pltpu
from jax.sharding import PartitionSpec as P

Z, N = 8, 128
ROWS = Z * N
PITCH = N + 8
CHUNKS, STEP = 8, 16
F32 = jnp.float32
VM = pltpu.VMEM


def rcp(x):
    return pl.reciprocal(x, approx=True)


def link(a, b):
    return a * b * rcp(a + b)


def at(i):
    return pl.ds(pl.multiple_of(i * Z, Z), Z)


def strided(i):
    return pl.ds(i, Z, stride=PITCH)


def conductivity(t, reg, mag, soft):
    m = jnp.where(reg == 0, mag[0], jnp.where(reg == 1, mag[1], mag[2]))
    b = jnp.where(reg == 0, soft[0], jnp.where(reg == 1, soft[1], soft[2]))
    return m * jnp.exp(b * t)


def turn(src, dst):
    def body(z, _):
        lines = pl.ds(z, N, stride=Z)
        dst[lines, :] = src[lines, :].T
        return 0

    lax.fori_loop(0, Z, body, 0, unroll=2)


def factor(c_ref, pr_ref, gr_ref, rr_ref, sep_ref, net_ref, south=None, there=None):
    one = jnp.ones((Z, N), F32)
    zero = jnp.zeros((Z, N), F32)

    def cell(c, j, p, t, s, here, beyond=None):
        i = c * STEP + j
        edge = beyond is not None
        if not edge:
            beyond = c_ref[at(i + 1), :]
        g = link(here, beyond)
        if edge:
            g = jnp.where(there, g, 0.0)
        r = rcp(p + g + t)
        pr, gr = p * r, g * r
        pr_ref[at(i), :] = pr
        gr_ref[at(i), :] = gr
        rr_ref[at(i), :] = r
        return pr * g, gr * t if edge else 1.0 + gr * t, s + pr * t, beyond

    start = []
    for c in range(CHUNKS):
        here = c_ref[at(c * STEP + 1), :]
        start.append((link(c_ref[at(c * STEP), :], here), one, zero, here))

    def body(j, state):
        return [cell(c, j, *state[c]) for c in range(CHUNKS)]

    state = lax.fori_loop(1, STEP - 1, body, start)
    last = state[-1] if south is None else cell(CHUNKS - 1, STEP - 1, *state[-1], south)
    state = [cell(c, STEP - 1, *state[c]) for c in range(CHUNKS - 1)] + [last]
    q = state[0][0]
    left = 1.0 + state[0][2]
    t = state[0][1] + state[1][2]
    for c in range(1, CHUNKS):
        g = state[c][0]
        r = rcp(q + g + t)
        qr, gr = q * r, g * r
        sep_ref[0, c] = qr
        sep_ref[1, c] = gr
        sep_ref[2, c] = r
        left = left + qr * t
        t = state[c][1] + gr * t
        if c + 1 < CHUNKS:
            t = t + state[c + 1][2]
        q = qr * g
    net_ref[0] = q
    net_ref[1] = left
    net_ref[2] = t if south is None else jnp.where(there, t, 1.0)


def sweep(rhs, pr_ref, gr_ref, rr_ref, sep_ref, rd_ref, srd_ref, shared):
    def cell(c, j, d, s):
        i = c * STEP + j
        rd_ref[at(i), :] = rr_ref[at(i), :] * d
        beyond = gr_ref[at(i), :] * d
        if not (c == CHUNKS - 1 and j is STEP - 1):
            beyond = rhs(i + 1) + beyond
        return beyond, s + pr_ref[at(i), :] * d

    def body(j, state):
        return [cell(c, j, *state[c]) for c in range(CHUNKS)]

    start = [(rhs(c * STEP + 1), jnp.zeros((Z, N), F32)) for c in range(CHUNKS)]
    state = lax.fori_loop(1, STEP - 1, body, start)
    last = cell(CHUNKS - 1, STEP - 1, *state[-1]) if shared else state[-1]
    state = [cell(c, STEP - 1, *state[c]) for c in range(CHUNKS - 1)] + [last]
    left = rhs(0) + state[0][1]
    d = state[0][0] + state[1][1]
    for c in range(1, CHUNKS):
        left = left + sep_ref[0, c] * d
        srd_ref[c] = sep_ref[2, c] * d
        d = state[c][0] + sep_ref[1, c] * d
        if c + 1 < CHUNKS:
            d = d + state[c + 1][1]
    return left, d


def back(ul, ur, pr_ref, gr_ref, rd_ref, sep_ref, srd_ref, put, shared):
    seps = [None] * CHUNKS + [ur]
    for c in range(CHUNKS - 1, 0, -1):
        seps[c] = srd_ref[c] + sep_ref[0, c] * ul + sep_ref[1, c] * seps[c + 1]
    seps[0] = ul
    for c in range(CHUNKS):
        put(c * STEP, seps[c])

    def cell(c, j, u):
        i = c * STEP + j
        v = rd_ref[at(i), :] + pr_ref[at(i), :] * seps[c] + gr_ref[at(i), :] * u
        put(i, v)
        return v

    if not shared:
        put(N - 1, ur)
    last = cell(CHUNKS - 1, STEP - 1, ur) if shared else ur
    state = [cell(c, STEP - 1, seps[c + 1]) for c in range(CHUNKS - 1)] + [last]

    def body(k, state):
        return [cell(c, STEP - 2 - k, state[c]) for c in range(CHUNKS)]

    lax.fori_loop(0, STEP - 2, body, state)


def joined(own, other, left):
    a = [jnp.where(left, x, y) for x, y in zip(own, other)]
    b = [jnp.where(left, y, x) for x, y in zip(own, other)]
    if len(a) == 5:
        s, d = a[2] + b[1], a[4] + b[3]
        r = rcp(a[0] + b[0] + s)
        f, h = a[0] * r, b[0] * r
        return [f * b[0], a[1] + f * s, b[2] + h * s, a[3] + f * d, b[4] + h * d]
    between = link(a[6], b[5])
    r = rcp(a[0] + between + a[2])
    f, h = a[0] * r, between * r
    g1 = f * between
    s1 = b[1] + h * a[2]
    d1 = b[3] + h * a[4]
    left_s = a[1] + f * a[2]
    left_d = a[3] + f * a[4]
    r = rcp(g1 + b[0] + s1)
    f, h = g1 * r, b[0] * r
    return [f * b[0], left_s + f * s1, b[2] + h * s1, left_d + f * d1, b[4] + h * d1, a[5], b[6]]


def ends(me, owns, others):
    zero = jnp.zeros((Z, N), F32)
    yl = il = yr = ir = zero
    for k in reversed(range(len(others))):
        p, m = others[k], owns[k]
        left = (me >> k) % 2 == 1
        far_s = jnp.where(left, p[1] + yl, p[2] + yr)
        far_d = jnp.where(left, p[3] + il, p[4] + ir)
        near_s = jnp.where(left, p[2], p[1])
        near_d = jnp.where(left, p[4], p[3])
        f = p[0] * rcp(p[0] + far_s)
        y, i = near_s + f * far_s, near_d + f * far_d
        if len(p) == 7:
            between = link(jnp.where(left, p[6], p[5]), jnp.where(left, m[5], m[6]))
            f = between * rcp(between + y)
            y, i = f * y, f * i
        yl, il = jnp.where(left, y, yl), jnp.where(left, i, il)
        yr, ir = jnp.where(left, yr, y), jnp.where(left, ir, i)
    m = owns[0]
    sl, dl, sr, dr = m[1] + yl, m[3] + il, m[2] + yr, m[4] + ir
    r = rcp(m[0] + sl)
    f = m[0] * r
    ur = (dr + f * dl) * rcp(sr + f * sl)
    ul = (dl + m[0] * ur) * r
    return ul, ur


def edge_kernel(
    t_hbm, reg_hbm, s_hbm, mag_hbm, soft_hbm,
    t_ref, reg_ref, s_ref, up_ref, down_ref, par_ref, mag_ref, soft_ref, sem,
):
    pairs = (
        (mag_hbm, mag_ref), (soft_hbm, soft_ref), (t_hbm, t_ref), (reg_hbm, reg_ref), (s_hbm, s_ref),
    )
    copies = [
        pltpu.make_async_copy(a, b if k < 2 else b.at[:, pl.ds(0, N), :], sem.at[k])
        for k, (a, b) in enumerate(pairs)
    ]
    for copy in copies:
        copy.start()
    copies[0].wait()
    copies[1].wait()
    mag = [jnp.full((Z, N), mag_ref[k] * 1000.0) for k in range(3)]
    soft = [jnp.full((Z, N), -soft_ref[k]) for k in range(3)]
    for k in range(3):
        par_ref[k] = mag[k]
        par_ref[3 + k] = soft[k]
    copies[2].wait()
    copies[3].wait()
    for row, out in ((0, up_ref), (N - 1, down_ref)):
        t = t_ref[:, row, :]
        out[0] = t
        out[1] = conductivity(t, reg_ref[:, row, :], mag, soft)
    copies[4].wait()


def first_kernel(
    t_ref, reg_ref, s_ref, par_ref,
    ty_ref, cy_ref, r_ref, pr_ref, gr_ref, rr_ref, sep_ref, net_ref, cend_ref, cx_ref,
):
    mag = [par_ref[k] for k in range(3)]
    soft = [par_ref[3 + k] for k in range(3)]
    z = lax.broadcasted_iota(jnp.int32, (Z, N), 0)
    inner = jnp.where(z < Z - 1, 1.6e-4, 0.0)
    ground = jnp.where(z == 0, 8e-5, 0.0)

    def load(y):
        t = t_ref[strided(y), :]
        c = conductivity(t, reg_ref[strided(y), :], mag, soft)
        ty_ref[at(y), :] = t
        cy_ref[at(y), :] = c
        return t, c

    def row(y, t, c, before, after):
        flux = link(c, pltpu.roll(c, Z - 1, 0)) * (pltpu.roll(t, Z - 1, 0) - t) * inner
        up = flux - pltpu.roll(flux, 1, 0) - ground * (c * t)
        r_ref[at(y), :] = 2.0 * t + s_ref[strided(y), :] + 2.0 * (after - before) + up

    def body(k, state):
        t, c, before = state
        for j in range(8):
            y = k * 8 + j
            tn, cn = load(y + 1)
            after = link(c, cn) * (tn - t)
            row(y, t, c, before, after)
            t, c, before = tn, cn, after
        return t, c, before

    t, c = load(0)
    state = lax.fori_loop(0, N // 8 - 1, body, (t, c, jnp.zeros((Z, N), F32)))
    t, c, before = state
    for y in range(N - 8, N - 1):
        tn, cn = load(y + 1)
        after = link(c, cn) * (tn - t)
        row(y, t, c, before, after)
        t, c, before = tn, cn, after
    row(N - 1, t, c, before, jnp.zeros((Z, N), F32))
    turn(cy_ref, cx_ref)
    factor(cx_ref, pr_ref, gr_ref, rr_ref, sep_ref, net_ref)
    cend_ref[0] = cx_ref[at(0), :]
    cend_ref[1] = cx_ref[at(N - 1), :]


def side_kernel(
    r_ref, ty_ref, cy_ref, north_ref, south_ref, pr_ref, gr_ref, rr_ref, sep_ref, net_ref,
    cx_ref, rd_ref, srd_ref, out_ref, rx_ref, ry_ref,
):
    me = lax.axis_index("row")
    ry_ref[...] = r_ref[...]
    for row, halo, there in ((0, north_ref, me > 0), (N - 1, south_ref, me < lax.axis_size("row") - 1)):
        i = slice(row * Z, row * Z + Z)
        flux = link(cy_ref[i, :], halo[1]) * (halo[0] - ty_ref[i, :])
        ry_ref[i, :] = r_ref[i, :] + jnp.where(there, 2.0 * flux, 0.0)
    turn(ry_ref, rx_ref)
    left, right = sweep(
        lambda i: rx_ref[at(i), :], pr_ref, gr_ref, rr_ref, sep_ref, rd_ref, srd_ref, False
    )
    for k in range(3):
        out_ref[k] = net_ref[k]
    out_ref[3] = left
    out_ref[4] = right
    out_ref[5] = cx_ref[0]
    out_ref[6] = cx_ref[1]


def lines_kernel(c_ref, south_ref, *outs):
    there = lax.axis_index("row") < lax.axis_size("row") - 1
    factor(c_ref, *outs, south=south_ref[1], there=there)


def merge_kernel(axis, own_ref, other_ref, out_ref):
    left = lax.axis_index(axis) % 2 == 0
    new = joined([own_ref[k] for k in range(7)], [other_ref[k] for k in range(7)], left)
    for k in range(7):
        out_ref[k] = new[k]


def ring_kernel(axis, own_ref, before_ref, after_ref, across_ref, *outs):
    place = lax.axis_index(axis) // 2 % 4
    even = place % 2 == 0
    own, before, after, across = (
        [r[k] for k in range(7)] for r in (own_ref, before_ref, after_ref, across_ref)
    )
    near = [jnp.where(even, a, b) for a, b in zip(after, before)]
    far = [jnp.where(even, b, a) for a, b in zip(after, before)]
    pair = joined(own, near, even)
    rest = joined(across, far, even)
    every = joined(pair, rest, place < 2)
    for out, net in zip(outs, (near, pair, rest, every)):
        for k in range(7):
            out[k] = net[k]


def middle_kernel(*refs):
    owns, others, refs = refs[:4], refs[4:8], refs[8:]
    (
        pr_ref, gr_ref, rd_ref, sep_ref, srd_ref, ty_ref,
        ypr_ref, ygr_ref, yrr_ref, ysep_ref, ynet_ref,
        yrd_ref, ysrd_ref, out_ref, wx_ref, wy_ref,
    ) = refs
    nets = [[[r[k] for k in range(7)] for r in group] for group in (owns, others)]
    ul, ur = ends(lax.axis_index("col"), *nets)

    def put(i, v):
        wx_ref[at(i), :] = v

    back(ul, ur, pr_ref, gr_ref, rd_ref, sep_ref, srd_ref, put, False)
    turn(wx_ref, wy_ref)
    left, right = sweep(
        lambda i: wy_ref[at(i), :] - 2.0 * ty_ref[at(i), :],
        ypr_ref, ygr_ref, yrr_ref, ysep_ref, yrd_ref, ysrd_ref, True,
    )
    for b in range(out_ref.shape[0]):
        for k in range(3):
            out_ref[b, k] = ynet_ref[k]
        out_ref[b, 3] = left
        out_ref[b, 4] = right


def last_kernel(
    all_ref, pr_ref, gr_ref, rd_ref, sep_ref, srd_ref, ty_ref, out_hbm, new_ref, sem
):
    me = lax.axis_index("row")
    place = lambda m: [all_ref[me ^ m, k] for k in range(5)]
    one, two = me % 2 == 0, me // 2 % 2 == 0
    own = place(0)
    pair = joined(own, place(1), one)
    far = joined(place(2), place(3), one)
    half = joined(joined(place(4), place(5), one), joined(place(6), place(7), one), two)
    ul, ur = ends(me, [own, pair, None], [place(1), far, half])

    def put(i, v):
        new_ref[strided(i), :] = v + ty_ref[at(i), :]

    back(ul, ur, pr_ref, gr_ref, rd_ref, sep_ref, srd_ref, put, True)
    copies = [
        pltpu.make_async_copy(
            new_ref.at[pl.ds(z * PITCH, N), :], out_hbm.at[pl.ds(z * N, N), :], sem.at[z]
        )
        for z in range(Z)
    ]
    for copy in copies:
        copy.start()
    for copy in copies:
        copy.wait()


FIELD = (ROWS, N)
SPACED = (Z, PITCH, N)
NET = (7, Z, N)
SHARED = (5, Z, N)
PART = (3, Z, N)
SEPS = (3, CHUNKS, Z, N)
SEPD = (CHUNKS, Z, N)


def vm(shape):
    return VM(shape, F32)


def call(kernel, args, outs, scratch=(), flops=0, out_space=VM):
    args = [pltpu.with_memory_space_constraint(a, VM) for a in args]
    whole = pl.BlockSpec(memory_space=VM)
    many = isinstance(outs, tuple)
    return pl.pallas_call(
        kernel,
        in_specs=[whole] * len(args),
        out_specs=(whole,) * len(outs) if many else pl.BlockSpec(memory_space=out_space),
        out_shape=outs,
        scratch_shapes=list(scratch),
        cost_estimate=pl.CostEstimate(flops=flops, bytes_accessed=flops, transcendentals=0),
        compiler_params=pltpu.CompilerParams(vmem_limit_bytes=16 * 1024 * 1024),
    )(*args)


def partner(x, axis, mask):
    return lax.ppermute(x, axis, [(i, i ^ mask) for i in range(lax.axis_size(axis))])


def around(x, axis, shift):
    n = lax.axis_size(axis)
    to = lambda i: i // 8 * 8 + (i // 2 + shift) % 4 * 2 + (i + 1) % 2
    return lax.ppermute(x, axis, [(i, to(i)) for i in range(n)])


def spread_col(net, axis):
    owns, others = [net], [partner(net, axis, 1)]
    own = call(lambda *refs: merge_kernel(axis, *refs), [net, others[0]], vm(NET))
    near, pair, rest, every = call(
        lambda *refs: ring_kernel(axis, *refs),
        [own, around(own, axis, 1), around(own, axis, 3), around(own, axis, 2)],
        (vm(NET),) * 4,
    )
    return [net, own, pair, every], others + [near, rest, partner(every, axis, 9)]


def local(t, region, source, mag, soft):
    n = lax.axis_size("row")
    t, region, source, up, down, par = pl.pallas_call(
        edge_kernel,
        in_specs=[pl.BlockSpec(memory_space=pl.ANY)] * 5,
        out_specs=(pl.BlockSpec(memory_space=VM),) * 6,
        out_shape=(vm(SPACED), VM(SPACED, jnp.int32), vm(SPACED), vm((2, Z, N)), vm((2, Z, N)), vm((6, Z, N))),
        scratch_shapes=[
            pltpu.SMEM((3,), F32), pltpu.SMEM((3,), F32), pltpu.SemaphoreType.DMA((5,)),
        ],
    )(t, region, source, mag, soft)
    t, region, source = (a.reshape((Z * PITCH, N)) for a in (t, region, source))
    south = lax.ppermute(up, "row", [((i + 1) % n, i) for i in range(n)])
    north = lax.ppermute(down, "row", [(i, (i + 1) % n) for i in range(n)])
    ty, cy, r, pr, gr, rr, sep, net, cend = call(
        first_kernel,
        [t, region, source, par],
        (vm(FIELD),) * 6 + (vm(SEPS), vm(PART), vm((2, Z, N))),
        scratch=[vm(FIELD)],
        flops=20_000_000,
    )
    rd, srd, own = call(
        side_kernel,
        [r, ty, cy, north, south, pr, gr, rr, sep, net, cend],
        (vm(FIELD), vm(SEPD), vm(NET)),
        scratch=[vm(FIELD), vm(FIELD)],
    )
    ypr, ygr, yrr, ysep, ynet = call(
        lines_kernel, [cy, south], (vm(FIELD),) * 3 + (vm(SEPS), vm(PART)), flops=5_000_000
    )
    owns, others = spread_col(own, "col")
    yrd, ysrd, send = call(
        middle_kernel,
        owns + others + [pr, gr, rd, sep, srd, ty, ypr, ygr, yrr, ysep, ynet],
        (vm(FIELD), vm(SEPD), vm((n,) + SHARED)),
        scratch=[vm(FIELD), vm(FIELD)],
    )
    got = lax.all_to_all(send, "row", 0, 0, tiled=True)
    out = call(
        last_kernel,
        [got, ypr, ygr, yrd, ysep, ysrd, ty],
        jax.ShapeDtypeStruct(FIELD, F32),
        scratch=[vm((Z * PITCH, N)), pltpu.SemaphoreType.DMA((Z,))],
        out_space=pl.ANY,
    )
    return out.reshape((Z, N, N))


def solution(mesh):
    specs = (P(None, "row", "col"),) * 3 + (P(), P())
    return jax.shard_map(
        local, mesh=mesh, in_specs=specs, out_specs=P(None, "row", "col"), check_vma=False
    )
```

```python
import jax
import jax.numpy as jnp
from jax import lax
from jax.experimental import pallas as pl
from jax.experimental.pallas import tpu as pltpu
from jax.sharding import PartitionSpec as P

Z, N = 8, 128
ROWS = Z * N
PITCH = N + 8
CHUNKS, STEP = 8, 16
F32 = jnp.float32
VM = pltpu.VMEM


def rcp(x):
    return pl.reciprocal(x, approx=True)


def link(a, b):
    return a * b * rcp(a + b)


def at(i):
    return pl.ds(pl.multiple_of(i * Z, Z), Z)


def strided(i):
    return pl.ds(i, Z, stride=PITCH)


def conductivity(t, reg, mag, soft):
    m = jnp.where(reg == 0, mag[0], jnp.where(reg == 1, mag[1], mag[2]))
    b = jnp.where(reg == 0, soft[0], jnp.where(reg == 1, soft[1], soft[2]))
    return m * jnp.exp(b * t)


def turn(src, dst):
    def body(z, _):
        lines = pl.ds(z, N, stride=Z)
        dst[lines, :] = src[lines, :].T
        return 0

    lax.fori_loop(0, Z, body, 0, unroll=True)


def factor(c_ref, pr_ref, gr_ref, rr_ref, sep_ref, net_ref, south=None, there=None):
    one = jnp.ones((Z, N), F32)
    zero = jnp.zeros((Z, N), F32)

    def cell(c, j, p, t, s, here, beyond=None):
        i = c * STEP + j
        edge = beyond is not None
        if not edge:
            beyond = c_ref[at(i + 1), :]
        g = link(here, beyond)
        if edge:
            g = jnp.where(there, g, 0.0)
        r = rcp(p + g + t)
        pr, gr = p * r, g * r
        pr_ref[at(i), :] = pr
        gr_ref[at(i), :] = gr
        rr_ref[at(i), :] = r
        return pr * g, gr * t if edge else 1.0 + gr * t, s + pr * t, beyond

    start = []
    for c in range(CHUNKS):
        here = c_ref[at(c * STEP + 1), :]
        start.append((link(c_ref[at(c * STEP), :], here), one, zero, here))

    def body(j, state):
        return [cell(c, j, *state[c]) for c in range(CHUNKS)]

    state = lax.fori_loop(1, STEP - 1, body, start, unroll=2)
    last = state[-1] if south is None else cell(CHUNKS - 1, STEP - 1, *state[-1], south)
    state = [cell(c, STEP - 1, *state[c]) for c in range(CHUNKS - 1)] + [last]
    q = state[0][0]
    left = 1.0 + state[0][2]
    t = state[0][1] + state[1][2]
    for c in range(1, CHUNKS):
        g = state[c][0]
        r = rcp(q + g + t)
        qr, gr = q * r, g * r
        sep_ref[0, c] = qr
        sep_ref[1, c] = gr
        sep_ref[2, c] = r
        left = left + qr * t
        t = state[c][1] + gr * t
        if c + 1 < CHUNKS:
            t = t + state[c + 1][2]
        q = qr * g
    net_ref[0] = q
    net_ref[1] = left
    net_ref[2] = t if south is None else jnp.where(there, t, 1.0)


def sweep(rhs, pr_ref, gr_ref, rr_ref, sep_ref, rd_ref, srd_ref, shared):
    def cell(c, j, d, s):
        i = c * STEP + j
        rd_ref[at(i), :] = rr_ref[at(i), :] * d
        beyond = gr_ref[at(i), :] * d
        if not (c == CHUNKS - 1 and isinstance(j, int)):
            beyond = rhs(i + 1) + beyond
        return beyond, s + pr_ref[at(i), :] * d

    def body(j, state):
        return [cell(c, j, *state[c]) for c in range(CHUNKS)]

    start = [(rhs(c * STEP + 1), jnp.zeros((Z, N), F32)) for c in range(CHUNKS)]
    state = lax.fori_loop(1, STEP - 1, body, start, unroll=True)
    last = cell(CHUNKS - 1, STEP - 1, *state[-1]) if shared else state[-1]
    state = [cell(c, STEP - 1, *state[c]) for c in range(CHUNKS - 1)] + [last]
    left = rhs(0) + state[0][1]
    d = state[0][0] + state[1][1]
    for c in range(1, CHUNKS):
        left = left + sep_ref[0, c] * d
        srd_ref[c] = sep_ref[2, c] * d
        d = state[c][0] + sep_ref[1, c] * d
        if c + 1 < CHUNKS:
            d = d + state[c + 1][1]
    return left, d


def back(ul, ur, pr_ref, gr_ref, rd_ref, sep_ref, srd_ref, put, shared):
    seps = [None] * CHUNKS + [ur]
    for c in range(CHUNKS - 1, 0, -1):
        seps[c] = srd_ref[c] + sep_ref[0, c] * ul + sep_ref[1, c] * seps[c + 1]
    seps[0] = ul
    for c in range(CHUNKS):
        put(c * STEP, seps[c])

    def cell(c, j, u):
        i = c * STEP + j
        v = rd_ref[at(i), :] + pr_ref[at(i), :] * seps[c] + gr_ref[at(i), :] * u
        put(i, v)
        return v

    if not shared:
        put(N - 1, ur)
    last = cell(CHUNKS - 1, STEP - 1, ur) if shared else ur
    state = [cell(c, STEP - 1, seps[c + 1]) for c in range(CHUNKS - 1)] + [last]

    def body(k, state):
        return [cell(c, STEP - 2 - k, state[c]) for c in range(CHUNKS)]

    lax.fori_loop(0, STEP - 2, body, state, unroll=True)


def joined(own, other, left):
    a = [jnp.where(left, x, y) for x, y in zip(own, other)]
    b = [jnp.where(left, y, x) for x, y in zip(own, other)]
    if len(a) == 5:
        s, d = a[2] + b[1], a[4] + b[3]
        r = rcp(a[0] + b[0] + s)
        f, h = a[0] * r, b[0] * r
        return [f * b[0], a[1] + f * s, b[2] + h * s, a[3] + f * d, b[4] + h * d]
    between = link(a[6], b[5])
    r = rcp(a[0] + between + a[2])
    f, h = a[0] * r, between * r
    g1 = f * between
    s1 = b[1] + h * a[2]
    d1 = b[3] + h * a[4]
    left_s = a[1] + f * a[2]
    left_d = a[3] + f * a[4]
    r = rcp(g1 + b[0] + s1)
    f, h = g1 * r, b[0] * r
    return [f * b[0], left_s + f * s1, b[2] + h * s1, left_d + f * d1, b[4] + h * d1, a[5], b[6]]


def ends(me, owns, others):
    zero = jnp.zeros((Z, N), F32)
    yl = il = yr = ir = zero
    for k in reversed(range(len(others))):
        p, m = others[k], owns[k]
        left = (me >> k) % 2 == 1
        far_s = jnp.where(left, p[1] + yl, p[2] + yr)
        far_d = jnp.where(left, p[3] + il, p[4] + ir)
        near_s = jnp.where(left, p[2], p[1])
        near_d = jnp.where(left, p[4], p[3])
        f = p[0] * rcp(p[0] + far_s)
        y, i = near_s + f * far_s, near_d + f * far_d
        if len(p) == 7:
            between = link(jnp.where(left, p[6], p[5]), jnp.where(left, m[5], m[6]))
            f = between * rcp(between + y)
            y, i = f * y, f * i
        yl, il = jnp.where(left, y, yl), jnp.where(left, i, il)
        yr, ir = jnp.where(left, yr, y), jnp.where(left, ir, i)
    m = owns[0]
    sl, dl, sr, dr = m[1] + yl, m[3] + il, m[2] + yr, m[4] + ir
    r = rcp(m[0] + sl)
    f = m[0] * r
    ur = (dr + f * dl) * rcp(sr + f * sl)
    ul = (dl + m[0] * ur) * r
    return ul, ur


def edge_kernel(
    t_hbm, reg_hbm, mag_hbm, soft_hbm,
    up_ref, down_ref, par_ref, t_ref, reg_ref, mag_ref, soft_ref, sem,
):
    copies = [
        pltpu.make_async_copy(mag_hbm, mag_ref, sem.at[0]),
        pltpu.make_async_copy(soft_hbm, soft_ref, sem.at[1]),
    ]
    for k, first in enumerate((0, N - 8)):
        rows = pl.ds(first, 8)
        copies.append(pltpu.make_async_copy(t_hbm.at[:, rows, :], t_ref.at[k], sem.at[2 + k]))
        copies.append(pltpu.make_async_copy(reg_hbm.at[:, rows, :], reg_ref.at[k], sem.at[4 + k]))
    for copy in copies[2:] + copies[:2]:
        copy.start()
    for copy in copies:
        copy.wait()
    mag = [jnp.full((Z, N), mag_ref[k] * 1000.0) for k in range(3)]
    soft = [jnp.full((Z, N), -soft_ref[k]) for k in range(3)]
    for k in range(3):
        par_ref[k] = mag[k]
        par_ref[3 + k] = soft[k]
    for k, row, out in ((0, 0, up_ref), (1, 7, down_ref)):
        t = t_ref[k, :, row, :]
        out[0] = t
        out[1] = conductivity(t, reg_ref[k, :, row, :], mag, soft)


def first_kernel(
    par_ref, t_hbm, reg_hbm, s_hbm,
    ty_ref, cy_ref, r_ref, pr_ref, gr_ref, rr_ref, sep_ref, net_ref, cend_ref,
    cx_ref, t_box, reg_box, s_box, sem,
):
    cuts = (0, N // 2 + 8, N)
    copies = [[], []]
    for k in range(2):
        rows = pl.ds(cuts[k], cuts[k + 1] - cuts[k])
        for j, (a, b) in enumerate(((t_hbm, t_box), (reg_hbm, reg_box), (s_hbm, s_box))):
            copies[k].append(pltpu.make_async_copy(a.at[:, rows, :], b.at[:, rows, :], sem.at[k, j]))
            copies[k][-1].start()
    t_ref, reg_ref, s_ref = (box.reshape(Z * PITCH, N) for box in (t_box, reg_box, s_box))
    mag = [par_ref[k] for k in range(3)]
    soft = [par_ref[3 + k] for k in range(3)]
    z = lax.broadcasted_iota(jnp.int32, (Z, N), 0)
    inner = jnp.where(z < Z - 1, 1.6e-4, 0.0)
    ground = jnp.where(z == 0, 8e-5, 0.0)

    def load(y):
        t = t_ref[strided(y), :]
        c = conductivity(t, reg_ref[strided(y), :], mag, soft)
        ty_ref[at(y), :] = t
        cy_ref[at(y), :] = c
        return t, c

    def row(y, t, c, before, after):
        flux = link(c, pltpu.roll(c, Z - 1, 0)) * (pltpu.roll(t, Z - 1, 0) - t) * inner
        up = flux - pltpu.roll(flux, 1, 0) - ground * (c * t)
        r_ref[at(y), :] = 2.0 * t + s_ref[strided(y), :] + 2.0 * (after - before) + up

    def step(y, t, c, before):
        tn, cn = load(y + 1)
        after = link(c, cn) * (tn - t)
        row(y, t, c, before, after)
        return tn, cn, after

    def body(k, state):
        for j in range(8):
            state = step(k * 8 + j, *state)
        return state

    for copy in copies[0]:
        copy.wait()
    state = *load(0), jnp.zeros((Z, N), F32)
    state = lax.fori_loop(0, N // 16, body, state)
    for copy in copies[1]:
        copy.wait()
    state = lax.fori_loop(N // 16, N // 8 - 1, body, state)
    for y in range(N - 8, N - 1):
        state = step(y, *state)
    row(N - 1, *state, jnp.zeros((Z, N), F32))
    turn(cy_ref, cx_ref)
    factor(cx_ref, pr_ref, gr_ref, rr_ref, sep_ref, net_ref)
    cend_ref[0] = cx_ref[at(0), :]
    cend_ref[1] = cx_ref[at(N - 1), :]


def side_kernel(
    r_ref, ty_ref, cy_ref, north_ref, south_ref, pr_ref, gr_ref, rr_ref, sep_ref, net_ref,
    cx_ref, rd_ref, srd_ref, out_ref, rx_ref, ry_ref,
):
    me = lax.axis_index("row")
    ry_ref[...] = r_ref[...]
    for row, halo, there in ((0, north_ref, me > 0), (N - 1, south_ref, me < lax.axis_size("row") - 1)):
        i = slice(row * Z, row * Z + Z)
        flux = link(cy_ref[i, :], halo[1]) * (halo[0] - ty_ref[i, :])
        ry_ref[i, :] = r_ref[i, :] + jnp.where(there, 2.0 * flux, 0.0)
    turn(ry_ref, rx_ref)
    left, right = sweep(
        lambda i: rx_ref[at(i), :], pr_ref, gr_ref, rr_ref, sep_ref, rd_ref, srd_ref, False
    )
    for k in range(3):
        out_ref[k] = net_ref[k]
    out_ref[3] = left
    out_ref[4] = right
    out_ref[5] = cx_ref[0]
    out_ref[6] = cx_ref[1]


def lines_kernel(c_ref, south_ref, *outs):
    there = lax.axis_index("row") < lax.axis_size("row") - 1
    factor(c_ref, *outs, south=south_ref[1], there=there)


def merge_kernel(axis, own_ref, other_ref, out_ref):
    left = lax.axis_index(axis) % 2 == 0
    new = joined([own_ref[k] for k in range(7)], [other_ref[k] for k in range(7)], left)
    for k in range(7):
        out_ref[k] = new[k]


def ring_kernel(axis, own_ref, before_ref, after_ref, across_ref, *outs):
    place = lax.axis_index(axis) // 2 % 4
    even = place % 2 == 0
    own, before, after, across = (
        [r[k] for k in range(7)] for r in (own_ref, before_ref, after_ref, across_ref)
    )
    near = [jnp.where(even, a, b) for a, b in zip(after, before)]
    far = [jnp.where(even, b, a) for a, b in zip(after, before)]
    pair = joined(own, near, even)
    rest = joined(across, far, even)
    every = joined(pair, rest, place < 2)
    for out, net in zip(outs, (near, pair, rest, every)):
        for k in range(7):
            out[k] = net[k]


def middle_kernel(*refs):
    owns, others, refs = refs[:4], refs[4:8], refs[8:]
    (
        pr_ref, gr_ref, rd_ref, sep_ref, srd_ref, ty_ref,
        ypr_ref, ygr_ref, yrr_ref, ysep_ref, ynet_ref,
        yrd_ref, ysrd_ref, out_ref, wx_ref, wy_ref,
    ) = refs
    nets = [[[r[k] for k in range(7)] for r in group] for group in (owns, others)]
    ul, ur = ends(lax.axis_index("col"), *nets)

    def put(i, v):
        wx_ref[at(i), :] = v

    back(ul, ur, pr_ref, gr_ref, rd_ref, sep_ref, srd_ref, put, False)
    turn(wx_ref, wy_ref)
    left, right = sweep(
        lambda i: wy_ref[at(i), :] - 2.0 * ty_ref[at(i), :],
        ypr_ref, ygr_ref, yrr_ref, ysep_ref, yrd_ref, ysrd_ref, True,
    )
    for b in range(out_ref.shape[0]):
        for k in range(3):
            out_ref[b, k] = ynet_ref[k]
        out_ref[b, 3] = left
        out_ref[b, 4] = right


def last_kernel(
    all_ref, pr_ref, gr_ref, rd_ref, sep_ref, srd_ref, ty_ref, out_hbm, new_ref, sem
):
    me = lax.axis_index("row")
    place = lambda m: [all_ref[me ^ m, k] for k in range(5)]
    one, two = me % 2 == 0, me // 2 % 2 == 0
    own = place(0)
    pair = joined(own, place(1), one)
    far = joined(place(2), place(3), one)
    half = joined(joined(place(4), place(5), one), joined(place(6), place(7), one), two)
    ul, ur = ends(me, [own, pair, None], [place(1), far, half])

    def put(i, v):
        new_ref[strided(i), :] = v + ty_ref[at(i), :]

    back(ul, ur, pr_ref, gr_ref, rd_ref, sep_ref, srd_ref, put, True)
    copies = [
        pltpu.make_async_copy(
            new_ref.at[pl.ds(z * PITCH, N), :], out_hbm.at[pl.ds(z * N, N), :], sem.at[z]
        )
        for z in range(Z)
    ]
    for copy in copies:
        copy.start()
    for copy in copies:
        copy.wait()


FIELD = (ROWS, N)
SPACED = (Z, PITCH, N)
NET = (7, Z, N)
SHARED = (5, Z, N)
PART = (3, Z, N)
SEPS = (3, CHUNKS, Z, N)
SEPD = (CHUNKS, Z, N)


def vm(shape):
    return VM(shape, F32)


def call(kernel, args, outs, scratch=(), flops=0, out_space=VM, outside=()):
    args = [pltpu.with_memory_space_constraint(a, VM) for a in args]
    whole = pl.BlockSpec(memory_space=VM)
    many = isinstance(outs, tuple)
    return pl.pallas_call(
        kernel,
        in_specs=[whole] * len(args) + [pl.BlockSpec(memory_space=pltpu.HBM)] * len(outside),
        out_specs=(whole,) * len(outs) if many else pl.BlockSpec(memory_space=out_space),
        out_shape=outs,
        scratch_shapes=list(scratch),
        cost_estimate=pl.CostEstimate(flops=flops, bytes_accessed=flops, transcendentals=0),
        compiler_params=pltpu.CompilerParams(vmem_limit_bytes=16 * 1024 * 1024),
    )(*args, *(pltpu.with_memory_space_constraint(a, pltpu.HBM) for a in outside))


def partner(x, axis, mask):
    return lax.ppermute(x, axis, [(i, i ^ mask) for i in range(lax.axis_size(axis))])


def around(x, axis, shift):
    n = lax.axis_size(axis)
    to = lambda i: i // 8 * 8 + (i // 2 + shift) % 4 * 2 + (i + 1) % 2
    return lax.ppermute(x, axis, [(i, to(i)) for i in range(n)])


def spread_col(net, axis):
    owns, others = [net], [partner(net, axis, 1)]
    own = call(lambda *refs: merge_kernel(axis, *refs), [net, others[0]], vm(NET))
    after = around(own, axis, 3)
    before = around(own, axis, 1)
    across = around(own, axis, 2)
    near, pair, rest, every = call(
        lambda *refs: ring_kernel(axis, *refs),
        [own, before, after, across],
        (vm(NET),) * 4,
    )
    return [net, own, pair, every], others + [near, rest, partner(every, axis, 9)]


def local(t, region, source, mag, soft):
    n = lax.axis_size("row")
    edge = (2, Z, 8, N)
    up, down, par = pl.pallas_call(
        edge_kernel,
        in_specs=[pl.BlockSpec(memory_space=pltpu.HBM)] * 4,
        out_specs=(pl.BlockSpec(memory_space=VM),) * 3,
        out_shape=(vm((2, Z, N)), vm((2, Z, N)), vm((6, Z, N))),
        scratch_shapes=[
            vm(edge), VM(edge, jnp.int32), pltpu.SMEM((3,), F32), pltpu.SMEM((3,), F32),
            pltpu.SemaphoreType.DMA((6,)),
        ],
    )(t, region, mag, soft)
    south = lax.ppermute(up, "row", [((i + 1) % n, i) for i in range(n)])
    north = lax.ppermute(down, "row", [(i, (i + 1) % n) for i in range(n)])
    ty, cy, r, pr, gr, rr, sep, net, cend = call(
        first_kernel,
        [par],
        (vm(FIELD),) * 6 + (vm(SEPS), vm(PART), vm((2, Z, N))),
        scratch=[
            vm(FIELD), vm(SPACED), VM(SPACED, jnp.int32), vm(SPACED), pltpu.SemaphoreType.DMA((2, 3)),
        ],
        outside=[t, region, source],
        flops=20_000_000,
    )
    rd, srd, own = call(
        side_kernel,
        [r, ty, cy, north, south, pr, gr, rr, sep, net, cend],
        (vm(FIELD), vm(SEPD), vm(NET)),
        scratch=[vm(FIELD), vm(FIELD)],
    )
    ypr, ygr, yrr, ysep, ynet = call(
        lines_kernel, [cy, south], (vm(FIELD),) * 3 + (vm(SEPS), vm(PART)), flops=5_000_000
    )
    owns, others = spread_col(own, "col")
    yrd, ysrd, send = call(
        middle_kernel,
        owns + others + [pr, gr, rd, sep, srd, ty, ypr, ygr, yrr, ysep, ynet],
        (vm(FIELD), vm(SEPD), vm((n,) + SHARED)),
        scratch=[vm(FIELD), vm(FIELD)],
    )
    got = lax.all_to_all(send, "row", 0, 0, tiled=True)
    out = call(
        last_kernel,
        [got, ypr, ygr, yrd, ysep, ysrd, ty],
        jax.ShapeDtypeStruct(FIELD, F32),
        scratch=[vm((Z * PITCH, N)), pltpu.SemaphoreType.DMA((Z,))],
        out_space=pl.ANY,
    )
    return out.reshape((Z, N, N))


def solution(mesh):
    specs = (P(None, "row", "col"),) * 3 + (P(), P())
    return jax.shard_map(
        local, mesh=mesh, in_specs=specs, out_specs=P(None, "row", "col"), check_vma=False
    )
```

```python
import jax
import jax.numpy as jnp
from jax import lax
from jax.experimental import pallas as pl
from jax.experimental.pallas import tpu as pltpu
from jax.sharding import PartitionSpec as P

Z, N = 8, 128
ROWS = Z * N
PITCH = N + 8
CHUNKS, STEP = 8, 16
F32 = jnp.float32
VM = pltpu.VMEM


def rcp(x):
    return pl.reciprocal(x, approx=True)


def link(a, b):
    return a * b * rcp(a + b)


def at(i):
    return pl.ds(pl.multiple_of(i * Z, Z), Z)


def strided(i):
    return pl.ds(i, Z, stride=PITCH)


def conductivity(t, reg, mag, soft):
    m = jnp.where(reg == 0, mag[0], jnp.where(reg == 1, mag[1], mag[2]))
    b = jnp.where(reg == 0, soft[0], jnp.where(reg == 1, soft[1], soft[2]))
    return m * jnp.exp(b * t)


def turn(src, dst):
    def body(z, _):
        lines = pl.ds(z, N, stride=Z)
        dst[lines, :] = src[lines, :].T
        return 0

    lax.fori_loop(0, Z, body, 0, unroll=True)


def factor(c_ref, pr_ref, gr_ref, rr_ref, sep_ref, net_ref, south=None, there=None):
    one = jnp.ones((Z, N), F32)
    zero = jnp.zeros((Z, N), F32)

    def cell(c, j, p, t, s, here, beyond=None):
        i = c * STEP + j
        edge = beyond is not None
        if not edge:
            beyond = c_ref[at(i + 1), :]
        g = link(here, beyond)
        if edge:
            g = jnp.where(there, g, 0.0)
        r = rcp(p + g + t)
        pr, gr = p * r, g * r
        pr_ref[at(i), :] = pr
        gr_ref[at(i), :] = gr
        rr_ref[at(i), :] = r
        return pr * g, gr * t if edge else 1.0 + gr * t, s + pr * t, beyond

    start = []
    for c in range(CHUNKS):
        here = c_ref[at(c * STEP + 1), :]
        start.append((link(c_ref[at(c * STEP), :], here), one, zero, here))

    def body(j, state):
        return [cell(c, j, *state[c]) for c in range(CHUNKS)]

    state = lax.fori_loop(1, STEP - 1, body, start, unroll=2)
    last = state[-1] if south is None else cell(CHUNKS - 1, STEP - 1, *state[-1], south)
    state = [cell(c, STEP - 1, *state[c]) for c in range(CHUNKS - 1)] + [last]
    q = state[0][0]
    left = 1.0 + state[0][2]
    t = state[0][1] + state[1][2]
    for c in range(1, CHUNKS):
        g = state[c][0]
        r = rcp(q + g + t)
        qr, gr = q * r, g * r
        sep_ref[0, c] = qr
        sep_ref[1, c] = gr
        sep_ref[2, c] = r
        left = left + qr * t
        t = state[c][1] + gr * t
        if c + 1 < CHUNKS:
            t = t + state[c + 1][2]
        q = qr * g
    net_ref[0] = q
    net_ref[1] = left
    net_ref[2] = t if south is None else jnp.where(there, t, 1.0)


def sweep(rhs, pr_ref, gr_ref, rr_ref, sep_ref, rd_ref, srd_ref, shared):
    def cell(c, j, d, s):
        i = c * STEP + j
        rd_ref[at(i), :] = rr_ref[at(i), :] * d
        beyond = gr_ref[at(i), :] * d
        if not (c == CHUNKS - 1 and isinstance(j, int)):
            beyond = rhs(i + 1) + beyond
        return beyond, s + pr_ref[at(i), :] * d

    def body(j, state):
        return [cell(c, j, *state[c]) for c in range(CHUNKS)]

    start = [(rhs(c * STEP + 1), jnp.zeros((Z, N), F32)) for c in range(CHUNKS)]
    state = lax.fori_loop(1, STEP - 1, body, start, unroll=True)
    last = cell(CHUNKS - 1, STEP - 1, *state[-1]) if shared else state[-1]
    state = [cell(c, STEP - 1, *state[c]) for c in range(CHUNKS - 1)] + [last]
    left = rhs(0) + state[0][1]
    d = state[0][0] + state[1][1]
    for c in range(1, CHUNKS):
        left = left + sep_ref[0, c] * d
        srd_ref[c] = sep_ref[2, c] * d
        d = state[c][0] + sep_ref[1, c] * d
        if c + 1 < CHUNKS:
            d = d + state[c + 1][1]
    return left, d


def back(ul, ur, pr_ref, gr_ref, rd_ref, sep_ref, srd_ref, put, shared):
    seps = [None] * CHUNKS + [ur]
    for c in range(CHUNKS - 1, 0, -1):
        seps[c] = srd_ref[c] + sep_ref[0, c] * ul + sep_ref[1, c] * seps[c + 1]
    seps[0] = ul
    for c in range(CHUNKS):
        put(c * STEP, seps[c])

    def cell(c, j, u):
        i = c * STEP + j
        v = rd_ref[at(i), :] + pr_ref[at(i), :] * seps[c] + gr_ref[at(i), :] * u
        put(i, v)
        return v

    if not shared:
        put(N - 1, ur)
    last = cell(CHUNKS - 1, STEP - 1, ur) if shared else ur
    state = [cell(c, STEP - 1, seps[c + 1]) for c in range(CHUNKS - 1)] + [last]

    def body(k, state):
        return [cell(c, STEP - 2 - k, state[c]) for c in range(CHUNKS)]

    lax.fori_loop(0, STEP - 2, body, state, unroll=True)


def joined(own, other, left):
    a = [jnp.where(left, x, y) for x, y in zip(own, other)]
    b = [jnp.where(left, y, x) for x, y in zip(own, other)]
    s, d = a[2] + b[1], a[4] + b[3]
    r = rcp(a[0] + b[0] + s)
    f, h = a[0] * r, b[0] * r
    return [f * b[0], a[1] + f * s, b[2] + h * s, a[3] + f * d, b[4] + h * d]


def ends(me, own, others):
    zero = jnp.zeros((Z, N), F32)
    yl = il = yr = ir = zero
    for k in reversed(range(len(others))):
        p = others[k]
        left = (me >> k) % 2 == 1
        far_s = jnp.where(left, p[1] + yl, p[2] + yr)
        far_d = jnp.where(left, p[3] + il, p[4] + ir)
        near_s = jnp.where(left, p[2], p[1])
        near_d = jnp.where(left, p[4], p[3])
        f = p[0] * rcp(p[0] + far_s)
        y, i = near_s + f * far_s, near_d + f * far_d
        yl, il = jnp.where(left, y, yl), jnp.where(left, i, il)
        yr, ir = jnp.where(left, yr, y), jnp.where(left, ir, i)
    sl, dl, sr, dr = own[1] + yl, own[3] + il, own[2] + yr, own[4] + ir
    r = rcp(own[0] + sl)
    f = own[0] * r
    ur = (dr + f * dl) * rcp(sr + f * sl)
    ul = (dl + own[0] * ur) * r
    return ul, ur


def edge_kernel(
    t_hbm, reg_hbm, mag_hbm, soft_hbm,
    up_ref, down_ref, par_ref, t_ref, reg_ref, mag_ref, soft_ref, sem,
):
    copies = [
        pltpu.make_async_copy(mag_hbm, mag_ref, sem.at[0]),
        pltpu.make_async_copy(soft_hbm, soft_ref, sem.at[1]),
    ]
    for k, first in enumerate((0, N - 8)):
        rows = pl.ds(first, 8)
        copies.append(pltpu.make_async_copy(t_hbm.at[:, rows, :], t_ref.at[k], sem.at[2 + k]))
        copies.append(pltpu.make_async_copy(reg_hbm.at[:, rows, :], reg_ref.at[k], sem.at[4 + k]))
    for copy in copies[2:] + copies[:2]:
        copy.start()
    for copy in copies:
        copy.wait()
    mag = [jnp.full((Z, N), mag_ref[k] * 1000.0) for k in range(3)]
    soft = [jnp.full((Z, N), -soft_ref[k]) for k in range(3)]
    for k in range(3):
        par_ref[k] = mag[k]
        par_ref[3 + k] = soft[k]
    for k, row, out in ((0, 0, up_ref), (1, 7, down_ref)):
        t = t_ref[k, :, row, :]
        out[0] = t
        out[1] = conductivity(t, reg_ref[k, :, row, :], mag, soft)


def first_kernel(
    par_ref, t_hbm, reg_hbm, s_hbm,
    ty_ref, cy_ref, r_ref, pr_ref, gr_ref, rr_ref, sep_ref, net_ref, face_ref,
    cx_ref, t_box, reg_box, s_box, sem,
):
    cuts = (0, N // 2 + 8, N)
    copies = [[], []]
    for k in range(2):
        rows = pl.ds(cuts[k], cuts[k + 1] - cuts[k])
        for j, (a, b) in enumerate(((t_hbm, t_box), (reg_hbm, reg_box), (s_hbm, s_box))):
            copies[k].append(pltpu.make_async_copy(a.at[:, rows, :], b.at[:, rows, :], sem.at[k, j]))
            copies[k][-1].start()
    t_ref, reg_ref, s_ref = (box.reshape(Z * PITCH, N) for box in (t_box, reg_box, s_box))
    mag = [par_ref[k] for k in range(3)]
    soft = [par_ref[3 + k] for k in range(3)]
    z = lax.broadcasted_iota(jnp.int32, (Z, N), 0)
    inner = jnp.where(z < Z - 1, 1.6e-4, 0.0)
    ground = jnp.where(z == 0, 8e-5, 0.0)

    def load(y):
        t = t_ref[strided(y), :]
        c = conductivity(t, reg_ref[strided(y), :], mag, soft)
        ty_ref[at(y), :] = t
        cy_ref[at(y), :] = c
        return t, c

    def row(y, t, c, before, after):
        flux = link(c, pltpu.roll(c, Z - 1, 0)) * (pltpu.roll(t, Z - 1, 0) - t) * inner
        up = flux - pltpu.roll(flux, 1, 0) - ground * (c * t)
        r_ref[at(y), :] = 2.0 * t + s_ref[strided(y), :] + 2.0 * (after - before) + up

    def step(y, t, c, before):
        tn, cn = load(y + 1)
        after = link(c, cn) * (tn - t)
        row(y, t, c, before, after)
        return tn, cn, after

    def body(k, state):
        for j in range(8):
            state = step(k * 8 + j, *state)
        return state

    for copy in copies[0]:
        copy.wait()
    state = *load(0), jnp.zeros((Z, N), F32)
    state = lax.fori_loop(0, N // 16, body, state)
    for copy in copies[1]:
        copy.wait()
    state = lax.fori_loop(N // 16, N // 8 - 1, body, state)
    for y in range(N - 8, N - 1):
        state = step(y, *state)
    row(N - 1, *state, jnp.zeros((Z, N), F32))
    turn(cy_ref, cx_ref)
    factor(cx_ref, pr_ref, gr_ref, rr_ref, sep_ref, net_ref)
    g, sl, sr = (net_ref[k] for k in range(3))
    cl, cr = cx_ref[at(0), :], cx_ref[at(N - 1), :]
    r = rcp(cl + g + sl)
    a, b = cl * r, g * r
    for k, v in enumerate((r, a, b)):
        face_ref[k] = v
    g, sr = a * g, sr + b * sl
    sl = a * sl
    r = rcp(g + cr + sr)
    a, b = g * r, cr * r
    for k, v in enumerate((r, a, b)):
        face_ref[3 + k] = v
    net_ref[0] = a * cr
    net_ref[1] = sl + a * sr
    net_ref[2] = b * sr


def side_kernel(
    r_ref, ty_ref, cy_ref, north_ref, south_ref, pr_ref, gr_ref, rr_ref, sep_ref, net_ref,
    face_ref, rd_ref, srd_ref, frd_ref, out_ref, rx_ref, ry_ref,
):
    me = lax.axis_index("row")
    ry_ref[...] = r_ref[...]
    for row, halo, there in ((0, north_ref, me > 0), (N - 1, south_ref, me < lax.axis_size("row") - 1)):
        i = slice(row * Z, row * Z + Z)
        flux = link(cy_ref[i, :], halo[1]) * (halo[0] - ty_ref[i, :])
        ry_ref[i, :] = r_ref[i, :] + jnp.where(there, 2.0 * flux, 0.0)
    turn(ry_ref, rx_ref)
    left, right = sweep(
        lambda i: rx_ref[at(i), :], pr_ref, gr_ref, rr_ref, sep_ref, rd_ref, srd_ref, False
    )
    for k in range(3):
        out_ref[k] = net_ref[k]
    right = right + face_ref[2] * left
    frd_ref[0] = face_ref[0] * left
    frd_ref[1] = face_ref[3] * right
    out_ref[3] = face_ref[1] * left + face_ref[4] * right
    out_ref[4] = face_ref[5] * right


def lines_kernel(c_ref, south_ref, *outs):
    there = lax.axis_index("row") < lax.axis_size("row") - 1
    factor(c_ref, *outs, south=south_ref[1], there=there)


def merge_kernel(axis, own_ref, other_ref, out_ref):
    left = lax.axis_index(axis) % 2 == 0
    new = joined([own_ref[k] for k in range(5)], [other_ref[k] for k in range(5)], left)
    for k in range(5):
        out_ref[k] = new[k]


def ring_kernel(axis, own_ref, before_ref, after_ref, across_ref, *outs):
    place = lax.axis_index(axis) // 2 % 4
    even = place % 2 == 0
    own, before, after, across = (
        [r[k] for k in range(5)] for r in (own_ref, before_ref, after_ref, across_ref)
    )
    near = [jnp.where(even, a, b) for a, b in zip(after, before)]
    far = [jnp.where(even, b, a) for a, b in zip(after, before)]
    pair = joined(own, near, even)
    rest = joined(across, far, even)
    every = joined(pair, rest, place < 2)
    for out, net in zip(outs, (near, rest, every)):
        for k in range(5):
            out[k] = net[k]


def middle_kernel(*refs):
    nets, refs = refs[:5], refs[5:]
    (
        face_ref, frd_ref, pr_ref, gr_ref, rd_ref, sep_ref, srd_ref, ty_ref,
        ypr_ref, ygr_ref, yrr_ref, ysep_ref, ynet_ref,
        yrd_ref, ysrd_ref, out_ref, wx_ref, wy_ref,
    ) = refs
    own, *others = ([r[k] for k in range(5)] for r in nets)
    ul, ur = ends(lax.axis_index("col"), own, others)
    ur = frd_ref[1] + face_ref[4] * ul + face_ref[5] * ur
    ul = frd_ref[0] + face_ref[1] * ul + face_ref[2] * ur

    def put(i, v):
        wx_ref[at(i), :] = v

    back(ul, ur, pr_ref, gr_ref, rd_ref, sep_ref, srd_ref, put, False)
    turn(wx_ref, wy_ref)
    left, right = sweep(
        lambda i: wy_ref[at(i), :] - 2.0 * ty_ref[at(i), :],
        ypr_ref, ygr_ref, yrr_ref, ysep_ref, yrd_ref, ysrd_ref, True,
    )
    for b in range(out_ref.shape[0]):
        for k in range(3):
            out_ref[b, k] = ynet_ref[k]
        out_ref[b, 3] = left
        out_ref[b, 4] = right


def last_kernel(
    all_ref, pr_ref, gr_ref, rd_ref, sep_ref, srd_ref, ty_ref, out_hbm, new_ref, sem
):
    me = lax.axis_index("row")
    place = lambda m: [all_ref[me ^ m, k] for k in range(5)]
    one, two = me % 2 == 0, me // 2 % 2 == 0
    own = place(0)
    far = joined(place(2), place(3), one)
    half = joined(joined(place(4), place(5), one), joined(place(6), place(7), one), two)
    ul, ur = ends(me, own, [place(1), far, half])

    def put(i, v):
        new_ref[strided(i), :] = v + ty_ref[at(i), :]

    back(ul, ur, pr_ref, gr_ref, rd_ref, sep_ref, srd_ref, put, True)
    copies = [
        pltpu.make_async_copy(
            new_ref.at[pl.ds(z * PITCH, N), :], out_hbm.at[pl.ds(z * N, N), :], sem.at[z]
        )
        for z in range(Z)
    ]
    for copy in copies:
        copy.start()
    for copy in copies:
        copy.wait()


FIELD = (ROWS, N)
SPACED = (Z, PITCH, N)
NET = (5, Z, N)
PART = (3, Z, N)
SEPS = (3, CHUNKS, Z, N)
SEPD = (CHUNKS, Z, N)


def vm(shape):
    return VM(shape, F32)


def call(kernel, args, outs, scratch=(), flops=0, out_space=VM, outside=()):
    args = [pltpu.with_memory_space_constraint(a, VM) for a in args]
    whole = pl.BlockSpec(memory_space=VM)
    many = isinstance(outs, tuple)
    return pl.pallas_call(
        kernel,
        in_specs=[whole] * len(args) + [pl.BlockSpec(memory_space=pltpu.HBM)] * len(outside),
        out_specs=(whole,) * len(outs) if many else pl.BlockSpec(memory_space=out_space),
        out_shape=outs,
        scratch_shapes=list(scratch),
        cost_estimate=pl.CostEstimate(flops=flops, bytes_accessed=flops, transcendentals=0),
        compiler_params=pltpu.CompilerParams(vmem_limit_bytes=16 * 1024 * 1024),
    )(*args, *(pltpu.with_memory_space_constraint(a, pltpu.HBM) for a in outside))


def partner(x, axis, mask):
    return lax.ppermute(x, axis, [(i, i ^ mask) for i in range(lax.axis_size(axis))])


def around(x, axis, shift):
    n = lax.axis_size(axis)
    to = lambda i: i // 8 * 8 + (i // 2 + shift) % 4 * 2 + (i + 1) % 2
    return lax.ppermute(x, axis, [(i, to(i)) for i in range(n)])


def spread_col(net, axis):
    other = partner(net, axis, 1)
    own = call(lambda *refs: merge_kernel(axis, *refs), [net, other], vm(NET))
    after = around(own, axis, 3)
    before = around(own, axis, 1)
    across = around(own, axis, 2)
    near, rest, every = call(
        lambda *refs: ring_kernel(axis, *refs), [own, before, after, across], (vm(NET),) * 3
    )
    return [other, near, rest, partner(every, axis, 9)]


def local(t, region, source, mag, soft):
    n = lax.axis_size("row")
    edge = (2, Z, 8, N)
    up, down, par = pl.pallas_call(
        edge_kernel,
        in_specs=[pl.BlockSpec(memory_space=pltpu.HBM)] * 4,
        out_specs=(pl.BlockSpec(memory_space=VM),) * 3,
        out_shape=(vm((2, Z, N)), vm((2, Z, N)), vm((6, Z, N))),
        scratch_shapes=[
            vm(edge), VM(edge, jnp.int32), pltpu.SMEM((3,), F32), pltpu.SMEM((3,), F32),
            pltpu.SemaphoreType.DMA((6,)),
        ],
    )(t, region, mag, soft)
    south = lax.ppermute(up, "row", [((i + 1) % n, i) for i in range(n)])
    north = lax.ppermute(down, "row", [(i, (i + 1) % n) for i in range(n)])
    ty, cy, r, pr, gr, rr, sep, net, face = call(
        first_kernel,
        [par],
        (vm(FIELD),) * 6 + (vm(SEPS), vm(PART), vm((6, Z, N))),
        scratch=[
            vm(FIELD), vm(SPACED), VM(SPACED, jnp.int32), vm(SPACED), pltpu.SemaphoreType.DMA((2, 3)),
        ],
        outside=[t, region, source],
        flops=20_000_000,
    )
    rd, srd, frd, own = call(
        side_kernel,
        [r, ty, cy, north, south, pr, gr, rr, sep, net, face],
        (vm(FIELD), vm(SEPD), vm((2, Z, N)), vm(NET)),
        scratch=[vm(FIELD), vm(FIELD)],
    )
    ypr, ygr, yrr, ysep, ynet = call(
        lines_kernel, [cy, south], (vm(FIELD),) * 3 + (vm(SEPS), vm(PART)), flops=5_000_000
    )
    others = spread_col(own, "col")
    yrd, ysrd, send = call(
        middle_kernel,
        [own] + others + [face, frd, pr, gr, rd, sep, srd, ty, ypr, ygr, yrr, ysep, ynet],
        (vm(FIELD), vm(SEPD), vm((n,) + NET)),
        scratch=[vm(FIELD), vm(FIELD)],
    )
    got = lax.all_to_all(send, "row", 0, 0, tiled=True)
    out = call(
        last_kernel,
        [got, ypr, ygr, yrd, ysep, ysrd, ty],
        jax.ShapeDtypeStruct(FIELD, F32),
        scratch=[vm((Z * PITCH, N)), pltpu.SemaphoreType.DMA((Z,))],
        out_space=pl.ANY,
    )
    return out.reshape((Z, N, N))


def solution(mesh):
    specs = (P(None, "row", "col"),) * 3 + (P(), P())
    return jax.shard_map(
        local, mesh=mesh, in_specs=specs, out_specs=P(None, "row", "col"), check_vma=False
    )
```

```python
import jax
import jax.numpy as jnp
from jax import lax
from jax.experimental import pallas as pl
from jax.experimental.pallas import tpu as pltpu
from jax.sharding import PartitionSpec as P

Z, N = 8, 128
ROWS = Z * N
PITCH = N + 8
CHUNKS, STEP = 8, 16
F32 = jnp.float32
VM = pltpu.VMEM


def rcp(x):
    return pl.reciprocal(x, approx=True)


def link(a, b):
    return a * b * rcp(a + b)


def at(i):
    return pl.ds(pl.multiple_of(i * Z, Z), Z)


def strided(i):
    return pl.ds(i, Z, stride=PITCH)


def conductivity(t, reg, mag, soft):
    m = jnp.where(reg == 0, mag[0], jnp.where(reg == 1, mag[1], mag[2]))
    b = jnp.where(reg == 0, soft[0], jnp.where(reg == 1, soft[1], soft[2]))
    return m * jnp.exp(b * t)


def turn(src, dst):
    def body(z, _):
        lines = pl.ds(z, N, stride=Z)
        dst[lines, :] = src[lines, :].T
        return 0

    lax.fori_loop(0, Z, body, 0, unroll=True)


def factor(c_ref, pr_ref, gr_ref, rr_ref, sep_ref, net_ref, south=None, there=None):
    one = jnp.ones((Z, N), F32)
    zero = jnp.zeros((Z, N), F32)

    def cell(c, j, p, t, s, here, beyond=None):
        i = c * STEP + j
        edge = beyond is not None
        if not edge:
            beyond = c_ref[at(i + 1), :]
        g = link(here, beyond)
        if edge:
            g = jnp.where(there, g, 0.0)
        r = rcp(p + g + t)
        pr, gr = p * r, g * r
        pr_ref[at(i), :] = pr
        gr_ref[at(i), :] = gr
        rr_ref[at(i), :] = r
        return pr * g, gr * t if edge else 1.0 + gr * t, s + pr * t, beyond

    start = []
    for c in range(CHUNKS):
        here = c_ref[at(c * STEP + 1), :]
        start.append((link(c_ref[at(c * STEP), :], here), one, zero, here))

    def body(j, state):
        return [cell(c, j, *state[c]) for c in range(CHUNKS)]

    state = lax.fori_loop(1, STEP - 1, body, start, unroll=2)
    last = state[-1] if south is None else cell(CHUNKS - 1, STEP - 1, *state[-1], south)
    state = [cell(c, STEP - 1, *state[c]) for c in range(CHUNKS - 1)] + [last]
    q = state[0][0]
    left = 1.0 + state[0][2]
    t = state[0][1] + state[1][2]
    for c in range(1, CHUNKS):
        g = state[c][0]
        r = rcp(q + g + t)
        qr, gr = q * r, g * r
        sep_ref[0, c] = qr
        sep_ref[1, c] = gr
        sep_ref[2, c] = r
        left = left + qr * t
        t = state[c][1] + gr * t
        if c + 1 < CHUNKS:
            t = t + state[c + 1][2]
        q = qr * g
    net_ref[0] = q
    net_ref[1] = left
    net_ref[2] = t if south is None else jnp.where(there, t, 1.0)


def sweep(rhs, pr_ref, gr_ref, rr_ref, sep_ref, rd_ref, srd_ref, shared):
    def cell(c, j, d, s):
        i = c * STEP + j
        rd_ref[at(i), :] = rr_ref[at(i), :] * d
        beyond = gr_ref[at(i), :] * d
        if not (c == CHUNKS - 1 and isinstance(j, int)):
            beyond = rhs(i + 1) + beyond
        return beyond, s + pr_ref[at(i), :] * d

    def body(j, state):
        return [cell(c, j, *state[c]) for c in range(CHUNKS)]

    start = [(rhs(c * STEP + 1), jnp.zeros((Z, N), F32)) for c in range(CHUNKS)]
    state = lax.fori_loop(1, STEP - 1, body, start, unroll=True)
    last = cell(CHUNKS - 1, STEP - 1, *state[-1]) if shared else state[-1]
    state = [cell(c, STEP - 1, *state[c]) for c in range(CHUNKS - 1)] + [last]
    left = rhs(0) + state[0][1]
    d = state[0][0] + state[1][1]
    for c in range(1, CHUNKS):
        left = left + sep_ref[0, c] * d
        srd_ref[c] = sep_ref[2, c] * d
        d = state[c][0] + sep_ref[1, c] * d
        if c + 1 < CHUNKS:
            d = d + state[c + 1][1]
    return left, d


def back(ul, ur, pr_ref, gr_ref, rd_ref, sep_ref, srd_ref, put, shared, groups=1, done=None):
    seps = [None] * CHUNKS + [ur]
    for c in range(CHUNKS - 1, 0, -1):
        seps[c] = srd_ref[c] + sep_ref[0, c] * ul + sep_ref[1, c] * seps[c + 1]
    seps[0] = ul

    def cell(c, j, u):
        i = c * STEP + j
        v = rd_ref[at(i), :] + pr_ref[at(i), :] * seps[c] + gr_ref[at(i), :] * u
        put(i, v)
        return v

    if not shared:
        put(N - 1, ur)
    size = CHUNKS // groups
    for group in reversed(range(groups)):
        chunks = range(group * size, group * size + size)
        state = []
        for c in chunks:
            put(c * STEP, seps[c])
            whole = shared or c < CHUNKS - 1
            state.append(cell(c, STEP - 1, seps[c + 1]) if whole else ur)

        def body(k, state):
            return [cell(c, STEP - 2 - k, u) for c, u in zip(chunks, state)]

        lax.fori_loop(0, STEP - 2, body, state, unroll=True)
        if done is not None:
            done(group)


def joined(own, other, left):
    a = [jnp.where(left, x, y) for x, y in zip(own, other)]
    b = [jnp.where(left, y, x) for x, y in zip(own, other)]
    s, d = a[2] + b[1], a[4] + b[3]
    r = rcp(a[0] + b[0] + s)
    f, h = a[0] * r, b[0] * r
    return [f * b[0], a[1] + f * s, b[2] + h * s, a[3] + f * d, b[4] + h * d]


def ends(me, own, others):
    zero = jnp.zeros((Z, N), F32)
    yl = il = yr = ir = zero
    for k in reversed(range(len(others))):
        p = others[k]
        left = (me >> k) % 2 == 1
        far_s = jnp.where(left, p[1] + yl, p[2] + yr)
        far_d = jnp.where(left, p[3] + il, p[4] + ir)
        near_s = jnp.where(left, p[2], p[1])
        near_d = jnp.where(left, p[4], p[3])
        f = p[0] * rcp(p[0] + far_s)
        y, i = near_s + f * far_s, near_d + f * far_d
        yl, il = jnp.where(left, y, yl), jnp.where(left, i, il)
        yr, ir = jnp.where(left, yr, y), jnp.where(left, ir, i)
    sl, dl, sr, dr = own[1] + yl, own[3] + il, own[2] + yr, own[4] + ir
    r = rcp(own[0] + sl)
    f = own[0] * r
    ur = (dr + f * dl) * rcp(sr + f * sl)
    ul = (dl + own[0] * ur) * r
    return ul, ur


def edge_kernel(t_hbm, reg_hbm, up_ref, down_ref, t_ref, reg_ref, sem):
    copies = []
    for k, first in enumerate((0, N - 8)):
        rows = pl.ds(first, 8)
        copies.append(pltpu.make_async_copy(t_hbm.at[:, rows, :], t_ref.at[k], sem.at[0, k]))
        copies.append(pltpu.make_async_copy(reg_hbm.at[:, rows, :], reg_ref.at[k], sem.at[1, k]))
    for copy in copies:
        copy.start()
    for copy in copies:
        copy.wait()
    for k, row, out in ((0, 0, up_ref), (1, 7, down_ref)):
        out[0] = t_ref[k, :, row, :]
        out[1] = reg_ref[k, :, row, :].astype(F32)


def first_kernel(
    t_hbm, reg_hbm, s_hbm, mag_hbm, soft_hbm,
    par_ref, ty_ref, cy_ref, r_ref, pr_ref, gr_ref, rr_ref, sep_ref, net_ref, face_ref,
    cx_ref, t_box, reg_box, s_box, mag_ref, soft_ref, sem, small_sem,
):
    small = [
        pltpu.make_async_copy(mag_hbm, mag_ref, small_sem.at[0]),
        pltpu.make_async_copy(soft_hbm, soft_ref, small_sem.at[1]),
    ]
    for copy in small:
        copy.start()
    cuts = (0, N // 2 + 8, N)
    copies = [[], []]
    for k in range(2):
        rows = pl.ds(cuts[k], cuts[k + 1] - cuts[k])
        for j, (a, b) in enumerate(((t_hbm, t_box), (reg_hbm, reg_box), (s_hbm, s_box))):
            copies[k].append(pltpu.make_async_copy(a.at[:, rows, :], b.at[:, rows, :], sem.at[k, j]))
            copies[k][-1].start()
    t_ref, reg_ref, s_ref = (box.reshape(Z * PITCH, N) for box in (t_box, reg_box, s_box))
    for copy in small:
        copy.wait()
    mag = [jnp.full((Z, N), mag_ref[k] * 1000.0) for k in range(3)]
    soft = [jnp.full((Z, N), -soft_ref[k]) for k in range(3)]
    for k in range(3):
        par_ref[k] = mag[k]
        par_ref[3 + k] = soft[k]
    z = lax.broadcasted_iota(jnp.int32, (Z, N), 0)
    inner = jnp.where(z < Z - 1, 1.6e-4, 0.0)
    ground = jnp.where(z == 0, 8e-5, 0.0)

    def load(y):
        t = t_ref[strided(y), :]
        c = conductivity(t, reg_ref[strided(y), :], mag, soft)
        ty_ref[at(y), :] = t
        cy_ref[at(y), :] = c
        return t, c

    def row(y, t, c, before, after):
        flux = link(c, pltpu.roll(c, Z - 1, 0)) * (pltpu.roll(t, Z - 1, 0) - t) * inner
        up = flux - pltpu.roll(flux, 1, 0) - ground * (c * t)
        r_ref[at(y), :] = 2.0 * t + s_ref[strided(y), :] + 2.0 * (after - before) + up

    def step(y, t, c, before):
        tn, cn = load(y + 1)
        after = link(c, cn) * (tn - t)
        row(y, t, c, before, after)
        return tn, cn, after

    def body(k, state):
        for j in range(8):
            state = step(k * 8 + j, *state)
        return state

    for copy in copies[0]:
        copy.wait()
    state = *load(0), jnp.zeros((Z, N), F32)
    state = lax.fori_loop(0, N // 16, body, state)
    for copy in copies[1]:
        copy.wait()
    state = lax.fori_loop(N // 16, N // 8 - 1, body, state)
    for y in range(N - 8, N - 1):
        state = step(y, *state)
    row(N - 1, *state, jnp.zeros((Z, N), F32))
    turn(cy_ref, cx_ref)
    factor(cx_ref, pr_ref, gr_ref, rr_ref, sep_ref, net_ref)
    g, sl, sr = (net_ref[k] for k in range(3))
    cl, cr = cx_ref[at(0), :], cx_ref[at(N - 1), :]
    r = rcp(cl + g + sl)
    a, b = cl * r, g * r
    for k, v in enumerate((r, a, b)):
        face_ref[k] = v
    g, sr = a * g, sr + b * sl
    sl = a * sl
    r = rcp(g + cr + sr)
    a, b = g * r, cr * r
    for k, v in enumerate((r, a, b)):
        face_ref[3 + k] = v
    net_ref[0] = a * cr
    net_ref[1] = sl + a * sr
    net_ref[2] = b * sr


def side_kernel(
    par_ref, r_ref, ty_ref, cy_ref, north_ref, south_ref, pr_ref, gr_ref, rr_ref, sep_ref, net_ref,
    face_ref, rd_ref, srd_ref, frd_ref, out_ref, beyond_ref, rx_ref, ry_ref,
):
    me = lax.axis_index("row")
    mag = [par_ref[k] for k in range(3)]
    soft = [par_ref[3 + k] for k in range(3)]
    ry_ref[...] = r_ref[...]
    for row, halo, there in ((0, north_ref, me > 0), (N - 1, south_ref, me < lax.axis_size("row") - 1)):
        i = slice(row * Z, row * Z + Z)
        beyond = conductivity(halo[0], halo[1], mag, soft)
        flux = link(cy_ref[i, :], beyond) * (halo[0] - ty_ref[i, :])
        ry_ref[i, :] = r_ref[i, :] + jnp.where(there, 2.0 * flux, 0.0)
    beyond_ref[...] = beyond
    turn(ry_ref, rx_ref)
    left, right = sweep(
        lambda i: rx_ref[at(i), :], pr_ref, gr_ref, rr_ref, sep_ref, rd_ref, srd_ref, False
    )
    for k in range(3):
        out_ref[k] = net_ref[k]
    right = right + face_ref[2] * left
    frd_ref[0] = face_ref[0] * left
    frd_ref[1] = face_ref[3] * right
    out_ref[3] = face_ref[1] * left + face_ref[4] * right
    out_ref[4] = face_ref[5] * right


def lines_kernel(c_ref, south_ref, *outs):
    there = lax.axis_index("row") < lax.axis_size("row") - 1
    factor(c_ref, *outs, south=south_ref[...], there=there)


def merge_kernel(axis, own_ref, other_ref, out_ref):
    left = lax.axis_index(axis) % 2 == 0
    new = joined([own_ref[k] for k in range(5)], [other_ref[k] for k in range(5)], left)
    for k in range(5):
        out_ref[k] = new[k]


def ring_kernel(axis, own_ref, before_ref, after_ref, across_ref, *outs):
    place = lax.axis_index(axis) // 2 % 4
    even = place % 2 == 0
    own, before, after, across = (
        [r[k] for k in range(5)] for r in (own_ref, before_ref, after_ref, across_ref)
    )
    near = [jnp.where(even, a, b) for a, b in zip(after, before)]
    far = [jnp.where(even, b, a) for a, b in zip(after, before)]
    pair = joined(own, near, even)
    rest = joined(across, far, even)
    every = joined(pair, rest, place < 2)
    for out, net in zip(outs, (near, rest, every)):
        for k in range(5):
            out[k] = net[k]


def middle_kernel(*refs):
    nets, refs = refs[:5], refs[5:]
    (
        face_ref, frd_ref, pr_ref, gr_ref, rd_ref, sep_ref, srd_ref, ty_ref,
        ypr_ref, ygr_ref, yrr_ref, ysep_ref, ynet_ref,
        yrd_ref, ysrd_ref, out_ref, wx_ref, wy_ref,
    ) = refs
    own, *others = ([r[k] for k in range(5)] for r in nets)
    ul, ur = ends(lax.axis_index("col"), own, others)
    ur = frd_ref[1] + face_ref[4] * ul + face_ref[5] * ur
    ul = frd_ref[0] + face_ref[1] * ul + face_ref[2] * ur

    def put(i, v):
        wx_ref[at(i), :] = v

    back(ul, ur, pr_ref, gr_ref, rd_ref, sep_ref, srd_ref, put, False)
    turn(wx_ref, wy_ref)
    left, right = sweep(
        lambda i: wy_ref[at(i), :] - 2.0 * ty_ref[at(i), :],
        ypr_ref, ygr_ref, yrr_ref, ysep_ref, yrd_ref, ysrd_ref, True,
    )
    for b in range(out_ref.shape[0]):
        for k in range(3):
            out_ref[b, k] = ynet_ref[k]
        out_ref[b, 3] = left
        out_ref[b, 4] = right


def last_kernel(
    all_ref, pr_ref, gr_ref, rd_ref, sep_ref, srd_ref, ty_ref, out_hbm, box, sem
):
    new_ref = box.reshape(Z * PITCH, N)
    me = lax.axis_index("row")
    place = lambda m: [all_ref[me ^ m, k] for k in range(5)]
    one, two = me % 2 == 0, me // 2 % 2 == 0
    own = place(0)
    far = joined(place(2), place(3), one)
    half = joined(joined(place(4), place(5), one), joined(place(6), place(7), one), two)
    ul, ur = ends(me, own, [place(1), far, half])

    def put(i, v):
        new_ref[strided(i), :] = v + ty_ref[at(i), :]

    copies = []

    def send(group):
        rows = pl.ds(group * (N // 2), N // 2)
        copies.append(
            pltpu.make_async_copy(box.at[:, rows, :], out_hbm.at[:, rows, :], sem.at[group])
        )
        copies[-1].start()

    back(ul, ur, pr_ref, gr_ref, rd_ref, sep_ref, srd_ref, put, True, 2, send)
    for copy in copies:
        copy.wait()


FIELD = (ROWS, N)
SPACED = (Z, PITCH, N)
NET = (5, Z, N)
PART = (3, Z, N)
SEPS = (3, CHUNKS, Z, N)
SEPD = (CHUNKS, Z, N)


def vm(shape):
    return VM(shape, F32)


def call(kernel, args, outs, scratch=(), flops=0, out_space=VM, outside=()):
    args = [pltpu.with_memory_space_constraint(a, VM) for a in args]
    whole = pl.BlockSpec(memory_space=VM)
    many = isinstance(outs, tuple)
    return pl.pallas_call(
        kernel,
        in_specs=[whole] * len(args) + [pl.BlockSpec(memory_space=pltpu.HBM)] * len(outside),
        out_specs=(whole,) * len(outs) if many else pl.BlockSpec(memory_space=out_space),
        out_shape=outs,
        scratch_shapes=list(scratch),
        cost_estimate=pl.CostEstimate(flops=flops, bytes_accessed=flops, transcendentals=0),
        compiler_params=pltpu.CompilerParams(vmem_limit_bytes=16 * 1024 * 1024),
    )(*args, *(pltpu.with_memory_space_constraint(a, pltpu.HBM) for a in outside))


def partner(x, axis, mask):
    return lax.ppermute(x, axis, [(i, i ^ mask) for i in range(lax.axis_size(axis))])


def around(x, axis, shift):
    n = lax.axis_size(axis)
    to = lambda i: i // 8 * 8 + (i // 2 + shift) % 4 * 2 + (i + 1) % 2
    return lax.ppermute(x, axis, [(i, to(i)) for i in range(n)])


def spread_col(net, axis):
    other = partner(net, axis, 1)
    own = call(lambda *refs: merge_kernel(axis, *refs), [net, other], vm(NET))
    after = around(own, axis, 3)
    before = around(own, axis, 1)
    across = around(own, axis, 2)
    near, rest, every = call(
        lambda *refs: ring_kernel(axis, *refs), [own, before, after, across], (vm(NET),) * 3
    )
    return [other, near, rest, partner(every, axis, 9)]


def local(t, region, source, mag, soft):
    n = lax.axis_size("row")
    edge = (2, Z, 8, N)
    up, down = pl.pallas_call(
        edge_kernel,
        in_specs=[pl.BlockSpec(memory_space=pltpu.HBM)] * 2,
        out_specs=(pl.BlockSpec(memory_space=VM),) * 2,
        out_shape=(vm((2, Z, N)),) * 2,
        scratch_shapes=[vm(edge), VM(edge, jnp.int32), pltpu.SemaphoreType.DMA((2, 2))],
    )(t, region)
    south = lax.ppermute(up, "row", [((i + 1) % n, i) for i in range(n)])
    north = lax.ppermute(down, "row", [(i, (i + 1) % n) for i in range(n)])
    par, ty, cy, r, pr, gr, rr, sep, net, face = call(
        first_kernel,
        [],
        (vm((6, Z, N)),) + (vm(FIELD),) * 6 + (vm(SEPS), vm(PART), vm((6, Z, N))),
        scratch=[
            vm(FIELD), vm(SPACED), VM(SPACED, jnp.int32), vm(SPACED),
            pltpu.SMEM((3,), F32), pltpu.SMEM((3,), F32),
            pltpu.SemaphoreType.DMA((2, 3)), pltpu.SemaphoreType.DMA((2,)),
        ],
        outside=[t, region, source, mag, soft],
        flops=20_000_000,
    )
    rd, srd, frd, own, beyond = call(
        side_kernel,
        [par, r, ty, cy, north, south, pr, gr, rr, sep, net, face],
        (vm(FIELD), vm(SEPD), vm((2, Z, N)), vm(NET), vm((Z, N))),
        scratch=[vm(FIELD), vm(FIELD)],
    )
    ypr, ygr, yrr, ysep, ynet = call(
        lines_kernel, [cy, beyond], (vm(FIELD),) * 3 + (vm(SEPS), vm(PART)), flops=5_000_000
    )
    others = spread_col(own, "col")
    yrd, ysrd, send = call(
        middle_kernel,
        [own] + others + [face, frd, pr, gr, rd, sep, srd, ty, ypr, ygr, yrr, ysep, ynet],
        (vm(FIELD), vm(SEPD), vm((n,) + NET)),
        scratch=[vm(FIELD), vm(FIELD)],
    )
    got = lax.all_to_all(send, "row", 0, 0, tiled=True)
    out = call(
        last_kernel,
        [got, ypr, ygr, yrd, ysep, ysrd, ty],
        jax.ShapeDtypeStruct((Z, N, N), F32),
        scratch=[vm(SPACED), pltpu.SemaphoreType.DMA((2,))],
        out_space=pl.ANY,
    )
    return out


def solution(mesh):
    specs = (P(None, "row", "col"),) * 3 + (P(), P())
    return jax.shard_map(
        local, mesh=mesh, in_specs=specs, out_specs=P(None, "row", "col"), check_vma=False
    )
```

```python
import jax
import jax.numpy as jnp
from jax import lax
from jax.experimental import pallas as pl
from jax.experimental.pallas import tpu as pltpu
from jax.sharding import PartitionSpec as P

Z, N = 8, 128
ROWS = Z * N
PITCH = N + 8
CHUNKS, STEP = 8, 16
F32 = jnp.float32
VM = pltpu.VMEM


def rcp(x):
    return pl.reciprocal(x, approx=True)


def link(a, b):
    return a * b * rcp(a + b)


def at(i):
    return pl.ds(pl.multiple_of(i * Z, Z), Z)


def strided(i):
    return pl.ds(i, Z, stride=PITCH)


def conductivity(t, reg, mag, soft):
    m = jnp.where(reg == 0, mag[0], jnp.where(reg == 1, mag[1], mag[2]))
    b = jnp.where(reg == 0, soft[0], jnp.where(reg == 1, soft[1], soft[2]))
    return m * jnp.exp(b * t)


def turn(src, dst):
    def body(z, _):
        lines = pl.ds(z, N, stride=Z)
        dst[lines, :] = src[lines, :].T
        return 0

    lax.fori_loop(0, Z, body, 0, unroll=True)


def factor(c_ref, pr_ref, gr_ref, rr_ref, sep_ref, net_ref, south=None, there=None):
    one = jnp.ones((Z, N), F32)
    zero = jnp.zeros((Z, N), F32)

    def cell(c, j, p, t, s, here, beyond=None):
        i = c * STEP + j
        edge = beyond is not None
        if not edge:
            beyond = c_ref[at(i + 1), :]
        g = link(here, beyond)
        if edge:
            g = jnp.where(there, g, 0.0)
        r = rcp(p + g + t)
        pr, gr = p * r, g * r
        pr_ref[at(i), :] = pr
        gr_ref[at(i), :] = gr
        rr_ref[at(i), :] = r
        return pr * g, gr * t if edge else 1.0 + gr * t, s + pr * t, beyond

    start = []
    for c in range(CHUNKS):
        here = c_ref[at(c * STEP + 1), :]
        start.append((link(c_ref[at(c * STEP), :], here), one, zero, here))

    def body(j, state):
        return [cell(c, j, *state[c]) for c in range(CHUNKS)]

    state = lax.fori_loop(1, STEP - 1, body, start, unroll=2)
    last = state[-1] if south is None else cell(CHUNKS - 1, STEP - 1, *state[-1], south)
    state = [cell(c, STEP - 1, *state[c]) for c in range(CHUNKS - 1)] + [last]
    q = state[0][0]
    left = 1.0 + state[0][2]
    t = state[0][1] + state[1][2]
    for c in range(1, CHUNKS):
        g = state[c][0]
        r = rcp(q + g + t)
        qr, gr = q * r, g * r
        sep_ref[0, c] = qr
        sep_ref[1, c] = gr
        sep_ref[2, c] = r
        left = left + qr * t
        t = state[c][1] + gr * t
        if c + 1 < CHUNKS:
            t = t + state[c + 1][2]
        q = qr * g
    net_ref[0] = q
    net_ref[1] = left
    net_ref[2] = t if south is None else jnp.where(there, t, 1.0)


def sweep(rhs, pr_ref, gr_ref, rr_ref, sep_ref, rd_ref, srd_ref, shared):
    def cell(c, j, d, s):
        i = c * STEP + j
        rd_ref[at(i), :] = rr_ref[at(i), :] * d
        beyond = gr_ref[at(i), :] * d
        if not (c == CHUNKS - 1 and isinstance(j, int)):
            beyond = rhs(i + 1) + beyond
        return beyond, s + pr_ref[at(i), :] * d

    def body(j, state):
        return [cell(c, j, *state[c]) for c in range(CHUNKS)]

    start = [(rhs(c * STEP + 1), jnp.zeros((Z, N), F32)) for c in range(CHUNKS)]
    state = lax.fori_loop(1, STEP - 1, body, start, unroll=True)
    last = cell(CHUNKS - 1, STEP - 1, *state[-1]) if shared else state[-1]
    state = [cell(c, STEP - 1, *state[c]) for c in range(CHUNKS - 1)] + [last]
    left = rhs(0) + state[0][1]
    d = state[0][0] + state[1][1]
    for c in range(1, CHUNKS):
        left = left + sep_ref[0, c] * d
        srd_ref[c] = sep_ref[2, c] * d
        d = state[c][0] + sep_ref[1, c] * d
        if c + 1 < CHUNKS:
            d = d + state[c + 1][1]
    return left, d


def back(ul, ur, pr_ref, gr_ref, rd_ref, sep_ref, srd_ref, put, shared, groups=1, done=None):
    seps = [None] * CHUNKS + [ur]
    for c in range(CHUNKS - 1, 0, -1):
        seps[c] = srd_ref[c] + sep_ref[0, c] * ul + sep_ref[1, c] * seps[c + 1]
    seps[0] = ul

    def cell(c, j, u):
        i = c * STEP + j
        v = rd_ref[at(i), :] + pr_ref[at(i), :] * seps[c] + gr_ref[at(i), :] * u
        put(i, v)
        return v

    if not shared:
        put(N - 1, ur)
    size = CHUNKS // groups
    for group in reversed(range(groups)):
        chunks = range(group * size, group * size + size)
        state = []
        for c in chunks:
            put(c * STEP, seps[c])
            whole = shared or c < CHUNKS - 1
            state.append(cell(c, STEP - 1, seps[c + 1]) if whole else ur)

        def body(k, state):
            return [cell(c, STEP - 2 - k, u) for c, u in zip(chunks, state)]

        lax.fori_loop(0, STEP - 2, body, state, unroll=True)
        if done is not None:
            done(group)


def joined(own, other, left):
    a = [jnp.where(left, x, y) for x, y in zip(own, other)]
    b = [jnp.where(left, y, x) for x, y in zip(own, other)]
    s, d = a[2] + b[1], a[4] + b[3]
    r = rcp(a[0] + b[0] + s)
    f, h = a[0] * r, b[0] * r
    return [f * b[0], a[1] + f * s, b[2] + h * s, a[3] + f * d, b[4] + h * d]


def ends(me, own, others):
    zero = jnp.zeros((Z, N), F32)
    yl = il = yr = ir = zero
    for k in reversed(range(len(others))):
        p = others[k]
        left = (me >> k) % 2 == 1
        far_s = jnp.where(left, p[1] + yl, p[2] + yr)
        far_d = jnp.where(left, p[3] + il, p[4] + ir)
        near_s = jnp.where(left, p[2], p[1])
        near_d = jnp.where(left, p[4], p[3])
        f = p[0] * rcp(p[0] + far_s)
        y, i = near_s + f * far_s, near_d + f * far_d
        yl, il = jnp.where(left, y, yl), jnp.where(left, i, il)
        yr, ir = jnp.where(left, yr, y), jnp.where(left, ir, i)
    sl, dl, sr, dr = own[1] + yl, own[3] + il, own[2] + yr, own[4] + ir
    r = rcp(own[0] + sl)
    f = own[0] * r
    ur = (dr + f * dl) * rcp(sr + f * sl)
    ul = (dl + own[0] * ur) * r
    return ul, ur


def edge_kernel(t_hbm, reg_hbm, up_ref, down_ref, t_ref, reg_ref, sem):
    copies = []
    for k, first in enumerate((0, N - 8)):
        rows = pl.ds(first, 8)
        copies.append(pltpu.make_async_copy(t_hbm.at[:, rows, :], t_ref.at[k], sem.at[0, k]))
        copies.append(pltpu.make_async_copy(reg_hbm.at[:, rows, :], reg_ref.at[k], sem.at[1, k]))
    for copy in copies:
        copy.start()
    for copy in copies:
        copy.wait()
    for k, row, out in ((0, 0, up_ref), (1, 7, down_ref)):
        out[0] = t_ref[k, :, row, :]
        out[1] = reg_ref[k, :, row, :].astype(F32)


def first_kernel(
    t_hbm, reg_hbm, s_hbm, mag_hbm, soft_hbm,
    par_ref, ty_ref, cy_ref, r_ref, pr_ref, gr_ref, rr_ref, sep_ref, net_ref, face_ref,
    cx_ref, t_box, reg_box, s_box, mag_ref, soft_ref, sem, small_sem,
):
    small = [
        pltpu.make_async_copy(mag_hbm, mag_ref, small_sem.at[0]),
        pltpu.make_async_copy(soft_hbm, soft_ref, small_sem.at[1]),
    ]
    for copy in small:
        copy.start()
    cuts = (0, N // 2 + 8, N)
    copies = [[], []]
    for k in range(2):
        rows = pl.ds(cuts[k], cuts[k + 1] - cuts[k])
        for j, (a, b) in enumerate(((t_hbm, t_box), (reg_hbm, reg_box), (s_hbm, s_box))):
            copies[k].append(pltpu.make_async_copy(a.at[:, rows, :], b.at[:, rows, :], sem.at[k, j]))
            copies[k][-1].start()
    t_ref, reg_ref, s_ref = (box.reshape(Z * PITCH, N) for box in (t_box, reg_box, s_box))
    for copy in small:
        copy.wait()
    mag = [jnp.full((Z, N), mag_ref[k] * 1000.0) for k in range(3)]
    soft = [jnp.full((Z, N), -soft_ref[k]) for k in range(3)]
    for k in range(3):
        par_ref[k] = mag[k]
        par_ref[3 + k] = soft[k]
    z = lax.broadcasted_iota(jnp.int32, (Z, N), 0)
    inner = jnp.where(z < Z - 1, 1.6e-4, 0.0)
    ground = jnp.where(z == 0, 8e-5, 0.0)

    def load(y):
        t = t_ref[strided(y), :]
        c = conductivity(t, reg_ref[strided(y), :], mag, soft)
        ty_ref[at(y), :] = t
        cy_ref[at(y), :] = c
        return t, c

    def row(y, t, c, before, after):
        flux = link(c, pltpu.roll(c, Z - 1, 0)) * (pltpu.roll(t, Z - 1, 0) - t) * inner
        up = flux - pltpu.roll(flux, 1, 0) - ground * (c * t)
        r_ref[at(y), :] = 2.0 * t + s_ref[strided(y), :] + 2.0 * (after - before) + up

    def step(y, t, c, before):
        tn, cn = load(y + 1)
        after = link(c, cn) * (tn - t)
        row(y, t, c, before, after)
        return tn, cn, after

    def body(k, state):
        for j in range(8):
            state = step(k * 8 + j, *state)
        return state

    for copy in copies[0]:
        copy.wait()
    state = *load(0), jnp.zeros((Z, N), F32)
    state = lax.fori_loop(0, N // 16, body, state)
    for copy in copies[1]:
        copy.wait()
    state = lax.fori_loop(N // 16, N // 8 - 1, body, state)
    for y in range(N - 8, N - 1):
        state = step(y, *state)
    row(N - 1, *state, jnp.zeros((Z, N), F32))
    turn(cy_ref, cx_ref)
    factor(cx_ref, pr_ref, gr_ref, rr_ref, sep_ref, net_ref)
    g, sl, sr = (net_ref[k] for k in range(3))
    cl, cr = cx_ref[at(0), :], cx_ref[at(N - 1), :]
    r = rcp(cl + g + sl)
    a, b = cl * r, g * r
    for k, v in enumerate((r, a, b)):
        face_ref[k] = v
    g, sr = a * g, sr + b * sl
    sl = a * sl
    r = rcp(g + cr + sr)
    a, b = g * r, cr * r
    for k, v in enumerate((r, a, b)):
        face_ref[3 + k] = v
    net_ref[0] = a * cr
    net_ref[1] = sl + a * sr
    net_ref[2] = b * sr


def side_kernel(
    par_ref, r_ref, ty_ref, cy_ref, north_ref, south_ref, pr_ref, gr_ref, rr_ref, sep_ref, net_ref,
    face_ref, rd_ref, srd_ref, frd_ref, out_ref, beyond_ref, rx_ref, ry_ref,
):
    me = lax.axis_index("row")
    mag = [par_ref[k] for k in range(3)]
    soft = [par_ref[3 + k] for k in range(3)]
    ry_ref[...] = r_ref[...]
    for row, halo, there in ((0, north_ref, me > 0), (N - 1, south_ref, me < lax.axis_size("row") - 1)):
        i = slice(row * Z, row * Z + Z)
        beyond = conductivity(halo[0], halo[1], mag, soft)
        flux = link(cy_ref[i, :], beyond) * (halo[0] - ty_ref[i, :])
        ry_ref[i, :] = r_ref[i, :] + jnp.where(there, 2.0 * flux, 0.0)
    beyond_ref[...] = beyond
    turn(ry_ref, rx_ref)
    left, right = sweep(
        lambda i: rx_ref[at(i), :], pr_ref, gr_ref, rr_ref, sep_ref, rd_ref, srd_ref, False
    )
    for k in range(3):
        out_ref[k] = net_ref[k]
    right = right + face_ref[2] * left
    frd_ref[0] = face_ref[0] * left
    frd_ref[1] = face_ref[3] * right
    out_ref[3] = face_ref[1] * left + face_ref[4] * right
    out_ref[4] = face_ref[5] * right


def lines_kernel(c_ref, south_ref, *outs):
    there = lax.axis_index("row") < lax.axis_size("row") - 1
    factor(c_ref, *outs, south=south_ref[...], there=there)


def level_kernel(axis, level, own_ref, other_ref, out_ref):
    left = (lax.axis_index(axis) >> level) % 2 == 0
    new = joined([own_ref[k] for k in range(5)], [other_ref[k] for k in range(5)], left)
    for k in range(5):
        out_ref[k] = new[k]


def middle_kernel(*refs):
    nets, refs = refs[:5], refs[5:]
    (
        face_ref, frd_ref, pr_ref, gr_ref, rd_ref, sep_ref, srd_ref, ty_ref,
        ypr_ref, ygr_ref, yrr_ref, ysep_ref, ynet_ref,
        yrd_ref, ysrd_ref, out_ref, wx_ref, wy_ref,
    ) = refs
    own, *others = ([r[k] for k in range(5)] for r in nets)
    ul, ur = ends(lax.axis_index("col"), own, others)
    ur = frd_ref[1] + face_ref[4] * ul + face_ref[5] * ur
    ul = frd_ref[0] + face_ref[1] * ul + face_ref[2] * ur

    def put(i, v):
        wx_ref[at(i), :] = v

    back(ul, ur, pr_ref, gr_ref, rd_ref, sep_ref, srd_ref, put, False)
    turn(wx_ref, wy_ref)
    left, right = sweep(
        lambda i: wy_ref[at(i), :] - 2.0 * ty_ref[at(i), :],
        ypr_ref, ygr_ref, yrr_ref, ysep_ref, yrd_ref, ysrd_ref, True,
    )
    for b in range(out_ref.shape[0]):
        for k in range(3):
            out_ref[b, k] = ynet_ref[k]
        out_ref[b, 3] = left
        out_ref[b, 4] = right


def last_kernel(
    all_ref, pr_ref, gr_ref, rd_ref, sep_ref, srd_ref, ty_ref, out_hbm, box, sem
):
    new_ref = box.reshape(Z * PITCH, N)
    me = lax.axis_index("row")
    place = lambda m: [all_ref[me ^ m, k] for k in range(5)]
    one, two = me % 2 == 0, me // 2 % 2 == 0
    own = place(0)
    far = joined(place(2), place(3), one)
    half = joined(joined(place(4), place(5), one), joined(place(6), place(7), one), two)
    ul, ur = ends(me, own, [place(1), far, half])

    def put(i, v):
        new_ref[strided(i), :] = v + ty_ref[at(i), :]

    copies = []

    def send(group):
        rows = pl.ds(group * (N // 2), N // 2)
        copies.append(
            pltpu.make_async_copy(box.at[:, rows, :], out_hbm.at[:, rows, :], sem.at[group])
        )
        copies[-1].start()

    back(ul, ur, pr_ref, gr_ref, rd_ref, sep_ref, srd_ref, put, True, 2, send)
    for copy in copies:
        copy.wait()


FIELD = (ROWS, N)
SPACED = (Z, PITCH, N)
NET = (5, Z, N)
PART = (3, Z, N)
SEPS = (3, CHUNKS, Z, N)
SEPD = (CHUNKS, Z, N)


def vm(shape):
    return VM(shape, F32)


def call(kernel, args, outs, scratch=(), flops=0, out_space=VM, outside=()):
    args = [pltpu.with_memory_space_constraint(a, VM) for a in args]
    whole = pl.BlockSpec(memory_space=VM)
    many = isinstance(outs, tuple)
    return pl.pallas_call(
        kernel,
        in_specs=[whole] * len(args) + [pl.BlockSpec(memory_space=pltpu.HBM)] * len(outside),
        out_specs=(whole,) * len(outs) if many else pl.BlockSpec(memory_space=out_space),
        out_shape=outs,
        scratch_shapes=list(scratch),
        cost_estimate=pl.CostEstimate(flops=flops, bytes_accessed=flops, transcendentals=0),
        compiler_params=pltpu.CompilerParams(vmem_limit_bytes=16 * 1024 * 1024),
    )(*args, *(pltpu.with_memory_space_constraint(a, pltpu.HBM) for a in outside))


def partner(x, axis, mask):
    return lax.ppermute(x, axis, [(i, i ^ mask) for i in range(lax.axis_size(axis))])


def spread_col(net, axis):
    others = []
    for level, mask in enumerate((1, 3, 5, 9)):
        others.append(partner(net, axis, mask))
        if level < 3:
            kernel = lambda *refs, level=level: level_kernel(axis, level, *refs)
            net = call(kernel, [net, others[-1]], vm(NET))
    return others


def local(t, region, source, mag, soft):
    n = lax.axis_size("row")
    edge = (2, Z, 8, N)
    up, down = pl.pallas_call(
        edge_kernel,
        in_specs=[pl.BlockSpec(memory_space=pltpu.HBM)] * 2,
        out_specs=(pl.BlockSpec(memory_space=VM),) * 2,
        out_shape=(vm((2, Z, N)),) * 2,
        scratch_shapes=[vm(edge), VM(edge, jnp.int32), pltpu.SemaphoreType.DMA((2, 2))],
    )(t, region)
    south = lax.ppermute(up, "row", [((i + 1) % n, i) for i in range(n)])
    north = lax.ppermute(down, "row", [(i, (i + 1) % n) for i in range(n)])
    par, ty, cy, r, pr, gr, rr, sep, net, face = call(
        first_kernel,
        [],
        (vm((6, Z, N)),) + (vm(FIELD),) * 6 + (vm(SEPS), vm(PART), vm((6, Z, N))),
        scratch=[
            vm(FIELD), vm(SPACED), VM(SPACED, jnp.int32), vm(SPACED),
            pltpu.SMEM((3,), F32), pltpu.SMEM((3,), F32),
            pltpu.SemaphoreType.DMA((2, 3)), pltpu.SemaphoreType.DMA((2,)),
        ],
        outside=[t, region, source, mag, soft],
        flops=20_000_000,
    )
    rd, srd, frd, own, beyond = call(
        side_kernel,
        [par, r, ty, cy, north, south, pr, gr, rr, sep, net, face],
        (vm(FIELD), vm(SEPD), vm((2, Z, N)), vm(NET), vm((Z, N))),
        scratch=[vm(FIELD), vm(FIELD)],
    )
    ypr, ygr, yrr, ysep, ynet = call(
        lines_kernel, [cy, beyond], (vm(FIELD),) * 3 + (vm(SEPS), vm(PART)), flops=5_000_000
    )
    others = spread_col(own, "col")
    yrd, ysrd, send = call(
        middle_kernel,
        [own] + others + [face, frd, pr, gr, rd, sep, srd, ty, ypr, ygr, yrr, ysep, ynet],
        (vm(FIELD), vm(SEPD), vm((n,) + NET)),
        scratch=[vm(FIELD), vm(FIELD)],
    )
    got = lax.all_to_all(send, "row", 0, 0, tiled=True)
    out = call(
        last_kernel,
        [got, ypr, ygr, yrd, ysep, ysrd, ty],
        jax.ShapeDtypeStruct((Z, N, N), F32),
        scratch=[vm(SPACED), pltpu.SemaphoreType.DMA((2,))],
        out_space=pl.ANY,
    )
    return out


def solution(mesh):
    specs = (P(None, "row", "col"),) * 3 + (P(), P())
    return jax.shard_map(
        local, mesh=mesh, in_specs=specs, out_specs=P(None, "row", "col"), check_vma=False
    )
```

```python
import jax
import jax.numpy as jnp
from jax import lax
from jax.experimental import pallas as pl
from jax.experimental.pallas import tpu as pltpu
from jax.sharding import PartitionSpec as P

Z, N = 8, 128
ROWS = Z * N
PITCH = N + 8
CHUNKS, STEP = 8, 16
F32 = jnp.float32
VM = pltpu.VMEM


def rcp(x):
    return pl.reciprocal(x, approx=True)


def link(a, b):
    return a * b * rcp(a + b)


def at(i):
    return pl.ds(pl.multiple_of(i * Z, Z), Z)


def strided(i):
    return pl.ds(i, Z, stride=PITCH)


def conductivity(t, reg, mag, soft):
    m = jnp.where(reg == 0, mag[0], jnp.where(reg == 1, mag[1], mag[2]))
    b = jnp.where(reg == 0, soft[0], jnp.where(reg == 1, soft[1], soft[2]))
    return m * jnp.exp(b * t)


def turn(src, dst):
    def body(z, _):
        lines = pl.ds(z, N, stride=Z)
        dst[lines, :] = src[lines, :].T
        return 0

    lax.fori_loop(0, Z, body, 0, unroll=True)


def factor(c_ref, pr_ref, gr_ref, rr_ref, sep_ref, net_ref, south=None, there=None):
    one = jnp.ones((Z, N), F32)
    zero = jnp.zeros((Z, N), F32)

    def cell(c, j, p, t, s, here, beyond=None):
        i = c * STEP + j
        edge = beyond is not None
        if not edge:
            beyond = c_ref[at(i + 1), :]
        g = link(here, beyond)
        if edge:
            g = jnp.where(there, g, 0.0)
        r = rcp(p + g + t)
        pr, gr = p * r, g * r
        pr_ref[at(i), :] = pr
        gr_ref[at(i), :] = gr
        rr_ref[at(i), :] = r
        return pr * g, gr * t if edge else 1.0 + gr * t, s + pr * t, beyond

    start = []
    for c in range(CHUNKS):
        here = c_ref[at(c * STEP + 1), :]
        start.append((link(c_ref[at(c * STEP), :], here), one, zero, here))

    def body(j, state):
        return [cell(c, j, *state[c]) for c in range(CHUNKS)]

    state = lax.fori_loop(1, STEP - 1, body, start, unroll=2)
    last = state[-1] if south is None else cell(CHUNKS - 1, STEP - 1, *state[-1], south)
    state = [cell(c, STEP - 1, *state[c]) for c in range(CHUNKS - 1)] + [last]
    q = state[0][0]
    left = 1.0 + state[0][2]
    t = state[0][1] + state[1][2]
    for c in range(1, CHUNKS):
        g = state[c][0]
        r = rcp(q + g + t)
        qr, gr = q * r, g * r
        sep_ref[0, c] = qr
        sep_ref[1, c] = gr
        sep_ref[2, c] = r
        left = left + qr * t
        t = state[c][1] + gr * t
        if c + 1 < CHUNKS:
            t = t + state[c + 1][2]
        q = qr * g
    net_ref[0] = q
    net_ref[1] = left
    net_ref[2] = t if south is None else jnp.where(there, t, 1.0)


def sweep(rhs, pr_ref, gr_ref, rr_ref, sep_ref, rd_ref, srd_ref, shared):
    def cell(c, j, d, s):
        i = c * STEP + j
        rd_ref[at(i), :] = rr_ref[at(i), :] * d
        beyond = gr_ref[at(i), :] * d
        if not (c == CHUNKS - 1 and isinstance(j, int)):
            beyond = rhs(i + 1) + beyond
        return beyond, s + pr_ref[at(i), :] * d

    def body(j, state):
        return [cell(c, j, *state[c]) for c in range(CHUNKS)]

    start = [(rhs(c * STEP + 1), jnp.zeros((Z, N), F32)) for c in range(CHUNKS)]
    state = lax.fori_loop(1, STEP - 1, body, start, unroll=True)
    last = cell(CHUNKS - 1, STEP - 1, *state[-1]) if shared else state[-1]
    state = [cell(c, STEP - 1, *state[c]) for c in range(CHUNKS - 1)] + [last]
    left = rhs(0) + state[0][1]
    d = state[0][0] + state[1][1]
    for c in range(1, CHUNKS):
        left = left + sep_ref[0, c] * d
        srd_ref[c] = sep_ref[2, c] * d
        d = state[c][0] + sep_ref[1, c] * d
        if c + 1 < CHUNKS:
            d = d + state[c + 1][1]
    return left, d


def back(ul, ur, pr_ref, gr_ref, rd_ref, sep_ref, srd_ref, put, shared, groups=1, done=None):
    seps = [None] * CHUNKS + [ur]
    for c in range(CHUNKS - 1, 0, -1):
        seps[c] = srd_ref[c] + sep_ref[0, c] * ul + sep_ref[1, c] * seps[c + 1]
    seps[0] = ul

    def cell(c, j, u):
        i = c * STEP + j
        v = rd_ref[at(i), :] + pr_ref[at(i), :] * seps[c] + gr_ref[at(i), :] * u
        put(i, v)
        return v

    if not shared:
        put(N - 1, ur)
    size = CHUNKS // groups
    for group in reversed(range(groups)):
        chunks = range(group * size, group * size + size)
        state = []
        for c in chunks:
            put(c * STEP, seps[c])
            whole = shared or c < CHUNKS - 1
            state.append(cell(c, STEP - 1, seps[c + 1]) if whole else ur)

        def body(k, state):
            return [cell(c, STEP - 2 - k, u) for c, u in zip(chunks, state)]

        lax.fori_loop(0, STEP - 2, body, state, unroll=True)
        if done is not None:
            done(group)


def joined(own, other, left):
    a = [jnp.where(left, x, y) for x, y in zip(own, other)]
    b = [jnp.where(left, y, x) for x, y in zip(own, other)]
    s, d = a[2] + b[1], a[4] + b[3]
    r = rcp(a[0] + b[0] + s)
    f, h = a[0] * r, b[0] * r
    return [f * b[0], a[1] + f * s, b[2] + h * s, a[3] + f * d, b[4] + h * d]


def ends(me, own, others):
    zero = jnp.zeros((Z, N), F32)
    yl = il = yr = ir = zero
    for k in reversed(range(len(others))):
        p = others[k]
        left = (me >> k) % 2 == 1
        far_s = jnp.where(left, p[1] + yl, p[2] + yr)
        far_d = jnp.where(left, p[3] + il, p[4] + ir)
        near_s = jnp.where(left, p[2], p[1])
        near_d = jnp.where(left, p[4], p[3])
        f = p[0] * rcp(p[0] + far_s)
        y, i = near_s + f * far_s, near_d + f * far_d
        yl, il = jnp.where(left, y, yl), jnp.where(left, i, il)
        yr, ir = jnp.where(left, yr, y), jnp.where(left, ir, i)
    sl, dl, sr, dr = own[1] + yl, own[3] + il, own[2] + yr, own[4] + ir
    r = rcp(own[0] + sl)
    f = own[0] * r
    ur = (dr + f * dl) * rcp(sr + f * sl)
    ul = (dl + own[0] * ur) * r
    return ul, ur


def edge_kernel(t_hbm, reg_hbm, up_ref, down_ref, t_ref, reg_ref, sem):
    copies = []
    for k, first in enumerate((0, N - 8)):
        rows = pl.ds(first, 8)
        copies.append(pltpu.make_async_copy(t_hbm.at[:, rows, :], t_ref.at[k], sem.at[0, k]))
        copies.append(pltpu.make_async_copy(reg_hbm.at[:, rows, :], reg_ref.at[k], sem.at[1, k]))
    for copy in copies:
        copy.start()
    for copy in copies:
        copy.wait()
    for k, row, out in ((0, 0, up_ref), (1, 7, down_ref)):
        out[0] = t_ref[k, :, row, :]
        out[1] = reg_ref[k, :, row, :].astype(F32)


def first_kernel(
    t_hbm, reg_hbm, s_hbm, mag_hbm, soft_hbm,
    par_ref, ty_ref, cy_ref, r_ref, pr_ref, gr_ref, rr_ref, sep_ref, net_ref, face_ref,
    cx_ref, t_box, reg_box, s_box, mag_ref, soft_ref, sem, small_sem,
):
    small = [
        pltpu.make_async_copy(mag_hbm, mag_ref, small_sem.at[0]),
        pltpu.make_async_copy(soft_hbm, soft_ref, small_sem.at[1]),
    ]
    for copy in small:
        copy.start()
    cuts = (0, N // 2 + 8, N)
    copies = [[], []]
    for k in range(2):
        rows = pl.ds(cuts[k], cuts[k + 1] - cuts[k])
        for j, (a, b) in enumerate(((t_hbm, t_box), (reg_hbm, reg_box), (s_hbm, s_box))):
            copies[k].append(pltpu.make_async_copy(a.at[:, rows, :], b.at[:, rows, :], sem.at[k, j]))
            copies[k][-1].start()
    t_ref, reg_ref, s_ref = (box.reshape(Z * PITCH, N) for box in (t_box, reg_box, s_box))
    for copy in small:
        copy.wait()
    mag = [jnp.full((Z, N), mag_ref[k] * 1000.0) for k in range(3)]
    soft = [jnp.full((Z, N), -soft_ref[k]) for k in range(3)]
    for k in range(3):
        par_ref[k] = mag[k]
        par_ref[3 + k] = soft[k]
    z = lax.broadcasted_iota(jnp.int32, (Z, N), 0)
    inner = jnp.where(z < Z - 1, 1.6e-4, 0.0)
    ground = jnp.where(z == 0, 8e-5, 0.0)

    def load(y):
        t = t_ref[strided(y), :]
        c = conductivity(t, reg_ref[strided(y), :], mag, soft)
        ty_ref[at(y), :] = t
        cy_ref[at(y), :] = c
        return t, c

    def row(y, t, c, before, after):
        flux = link(c, pltpu.roll(c, Z - 1, 0)) * (pltpu.roll(t, Z - 1, 0) - t) * inner
        up = flux - pltpu.roll(flux, 1, 0) - ground * (c * t)
        r_ref[at(y), :] = 2.0 * t + s_ref[strided(y), :] + 2.0 * (after - before) + up

    def step(y, t, c, before):
        tn, cn = load(y + 1)
        after = link(c, cn) * (tn - t)
        row(y, t, c, before, after)
        return tn, cn, after

    def body(k, state):
        for j in range(8):
            state = step(k * 8 + j, *state)
        return state

    for copy in copies[0]:
        copy.wait()
    state = *load(0), jnp.zeros((Z, N), F32)
    state = lax.fori_loop(0, N // 16, body, state)
    for copy in copies[1]:
        copy.wait()
    state = lax.fori_loop(N // 16, N // 8 - 1, body, state)
    for y in range(N - 8, N - 1):
        state = step(y, *state)
    row(N - 1, *state, jnp.zeros((Z, N), F32))
    turn(cy_ref, cx_ref)
    factor(cx_ref, pr_ref, gr_ref, rr_ref, sep_ref, net_ref)
    g, sl, sr = (net_ref[k] for k in range(3))
    cl, cr = cx_ref[at(0), :], cx_ref[at(N - 1), :]
    r = rcp(cl + g + sl)
    a, b = cl * r, g * r
    for k, v in enumerate((r, a, b)):
        face_ref[k] = v
    g, sr = a * g, sr + b * sl
    sl = a * sl
    r = rcp(g + cr + sr)
    a, b = g * r, cr * r
    for k, v in enumerate((r, a, b)):
        face_ref[3 + k] = v
    net_ref[0] = a * cr
    net_ref[1] = sl + a * sr
    net_ref[2] = b * sr


def side_kernel(
    par_ref, r_ref, ty_ref, cy_ref, north_ref, south_ref, pr_ref, gr_ref, rr_ref, sep_ref, net_ref,
    face_ref, rd_ref, srd_ref, frd_ref, out_ref, beyond_ref, rx_ref, ry_ref,
):
    me = lax.axis_index("row")
    mag = [par_ref[k] for k in range(3)]
    soft = [par_ref[3 + k] for k in range(3)]
    ry_ref[...] = r_ref[...]
    for row, halo, there in ((0, north_ref, me > 0), (N - 1, south_ref, me < lax.axis_size("row") - 1)):
        i = slice(row * Z, row * Z + Z)
        beyond = conductivity(halo[0], halo[1], mag, soft)
        flux = link(cy_ref[i, :], beyond) * (halo[0] - ty_ref[i, :])
        ry_ref[i, :] = r_ref[i, :] + jnp.where(there, 2.0 * flux, 0.0)
    beyond_ref[...] = beyond
    turn(ry_ref, rx_ref)
    left, right = sweep(
        lambda i: rx_ref[at(i), :], pr_ref, gr_ref, rr_ref, sep_ref, rd_ref, srd_ref, False
    )
    for k in range(3):
        out_ref[k] = net_ref[k]
    right = right + face_ref[2] * left
    frd_ref[0] = face_ref[0] * left
    frd_ref[1] = face_ref[3] * right
    out_ref[3] = face_ref[1] * left + face_ref[4] * right
    out_ref[4] = face_ref[5] * right


def lines_kernel(c_ref, south_ref, *outs):
    there = lax.axis_index("row") < lax.axis_size("row") - 1
    factor(c_ref, *outs, south=south_ref[...], there=there)


def level_kernel(axis, level, own_ref, other_ref, out_ref):
    left = (lax.axis_index(axis) >> level) % 2 == 0
    new = joined([own_ref[k] for k in range(5)], [other_ref[k] for k in range(5)], left)
    for k in range(5):
        out_ref[k] = new[k]


def middle_kernel(*refs):
    nets, refs = refs[:5], refs[5:]
    (
        face_ref, frd_ref, pr_ref, gr_ref, rd_ref, sep_ref, srd_ref, ty_ref,
        ypr_ref, ygr_ref, yrr_ref, ysep_ref, ynet_ref,
        yrd_ref, ysrd_ref, out_ref, wx_ref, wy_ref,
    ) = refs
    own, *others = ([r[k] for k in range(5)] for r in nets)
    ul, ur = ends(lax.axis_index("col"), own, others)
    ur = frd_ref[1] + face_ref[4] * ul + face_ref[5] * ur
    ul = frd_ref[0] + face_ref[1] * ul + face_ref[2] * ur

    def put(i, v):
        wx_ref[at(i), :] = v

    back(ul, ur, pr_ref, gr_ref, rd_ref, sep_ref, srd_ref, put, False)
    turn(wx_ref, wy_ref)
    left, right = sweep(
        lambda i: wy_ref[at(i), :] - 2.0 * ty_ref[at(i), :],
        ypr_ref, ygr_ref, yrr_ref, ysep_ref, yrd_ref, ysrd_ref, True,
    )
    for b in range(out_ref.shape[0]):
        for k in range(3):
            out_ref[b, k] = ynet_ref[k]
        out_ref[b, 3] = left
        out_ref[b, 4] = right


def last_kernel(
    all_ref, pr_ref, gr_ref, rd_ref, sep_ref, srd_ref, ty_ref, out_hbm, box, sem
):
    new_ref = box.reshape(Z * PITCH, N)
    me = lax.axis_index("row")
    place = lambda m: [all_ref[me ^ m, k] for k in range(5)]
    one, two = me % 2 == 0, me // 2 % 2 == 0
    own = place(0)
    far = joined(place(2), place(3), one)
    half = joined(joined(place(4), place(5), one), joined(place(6), place(7), one), two)
    ul, ur = ends(me, own, [place(1), far, half])

    def put(i, v):
        new_ref[strided(i), :] = v + ty_ref[at(i), :]

    copies = []

    def send(group):
        rows = pl.ds(group * (N // 2), N // 2)
        copies.append(
            pltpu.make_async_copy(box.at[:, rows, :], out_hbm.at[:, rows, :], sem.at[group])
        )
        copies[-1].start()

    back(ul, ur, pr_ref, gr_ref, rd_ref, sep_ref, srd_ref, put, True, 2, send)
    for copy in copies:
        copy.wait()


FIELD = (ROWS, N)
SPACED = (Z, PITCH, N)
NET = (5, Z, N)
PART = (3, Z, N)
SEPS = (3, CHUNKS, Z, N)
SEPD = (CHUNKS, Z, N)


def vm(shape):
    return VM(shape, F32)


def call(kernel, args, outs, scratch=(), flops=0, out_space=VM, outside=()):
    args = [pltpu.with_memory_space_constraint(a, VM) for a in args]
    whole = pl.BlockSpec(memory_space=VM)
    many = isinstance(outs, tuple)
    return pl.pallas_call(
        kernel,
        in_specs=[whole] * len(args) + [pl.BlockSpec(memory_space=pltpu.HBM)] * len(outside),
        out_specs=(whole,) * len(outs) if many else pl.BlockSpec(memory_space=out_space),
        out_shape=outs,
        scratch_shapes=list(scratch),
        cost_estimate=pl.CostEstimate(flops=flops, bytes_accessed=flops, transcendentals=0),
        compiler_params=pltpu.CompilerParams(vmem_limit_bytes=16 * 1024 * 1024),
    )(*args, *(pltpu.with_memory_space_constraint(a, pltpu.HBM) for a in outside))


def partner(x, axis, mask):
    return lax.ppermute(x, axis, [(i, i ^ mask) for i in range(lax.axis_size(axis))])


def spread_col(net, axis):
    others = []
    for level, mask in enumerate((1, 3, 7, 9)):
        others.append(partner(net, axis, mask))
        if level < 3:
            kernel = lambda *refs, level=level: level_kernel(axis, level, *refs)
            net = call(kernel, [net, others[-1]], vm(NET))
    return others


def local(t, region, source, mag, soft):
    n = lax.axis_size("row")
    edge = (2, Z, 8, N)
    up, down = pl.pallas_call(
        edge_kernel,
        in_specs=[pl.BlockSpec(memory_space=pltpu.HBM)] * 2,
        out_specs=(pl.BlockSpec(memory_space=VM),) * 2,
        out_shape=(vm((2, Z, N)),) * 2,
        scratch_shapes=[vm(edge), VM(edge, jnp.int32), pltpu.SemaphoreType.DMA((2, 2))],
    )(t, region)
    south = lax.ppermute(up, "row", [((i + 1) % n, i) for i in range(n)])
    north = lax.ppermute(down, "row", [(i, (i + 1) % n) for i in range(n)])
    par, ty, cy, r, pr, gr, rr, sep, net, face = call(
        first_kernel,
        [],
        (vm((6, Z, N)),) + (vm(FIELD),) * 6 + (vm(SEPS), vm(PART), vm((6, Z, N))),
        scratch=[
            vm(FIELD), vm(SPACED), VM(SPACED, jnp.int32), vm(SPACED),
            pltpu.SMEM((3,), F32), pltpu.SMEM((3,), F32),
            pltpu.SemaphoreType.DMA((2, 3)), pltpu.SemaphoreType.DMA((2,)),
        ],
        outside=[t, region, source, mag, soft],
        flops=20_000_000,
    )
    rd, srd, frd, own, beyond = call(
        side_kernel,
        [par, r, ty, cy, north, south, pr, gr, rr, sep, net, face],
        (vm(FIELD), vm(SEPD), vm((2, Z, N)), vm(NET), vm((Z, N))),
        scratch=[vm(FIELD), vm(FIELD)],
    )
    ypr, ygr, yrr, ysep, ynet = call(
        lines_kernel, [cy, beyond], (vm(FIELD),) * 3 + (vm(SEPS), vm(PART)), flops=5_000_000
    )
    others = spread_col(own, "col")
    yrd, ysrd, send = call(
        middle_kernel,
        [own] + others + [face, frd, pr, gr, rd, sep, srd, ty, ypr, ygr, yrr, ysep, ynet],
        (vm(FIELD), vm(SEPD), vm((n,) + NET)),
        scratch=[vm(FIELD), vm(FIELD)],
    )
    got = lax.all_to_all(send, "row", 0, 0, tiled=True)
    out = call(
        last_kernel,
        [got, ypr, ygr, yrd, ysep, ysrd, ty],
        jax.ShapeDtypeStruct((Z, N, N), F32),
        scratch=[vm(SPACED), pltpu.SemaphoreType.DMA((2,))],
        out_space=pl.ANY,
    )
    return out


def solution(mesh):
    specs = (P(None, "row", "col"),) * 3 + (P(), P())
    return jax.shard_map(
        local, mesh=mesh, in_specs=specs, out_specs=P(None, "row", "col"), check_vma=False
    )
```

```python
import jax
import jax.numpy as jnp
from jax import lax
from jax.experimental import pallas as pl
from jax.experimental.pallas import tpu as pltpu
from jax.sharding import PartitionSpec as P

Z, N = 8, 128
ROWS = Z * N
PITCH = N + 8
CHUNKS, STEP = 8, 16
F32 = jnp.float32
VM = pltpu.VMEM


def rcp(x):
    return pl.reciprocal(x, approx=True)


def link(a, b):
    return a * b * rcp(a + b)


def at(i):
    return pl.ds(pl.multiple_of(i * Z, Z), Z)


def strided(i):
    return pl.ds(i, Z, stride=PITCH)


def conductivity(t, reg, mag, soft):
    m = jnp.where(reg == 0, mag[0], jnp.where(reg == 1, mag[1], mag[2]))
    b = jnp.where(reg == 0, soft[0], jnp.where(reg == 1, soft[1], soft[2]))
    return m * jnp.exp(b * t)


def turn(src, dst):
    def body(z, _):
        lines = pl.ds(z, N, stride=Z)
        dst[lines, :] = src[lines, :].T
        return 0

    lax.fori_loop(0, Z, body, 0, unroll=True)


def factor(c_ref, pr_ref, gr_ref, rr_ref, sep_ref, net_ref, south=None, there=None):
    one = jnp.ones((Z, N), F32)
    zero = jnp.zeros((Z, N), F32)

    def cell(c, j, p, t, s, here, beyond=None):
        i = c * STEP + j
        edge = beyond is not None
        if not edge:
            beyond = c_ref[at(i + 1), :]
        g = link(here, beyond)
        if edge:
            g = jnp.where(there, g, 0.0)
        r = rcp(p + g + t)
        pr, gr = p * r, g * r
        pr_ref[at(i), :] = pr
        gr_ref[at(i), :] = gr
        rr_ref[at(i), :] = r
        return pr * g, gr * t if edge else 1.0 + gr * t, s + pr * t, beyond

    start = []
    for c in range(CHUNKS):
        here = c_ref[at(c * STEP + 1), :]
        start.append((link(c_ref[at(c * STEP), :], here), one, zero, here))

    def body(j, state):
        return [cell(c, j, *state[c]) for c in range(CHUNKS)]

    state = lax.fori_loop(1, STEP - 1, body, start, unroll=2)
    last = state[-1] if south is None else cell(CHUNKS - 1, STEP - 1, *state[-1], south)
    state = [cell(c, STEP - 1, *state[c]) for c in range(CHUNKS - 1)] + [last]
    q = state[0][0]
    left = 1.0 + state[0][2]
    t = state[0][1] + state[1][2]
    for c in range(1, CHUNKS):
        g = state[c][0]
        r = rcp(q + g + t)
        qr, gr = q * r, g * r
        sep_ref[0, c] = qr
        sep_ref[1, c] = gr
        sep_ref[2, c] = r
        left = left + qr * t
        t = state[c][1] + gr * t
        if c + 1 < CHUNKS:
            t = t + state[c + 1][2]
        q = qr * g
    net_ref[0] = q
    net_ref[1] = left
    net_ref[2] = t if south is None else jnp.where(there, t, 1.0)


def sweep(rhs, pr_ref, gr_ref, rr_ref, sep_ref, rd_ref, srd_ref, shared):
    def cell(c, j, d, s):
        i = c * STEP + j
        rd_ref[at(i), :] = rr_ref[at(i), :] * d
        beyond = gr_ref[at(i), :] * d
        if not (c == CHUNKS - 1 and isinstance(j, int)):
            beyond = rhs(i + 1) + beyond
        return beyond, s + pr_ref[at(i), :] * d

    def body(j, state):
        return [cell(c, j, *state[c]) for c in range(CHUNKS)]

    start = [(rhs(c * STEP + 1), jnp.zeros((Z, N), F32)) for c in range(CHUNKS)]
    state = lax.fori_loop(1, STEP - 1, body, start, unroll=True)
    last = cell(CHUNKS - 1, STEP - 1, *state[-1]) if shared else state[-1]
    state = [cell(c, STEP - 1, *state[c]) for c in range(CHUNKS - 1)] + [last]
    left = rhs(0) + state[0][1]
    d = state[0][0] + state[1][1]
    for c in range(1, CHUNKS):
        left = left + sep_ref[0, c] * d
        srd_ref[c] = sep_ref[2, c] * d
        d = state[c][0] + sep_ref[1, c] * d
        if c + 1 < CHUNKS:
            d = d + state[c + 1][1]
    return left, d


def back(ul, ur, pr_ref, gr_ref, rd_ref, sep_ref, srd_ref, put, shared, groups=1, done=None):
    seps = [None] * CHUNKS + [ur]
    for c in range(CHUNKS - 1, 0, -1):
        seps[c] = srd_ref[c] + sep_ref[0, c] * ul + sep_ref[1, c] * seps[c + 1]
    seps[0] = ul

    def cell(c, j, u):
        i = c * STEP + j
        v = rd_ref[at(i), :] + pr_ref[at(i), :] * seps[c] + gr_ref[at(i), :] * u
        put(i, v)
        return v

    if not shared:
        put(N - 1, ur)
    size = CHUNKS // groups
    for group in reversed(range(groups)):
        chunks = range(group * size, group * size + size)
        state = []
        for c in chunks:
            put(c * STEP, seps[c])
            whole = shared or c < CHUNKS - 1
            state.append(cell(c, STEP - 1, seps[c + 1]) if whole else ur)

        def body(k, state):
            return [cell(c, STEP - 2 - k, u) for c, u in zip(chunks, state)]

        lax.fori_loop(0, STEP - 2, body, state, unroll=True)
        if done is not None:
            done(group)


def joined(own, other, left):
    a = [jnp.where(left, x, y) for x, y in zip(own, other)]
    b = [jnp.where(left, y, x) for x, y in zip(own, other)]
    s, d = a[2] + b[1], a[4] + b[3]
    r = rcp(a[0] + b[0] + s)
    f, h = a[0] * r, b[0] * r
    return [f * b[0], a[1] + f * s, b[2] + h * s, a[3] + f * d, b[4] + h * d]


def ends(me, own, others):
    zero = jnp.zeros((Z, N), F32)
    yl = il = yr = ir = zero
    for k in reversed(range(len(others))):
        p = others[k]
        left = (me >> k) % 2 == 1
        far_s = jnp.where(left, p[1] + yl, p[2] + yr)
        far_d = jnp.where(left, p[3] + il, p[4] + ir)
        near_s = jnp.where(left, p[2], p[1])
        near_d = jnp.where(left, p[4], p[3])
        f = p[0] * rcp(p[0] + far_s)
        y, i = near_s + f * far_s, near_d + f * far_d
        yl, il = jnp.where(left, y, yl), jnp.where(left, i, il)
        yr, ir = jnp.where(left, yr, y), jnp.where(left, ir, i)
    sl, dl, sr, dr = own[1] + yl, own[3] + il, own[2] + yr, own[4] + ir
    r = rcp(own[0] + sl)
    f = own[0] * r
    ur = (dr + f * dl) * rcp(sr + f * sl)
    ul = (dl + own[0] * ur) * r
    return ul, ur


def edge_kernel(t_hbm, reg_hbm, up_ref, down_ref, t_ref, reg_ref, sem):
    copies = []
    for k, first in enumerate((0, N - 8)):
        rows = pl.ds(first, 8)
        copies.append(pltpu.make_async_copy(t_hbm.at[:, rows, :], t_ref.at[k], sem.at[0, k]))
        copies.append(pltpu.make_async_copy(reg_hbm.at[:, rows, :], reg_ref.at[k], sem.at[1, k]))
    for copy in copies:
        copy.start()
    for copy in copies:
        copy.wait()
    even = lax.axis_index("row") % 2 == 0
    up = t_ref[0, :, 0, :], reg_ref[0, :, 0, :].astype(F32)
    down = t_ref[1, :, 7, :], reg_ref[1, :, 7, :].astype(F32)
    for k in range(2):
        up_ref[k] = jnp.where(even, up[k], down[k])
        down_ref[k] = jnp.where(even, down[k], up[k])


def first_kernel(
    t_hbm, reg_hbm, s_hbm, mag_hbm, soft_hbm,
    par_ref, ty_ref, cy_ref, r_ref, pr_ref, gr_ref, rr_ref, sep_ref, net_ref, face_ref,
    cx_ref, t_box, reg_box, s_box, mag_ref, soft_ref, sem, small_sem,
):
    small = [
        pltpu.make_async_copy(mag_hbm, mag_ref, small_sem.at[0]),
        pltpu.make_async_copy(soft_hbm, soft_ref, small_sem.at[1]),
    ]
    for copy in small:
        copy.start()
    cuts = (0, N // 2 + 8, N)
    copies = [[], []]
    for k in range(2):
        rows = pl.ds(cuts[k], cuts[k + 1] - cuts[k])
        for j, (a, b) in enumerate(((t_hbm, t_box), (reg_hbm, reg_box), (s_hbm, s_box))):
            copies[k].append(pltpu.make_async_copy(a.at[:, rows, :], b.at[:, rows, :], sem.at[k, j]))
            copies[k][-1].start()
    t_ref, reg_ref, s_ref = (box.reshape(Z * PITCH, N) for box in (t_box, reg_box, s_box))
    for copy in small:
        copy.wait()
    mag = [jnp.full((Z, N), mag_ref[k] * 1000.0) for k in range(3)]
    soft = [jnp.full((Z, N), -soft_ref[k]) for k in range(3)]
    for k in range(3):
        par_ref[k] = mag[k]
        par_ref[3 + k] = soft[k]
    z = lax.broadcasted_iota(jnp.int32, (Z, N), 0)
    inner = jnp.where(z < Z - 1, 1.6e-4, 0.0)
    ground = jnp.where(z == 0, 8e-5, 0.0)

    def load(y):
        t = t_ref[strided(y), :]
        c = conductivity(t, reg_ref[strided(y), :], mag, soft)
        ty_ref[at(y), :] = t
        cy_ref[at(y), :] = c
        return t, c

    def row(y, t, c, before, after):
        flux = link(c, pltpu.roll(c, Z - 1, 0)) * (pltpu.roll(t, Z - 1, 0) - t) * inner
        up = flux - pltpu.roll(flux, 1, 0) - ground * (c * t)
        r_ref[at(y), :] = 2.0 * t + s_ref[strided(y), :] + 2.0 * (after - before) + up

    def step(y, t, c, before):
        tn, cn = load(y + 1)
        after = link(c, cn) * (tn - t)
        row(y, t, c, before, after)
        return tn, cn, after

    def body(k, state):
        for j in range(8):
            state = step(k * 8 + j, *state)
        return state

    for copy in copies[0]:
        copy.wait()
    state = *load(0), jnp.zeros((Z, N), F32)
    state = lax.fori_loop(0, N // 16, body, state)
    for copy in copies[1]:
        copy.wait()
    state = lax.fori_loop(N // 16, N // 8 - 1, body, state)
    for y in range(N - 8, N - 1):
        state = step(y, *state)
    row(N - 1, *state, jnp.zeros((Z, N), F32))
    turn(cy_ref, cx_ref)
    factor(cx_ref, pr_ref, gr_ref, rr_ref, sep_ref, net_ref)
    g, sl, sr = (net_ref[k] for k in range(3))
    cl, cr = cx_ref[at(0), :], cx_ref[at(N - 1), :]
    r = rcp(cl + g + sl)
    a, b = cl * r, g * r
    for k, v in enumerate((r, a, b)):
        face_ref[k] = v
    g, sr = a * g, sr + b * sl
    sl = a * sl
    r = rcp(g + cr + sr)
    a, b = g * r, cr * r
    for k, v in enumerate((r, a, b)):
        face_ref[3 + k] = v
    net_ref[0] = a * cr
    net_ref[1] = sl + a * sr
    net_ref[2] = b * sr


def side_kernel(
    par_ref, r_ref, ty_ref, cy_ref, north_ref, south_ref, pr_ref, gr_ref, rr_ref, sep_ref, net_ref,
    face_ref, rd_ref, srd_ref, frd_ref, out_ref, beyond_ref, rx_ref, ry_ref,
):
    me = lax.axis_index("row")
    mag = [par_ref[k] for k in range(3)]
    soft = [par_ref[3 + k] for k in range(3)]
    ry_ref[...] = r_ref[...]
    even = me % 2 == 0
    first = [jnp.where(even, north_ref[k], south_ref[k]) for k in range(2)]
    last = [jnp.where(even, south_ref[k], north_ref[k]) for k in range(2)]
    for row, halo, there in ((0, first, me > 0), (N - 1, last, me < lax.axis_size("row") - 1)):
        i = slice(row * Z, row * Z + Z)
        beyond = conductivity(halo[0], halo[1], mag, soft)
        flux = link(cy_ref[i, :], beyond) * (halo[0] - ty_ref[i, :])
        ry_ref[i, :] = r_ref[i, :] + jnp.where(there, 2.0 * flux, 0.0)
    beyond_ref[...] = beyond
    turn(ry_ref, rx_ref)
    left, right = sweep(
        lambda i: rx_ref[at(i), :], pr_ref, gr_ref, rr_ref, sep_ref, rd_ref, srd_ref, False
    )
    for k in range(3):
        out_ref[k] = net_ref[k]
    right = right + face_ref[2] * left
    frd_ref[0] = face_ref[0] * left
    frd_ref[1] = face_ref[3] * right
    out_ref[3] = face_ref[1] * left + face_ref[4] * right
    out_ref[4] = face_ref[5] * right


def lines_kernel(c_ref, south_ref, *outs):
    there = lax.axis_index("row") < lax.axis_size("row") - 1
    factor(c_ref, *outs, south=south_ref[...], there=there)


def level_kernel(axis, level, own_ref, other_ref, out_ref):
    left = (lax.axis_index(axis) >> level) % 2 == 0
    new = joined([own_ref[k] for k in range(5)], [other_ref[k] for k in range(5)], left)
    for k in range(5):
        out_ref[k] = new[k]


def middle_kernel(*refs):
    nets, refs = refs[:5], refs[5:]
    (
        face_ref, frd_ref, pr_ref, gr_ref, rd_ref, sep_ref, srd_ref, ty_ref,
        ypr_ref, ygr_ref, yrr_ref, ysep_ref, ynet_ref,
        yrd_ref, ysrd_ref, out_ref, wx_ref, wy_ref,
    ) = refs
    own, *others = ([r[k] for k in range(5)] for r in nets)
    ul, ur = ends(lax.axis_index("col"), own, others)
    ur = frd_ref[1] + face_ref[4] * ul + face_ref[5] * ur
    ul = frd_ref[0] + face_ref[1] * ul + face_ref[2] * ur

    def put(i, v):
        wx_ref[at(i), :] = v

    back(ul, ur, pr_ref, gr_ref, rd_ref, sep_ref, srd_ref, put, False)
    turn(wx_ref, wy_ref)
    left, right = sweep(
        lambda i: wy_ref[at(i), :] - 2.0 * ty_ref[at(i), :],
        ypr_ref, ygr_ref, yrr_ref, ysep_ref, yrd_ref, ysrd_ref, True,
    )
    for b in range(out_ref.shape[0]):
        for k in range(3):
            out_ref[b, k] = ynet_ref[k]
        out_ref[b, 3] = left
        out_ref[b, 4] = right


def last_kernel(
    all_ref, pr_ref, gr_ref, rd_ref, sep_ref, srd_ref, ty_ref, out_hbm, box, sem
):
    new_ref = box.reshape(Z * PITCH, N)
    me = lax.axis_index("row")
    place = lambda m: [all_ref[me ^ m, k] for k in range(5)]
    one, two = me % 2 == 0, me // 2 % 2 == 0
    own = place(0)
    far = joined(place(2), place(3), one)
    half = joined(joined(place(4), place(5), one), joined(place(6), place(7), one), two)
    ul, ur = ends(me, own, [place(1), far, half])

    def put(i, v):
        new_ref[strided(i), :] = v + ty_ref[at(i), :]

    copies = []

    def send(group):
        rows = pl.ds(group * (N // 2), N // 2)
        copies.append(
            pltpu.make_async_copy(box.at[:, rows, :], out_hbm.at[:, rows, :], sem.at[group])
        )
        copies[-1].start()

    back(ul, ur, pr_ref, gr_ref, rd_ref, sep_ref, srd_ref, put, True, 2, send)
    for copy in copies:
        copy.wait()


FIELD = (ROWS, N)
SPACED = (Z, PITCH, N)
NET = (5, Z, N)
PART = (3, Z, N)
SEPS = (3, CHUNKS, Z, N)
SEPD = (CHUNKS, Z, N)


def vm(shape):
    return VM(shape, F32)


def call(kernel, args, outs, scratch=(), flops=0, out_space=VM, outside=()):
    args = [pltpu.with_memory_space_constraint(a, VM) for a in args]
    whole = pl.BlockSpec(memory_space=VM)
    many = isinstance(outs, tuple)
    return pl.pallas_call(
        kernel,
        in_specs=[whole] * len(args) + [pl.BlockSpec(memory_space=pltpu.HBM)] * len(outside),
        out_specs=(whole,) * len(outs) if many else pl.BlockSpec(memory_space=out_space),
        out_shape=outs,
        scratch_shapes=list(scratch),
        cost_estimate=pl.CostEstimate(flops=flops, bytes_accessed=flops, transcendentals=0),
        compiler_params=pltpu.CompilerParams(vmem_limit_bytes=16 * 1024 * 1024),
    )(*args, *(pltpu.with_memory_space_constraint(a, pltpu.HBM) for a in outside))


def partner(x, axis, mask):
    return lax.ppermute(x, axis, [(i, i ^ mask) for i in range(lax.axis_size(axis))])


def spread_col(net, axis):
    others = []
    for level, mask in enumerate((1, 3, 7, 9)):
        others.append(partner(net, axis, mask))
        if level < 3:
            kernel = lambda *refs, level=level: level_kernel(axis, level, *refs)
            net = call(kernel, [net, others[-1]], vm(NET))
    return others


def local(t, region, source, mag, soft):
    n = lax.axis_size("row")
    edge = (2, Z, 8, N)
    up, down = pl.pallas_call(
        edge_kernel,
        in_specs=[pl.BlockSpec(memory_space=pltpu.HBM)] * 2,
        out_specs=(pl.BlockSpec(memory_space=VM),) * 2,
        out_shape=(vm((2, Z, N)),) * 2,
        scratch_shapes=[vm(edge), VM(edge, jnp.int32), pltpu.SemaphoreType.DMA((2, 2))],
    )(t, region)
    south = partner(down, "row", 1)
    north = lax.ppermute(up, "row", [(i, (i + i % 2 * 2 - 1) % n) for i in range(n)])
    par, ty, cy, r, pr, gr, rr, sep, net, face = call(
        first_kernel,
        [],
        (vm((6, Z, N)),) + (vm(FIELD),) * 6 + (vm(SEPS), vm(PART), vm((6, Z, N))),
        scratch=[
            vm(FIELD), vm(SPACED), VM(SPACED, jnp.int32), vm(SPACED),
            pltpu.SMEM((3,), F32), pltpu.SMEM((3,), F32),
            pltpu.SemaphoreType.DMA((2, 3)), pltpu.SemaphoreType.DMA((2,)),
        ],
        outside=[t, region, source, mag, soft],
        flops=20_000_000,
    )
    rd, srd, frd, own, beyond = call(
        side_kernel,
        [par, r, ty, cy, north, south, pr, gr, rr, sep, net, face],
        (vm(FIELD), vm(SEPD), vm((2, Z, N)), vm(NET), vm((Z, N))),
        scratch=[vm(FIELD), vm(FIELD)],
    )
    ypr, ygr, yrr, ysep, ynet = call(
        lines_kernel, [cy, beyond], (vm(FIELD),) * 3 + (vm(SEPS), vm(PART)), flops=5_000_000
    )
    others = spread_col(own, "col")
    yrd, ysrd, send = call(
        middle_kernel,
        [own] + others + [face, frd, pr, gr, rd, sep, srd, ty, ypr, ygr, yrr, ysep, ynet],
        (vm(FIELD), vm(SEPD), vm((n,) + NET)),
        scratch=[vm(FIELD), vm(FIELD)],
    )
    got = lax.all_to_all(send, "row", 0, 0, tiled=True)
    out = call(
        last_kernel,
        [got, ypr, ygr, yrd, ysep, ysrd, ty],
        jax.ShapeDtypeStruct((Z, N, N), F32),
        scratch=[vm(SPACED), pltpu.SemaphoreType.DMA((2,))],
        out_space=pl.ANY,
    )
    return out


def solution(mesh):
    specs = (P(None, "row", "col"),) * 3 + (P(), P())
    return jax.shard_map(
        local, mesh=mesh, in_specs=specs, out_specs=P(None, "row", "col"), check_vma=False
    )
```

```python
import jax
import jax.numpy as jnp
from jax import lax
from jax.experimental import pallas as pl
from jax.experimental.pallas import tpu as pltpu
from jax.sharding import PartitionSpec as P

Z, N = 8, 128
ROWS = Z * N
PITCH = N + 8
CHUNKS, STEP = 8, 16
F32 = jnp.float32
VM = pltpu.VMEM


def rcp(x):
    return pl.reciprocal(x, approx=True)


def link(a, b):
    return a * b * rcp(a + b)


def at(i):
    return pl.ds(pl.multiple_of(i * Z, Z), Z)


def strided(i):
    return pl.ds(i, Z, stride=PITCH)


def conductivity(t, reg, mag, soft):
    m = jnp.where(reg == 0, mag[0], jnp.where(reg == 1, mag[1], mag[2]))
    b = jnp.where(reg == 0, soft[0], jnp.where(reg == 1, soft[1], soft[2]))
    return m * jnp.exp(b * t)


def turn(src, dst):
    def body(z, _):
        lines = pl.ds(z, N, stride=Z)
        dst[lines, :] = src[lines, :].T
        return 0

    lax.fori_loop(0, Z, body, 0, unroll=True)


def factor(c_ref, pr_ref, gr_ref, rr_ref, sep_ref, net_ref, south=None, there=None):
    one = jnp.ones((Z, N), F32)
    zero = jnp.zeros((Z, N), F32)

    def cell(c, j, p, t, s, here, beyond=None):
        i = c * STEP + j
        edge = beyond is not None
        if not edge:
            beyond = c_ref[at(i + 1), :]
        g = link(here, beyond)
        if edge:
            g = jnp.where(there, g, 0.0)
        r = rcp(p + g + t)
        pr, gr = p * r, g * r
        pr_ref[at(i), :] = pr
        gr_ref[at(i), :] = gr
        rr_ref[at(i), :] = r
        return pr * g, gr * t if edge else 1.0 + gr * t, s + pr * t, beyond

    start = []
    for c in range(CHUNKS):
        here = c_ref[at(c * STEP + 1), :]
        start.append((link(c_ref[at(c * STEP), :], here), one, zero, here))

    def body(j, state):
        return [cell(c, j, *state[c]) for c in range(CHUNKS)]

    state = lax.fori_loop(1, STEP - 1, body, start, unroll=2)
    last = state[-1] if south is None else cell(CHUNKS - 1, STEP - 1, *state[-1], south)
    state = [cell(c, STEP - 1, *state[c]) for c in range(CHUNKS - 1)] + [last]
    q = state[0][0]
    left = 1.0 + state[0][2]
    t = state[0][1] + state[1][2]
    for c in range(1, CHUNKS):
        g = state[c][0]
        r = rcp(q + g + t)
        qr, gr = q * r, g * r
        sep_ref[0, c] = qr
        sep_ref[1, c] = gr
        sep_ref[2, c] = r
        left = left + qr * t
        t = state[c][1] + gr * t
        if c + 1 < CHUNKS:
            t = t + state[c + 1][2]
        q = qr * g
    net_ref[0] = q
    net_ref[1] = left
    net_ref[2] = t if south is None else jnp.where(there, t, 1.0)


def sweep(rhs, pr_ref, gr_ref, rr_ref, sep_ref, rd_ref, srd_ref, shared):
    def cell(c, j, d, s):
        i = c * STEP + j
        rd_ref[at(i), :] = rr_ref[at(i), :] * d
        beyond = gr_ref[at(i), :] * d
        if not (c == CHUNKS - 1 and isinstance(j, int)):
            beyond = rhs(i + 1) + beyond
        return beyond, s + pr_ref[at(i), :] * d

    def body(j, state):
        return [cell(c, j, *state[c]) for c in range(CHUNKS)]

    start = [(rhs(c * STEP + 1), jnp.zeros((Z, N), F32)) for c in range(CHUNKS)]
    state = lax.fori_loop(1, STEP - 1, body, start, unroll=True)
    last = cell(CHUNKS - 1, STEP - 1, *state[-1]) if shared else state[-1]
    state = [cell(c, STEP - 1, *state[c]) for c in range(CHUNKS - 1)] + [last]
    left = rhs(0) + state[0][1]
    d = state[0][0] + state[1][1]
    for c in range(1, CHUNKS):
        left = left + sep_ref[0, c] * d
        srd_ref[c] = sep_ref[2, c] * d
        d = state[c][0] + sep_ref[1, c] * d
        if c + 1 < CHUNKS:
            d = d + state[c + 1][1]
    return left, d


def back(ul, ur, pr_ref, gr_ref, rd_ref, sep_ref, srd_ref, put, shared, groups=1, done=None):
    seps = [None] * CHUNKS + [ur]
    for c in range(CHUNKS - 1, 0, -1):
        seps[c] = srd_ref[c] + sep_ref[0, c] * ul + sep_ref[1, c] * seps[c + 1]
    seps[0] = ul

    def cell(c, j, u):
        i = c * STEP + j
        v = rd_ref[at(i), :] + pr_ref[at(i), :] * seps[c] + gr_ref[at(i), :] * u
        put(i, v)
        return v

    if not shared:
        put(N - 1, ur)
    size = CHUNKS // groups
    for group in reversed(range(groups)):
        chunks = range(group * size, group * size + size)
        state = []
        for c in chunks:
            put(c * STEP, seps[c])
            whole = shared or c < CHUNKS - 1
            state.append(cell(c, STEP - 1, seps[c + 1]) if whole else ur)

        def body(k, state):
            return [cell(c, STEP - 2 - k, u) for c, u in zip(chunks, state)]

        lax.fori_loop(0, STEP - 2, body, state, unroll=True)
        if done is not None:
            done(group)


def joined(own, other, left):
    a = [jnp.where(left, x, y) for x, y in zip(own, other)]
    b = [jnp.where(left, y, x) for x, y in zip(own, other)]
    s, d = a[2] + b[1], a[4] + b[3]
    r = rcp(a[0] + b[0] + s)
    f, h = a[0] * r, b[0] * r
    return [f * b[0], a[1] + f * s, b[2] + h * s, a[3] + f * d, b[4] + h * d]


def ends(me, own, others):
    zero = jnp.zeros((Z, N), F32)
    yl = il = yr = ir = zero
    for k in reversed(range(len(others))):
        p = others[k]
        left = (me >> k) % 2 == 1
        far_s = jnp.where(left, p[1] + yl, p[2] + yr)
        far_d = jnp.where(left, p[3] + il, p[4] + ir)
        near_s = jnp.where(left, p[2], p[1])
        near_d = jnp.where(left, p[4], p[3])
        f = p[0] * rcp(p[0] + far_s)
        y, i = near_s + f * far_s, near_d + f * far_d
        yl, il = jnp.where(left, y, yl), jnp.where(left, i, il)
        yr, ir = jnp.where(left, yr, y), jnp.where(left, ir, i)
    sl, dl, sr, dr = own[1] + yl, own[3] + il, own[2] + yr, own[4] + ir
    r = rcp(own[0] + sl)
    f = own[0] * r
    ur = (dr + f * dl) * rcp(sr + f * sl)
    ul = (dl + own[0] * ur) * r
    return ul, ur


def edge_kernel(t_hbm, reg_hbm, up_ref, down_ref, t_ref, reg_ref, sem):
    copies = []
    for k, first in enumerate((0, N - 8)):
        rows = pl.ds(first, 8)
        copies.append(pltpu.make_async_copy(t_hbm.at[:, rows, :], t_ref.at[k], sem.at[0, k]))
        copies.append(pltpu.make_async_copy(reg_hbm.at[:, rows, :], reg_ref.at[k], sem.at[1, k]))
    for copy in copies:
        copy.start()
    for copy in copies:
        copy.wait()
    even = lax.axis_index("row") % 2 == 0
    up = t_ref[0, :, 0, :], reg_ref[0, :, 0, :].astype(F32)
    down = t_ref[1, :, 7, :], reg_ref[1, :, 7, :].astype(F32)
    for k in range(2):
        up_ref[k] = jnp.where(even, up[k], down[k])
        down_ref[k] = jnp.where(even, down[k], up[k])


def first_kernel(
    t_hbm, reg_hbm, s_hbm, mag_hbm, soft_hbm,
    par_ref, ty_ref, cy_ref, r_ref, pr_ref, gr_ref, rr_ref, sep_ref, net_ref, face_ref,
    cx_ref, t_box, reg_box, s_box, mag_ref, soft_ref, sem, small_sem,
):
    small = [
        pltpu.make_async_copy(mag_hbm, mag_ref, small_sem.at[0]),
        pltpu.make_async_copy(soft_hbm, soft_ref, small_sem.at[1]),
    ]
    for copy in small:
        copy.start()
    cuts = (0, N // 2 + 8, N)
    copies = [[], []]
    for k in range(2):
        rows = pl.ds(cuts[k], cuts[k + 1] - cuts[k])
        for j, (a, b) in enumerate(((t_hbm, t_box), (reg_hbm, reg_box), (s_hbm, s_box))):
            copies[k].append(pltpu.make_async_copy(a.at[:, rows, :], b.at[:, rows, :], sem.at[k, j]))
            copies[k][-1].start()
    t_ref, reg_ref, s_ref = (box.reshape(Z * PITCH, N) for box in (t_box, reg_box, s_box))
    for copy in small:
        copy.wait()
    mag = [jnp.full((Z, N), mag_ref[k] * 1000.0) for k in range(3)]
    soft = [jnp.full((Z, N), -soft_ref[k]) for k in range(3)]
    for k in range(3):
        par_ref[k] = mag[k]
        par_ref[3 + k] = soft[k]
    z = lax.broadcasted_iota(jnp.int32, (Z, N), 0)
    inner = jnp.where(z < Z - 1, 1.6e-4, 0.0)
    ground = jnp.where(z == 0, 8e-5, 0.0)

    def load(y):
        t = t_ref[strided(y), :]
        c = conductivity(t, reg_ref[strided(y), :], mag, soft)
        ty_ref[at(y), :] = t
        cy_ref[at(y), :] = c
        return t, c

    def row(y, t, c, before, after):
        flux = link(c, pltpu.roll(c, Z - 1, 0)) * (pltpu.roll(t, Z - 1, 0) - t) * inner
        up = flux - pltpu.roll(flux, 1, 0) - ground * (c * t)
        r_ref[at(y), :] = 2.0 * t + s_ref[strided(y), :] + 2.0 * (after - before) + up

    def step(y, t, c, before):
        tn, cn = load(y + 1)
        after = link(c, cn) * (tn - t)
        row(y, t, c, before, after)
        return tn, cn, after

    def body(k, state):
        for j in range(8):
            state = step(k * 8 + j, *state)
        return state

    for copy in copies[0]:
        copy.wait()
    state = *load(0), jnp.zeros((Z, N), F32)
    state = lax.fori_loop(0, N // 16, body, state)
    for copy in copies[1]:
        copy.wait()
    state = lax.fori_loop(N // 16, N // 8 - 1, body, state)
    for y in range(N - 8, N - 1):
        state = step(y, *state)
    row(N - 1, *state, jnp.zeros((Z, N), F32))
    turn(cy_ref, cx_ref)
    factor(cx_ref, pr_ref, gr_ref, rr_ref, sep_ref, net_ref)
    g, sl, sr = (net_ref[k] for k in range(3))
    cl, cr = cx_ref[at(0), :], cx_ref[at(N - 1), :]
    r = rcp(cl + g + sl)
    a, b = cl * r, g * r
    for k, v in enumerate((r, a, b)):
        face_ref[k] = v
    g, sr = a * g, sr + b * sl
    sl = a * sl
    r = rcp(g + cr + sr)
    a, b = g * r, cr * r
    for k, v in enumerate((r, a, b)):
        face_ref[3 + k] = v
    net_ref[0] = a * cr
    net_ref[1] = sl + a * sr
    net_ref[2] = b * sr


def side_kernel(
    par_ref, r_ref, ty_ref, cy_ref, north_ref, south_ref, pr_ref, gr_ref, rr_ref, sep_ref, net_ref,
    face_ref, rd_ref, srd_ref, frd_ref, out_ref, beyond_ref, rx_ref, ry_ref,
):
    me = lax.axis_index("row")
    mag = [par_ref[k] for k in range(3)]
    soft = [par_ref[3 + k] for k in range(3)]
    ry_ref[...] = r_ref[...]
    even = me % 2 == 0
    first = [jnp.where(even, north_ref[k], south_ref[k]) for k in range(2)]
    last = [jnp.where(even, south_ref[k], north_ref[k]) for k in range(2)]
    for row, halo, there in ((0, first, me > 0), (N - 1, last, me < lax.axis_size("row") - 1)):
        i = slice(row * Z, row * Z + Z)
        beyond = conductivity(halo[0], halo[1], mag, soft)
        flux = link(cy_ref[i, :], beyond) * (halo[0] - ty_ref[i, :])
        ry_ref[i, :] = r_ref[i, :] + jnp.where(there, 2.0 * flux, 0.0)
    beyond_ref[...] = beyond
    turn(ry_ref, rx_ref)
    left, right = sweep(
        lambda i: rx_ref[at(i), :], pr_ref, gr_ref, rr_ref, sep_ref, rd_ref, srd_ref, False
    )
    for k in range(3):
        out_ref[k] = net_ref[k]
    right = right + face_ref[2] * left
    frd_ref[0] = face_ref[0] * left
    frd_ref[1] = face_ref[3] * right
    out_ref[3] = face_ref[1] * left + face_ref[4] * right
    out_ref[4] = face_ref[5] * right


def lines_kernel(c_ref, south_ref, *outs):
    there = lax.axis_index("row") < lax.axis_size("row") - 1
    factor(c_ref, *outs, south=south_ref[...], there=there)


def level_kernel(axis, level, own_ref, other_ref, out_ref):
    left = (lax.axis_index(axis) >> level) % 2 == 0
    new = joined([own_ref[k] for k in range(5)], [other_ref[k] for k in range(5)], left)
    for k in range(5):
        out_ref[k] = new[k]


def middle_kernel(*refs):
    nets, refs = refs[:5], refs[5:]
    (
        face_ref, frd_ref, pr_ref, gr_ref, rd_ref, sep_ref, srd_ref, ty_ref,
        ypr_ref, ygr_ref, yrr_ref, ysep_ref, ynet_ref,
        yrd_ref, ysrd_ref, out_ref, wx_ref, wy_ref,
    ) = refs
    own, *others = ([r[k] for k in range(5)] for r in nets)
    ul, ur = ends(lax.axis_index("col"), own, others)
    ur = frd_ref[1] + face_ref[4] * ul + face_ref[5] * ur
    ul = frd_ref[0] + face_ref[1] * ul + face_ref[2] * ur

    def put(i, v):
        wx_ref[at(i), :] = v

    back(ul, ur, pr_ref, gr_ref, rd_ref, sep_ref, srd_ref, put, False)
    turn(wx_ref, wy_ref)
    left, right = sweep(
        lambda i: wy_ref[at(i), :] - 2.0 * ty_ref[at(i), :],
        ypr_ref, ygr_ref, yrr_ref, ysep_ref, yrd_ref, ysrd_ref, True,
    )
    for b in range(out_ref.shape[0]):
        for k in range(3):
            out_ref[b, k] = ynet_ref[k]
        out_ref[b, 3] = left
        out_ref[b, 4] = right


def last_kernel(
    all_ref, pr_ref, gr_ref, rd_ref, sep_ref, srd_ref, ty_ref, out_hbm, box, sem
):
    new_ref = box.reshape(Z * PITCH, N)
    me = lax.axis_index("row")
    place = lambda m: [all_ref[me ^ m, k] for k in range(5)]
    one, two = me % 2 == 0, me // 2 % 2 == 0
    own = place(0)
    far = joined(place(2), place(3), one)
    half = joined(joined(place(4), place(5), one), joined(place(6), place(7), one), two)
    ul, ur = ends(me, own, [place(1), far, half])

    def put(i, v):
        new_ref[strided(i), :] = v + ty_ref[at(i), :]

    copies = []

    def send(group):
        rows = pl.ds(group * (N // 4), N // 4)
        copies.append(
            pltpu.make_async_copy(box.at[:, rows, :], out_hbm.at[:, rows, :], sem.at[group])
        )
        copies[-1].start()

    back(ul, ur, pr_ref, gr_ref, rd_ref, sep_ref, srd_ref, put, True, 4, send)
    for copy in copies:
        copy.wait()


FIELD = (ROWS, N)
SPACED = (Z, PITCH, N)
NET = (5, Z, N)
PART = (3, Z, N)
SEPS = (3, CHUNKS, Z, N)
SEPD = (CHUNKS, Z, N)


def vm(shape):
    return VM(shape, F32)


def call(kernel, args, outs, scratch=(), flops=0, out_space=VM, outside=()):
    args = [pltpu.with_memory_space_constraint(a, VM) for a in args]
    whole = pl.BlockSpec(memory_space=VM)
    many = isinstance(outs, tuple)
    return pl.pallas_call(
        kernel,
        in_specs=[whole] * len(args) + [pl.BlockSpec(memory_space=pltpu.HBM)] * len(outside),
        out_specs=(whole,) * len(outs) if many else pl.BlockSpec(memory_space=out_space),
        out_shape=outs,
        scratch_shapes=list(scratch),
        cost_estimate=pl.CostEstimate(flops=flops, bytes_accessed=flops, transcendentals=0),
        compiler_params=pltpu.CompilerParams(vmem_limit_bytes=16 * 1024 * 1024),
    )(*args, *(pltpu.with_memory_space_constraint(a, pltpu.HBM) for a in outside))


def partner(x, axis, mask):
    return lax.ppermute(x, axis, [(i, i ^ mask) for i in range(lax.axis_size(axis))])


def spread_col(net, axis):
    others = []
    for level, mask in enumerate((1, 3, 7, 9)):
        others.append(partner(net, axis, mask))
        if level < 3:
            kernel = lambda *refs, level=level: level_kernel(axis, level, *refs)
            net = call(kernel, [net, others[-1]], vm(NET))
    return others


def local(t, region, source, mag, soft):
    n = lax.axis_size("row")
    edge = (2, Z, 8, N)
    up, down = pl.pallas_call(
        edge_kernel,
        in_specs=[pl.BlockSpec(memory_space=pltpu.HBM)] * 2,
        out_specs=(pl.BlockSpec(memory_space=VM),) * 2,
        out_shape=(vm((2, Z, N)),) * 2,
        scratch_shapes=[vm(edge), VM(edge, jnp.int32), pltpu.SemaphoreType.DMA((2, 2))],
    )(t, region)
    south = partner(down, "row", 1)
    north = lax.ppermute(up, "row", [(i, (i + i % 2 * 2 - 1) % n) for i in range(n)])
    par, ty, cy, r, pr, gr, rr, sep, net, face = call(
        first_kernel,
        [],
        (vm((6, Z, N)),) + (vm(FIELD),) * 6 + (vm(SEPS), vm(PART), vm((6, Z, N))),
        scratch=[
            vm(FIELD), vm(SPACED), VM(SPACED, jnp.int32), vm(SPACED),
            pltpu.SMEM((3,), F32), pltpu.SMEM((3,), F32),
            pltpu.SemaphoreType.DMA((2, 3)), pltpu.SemaphoreType.DMA((2,)),
        ],
        outside=[t, region, source, mag, soft],
        flops=20_000_000,
    )
    rd, srd, frd, own, beyond = call(
        side_kernel,
        [par, r, ty, cy, north, south, pr, gr, rr, sep, net, face],
        (vm(FIELD), vm(SEPD), vm((2, Z, N)), vm(NET), vm((Z, N))),
        scratch=[vm(FIELD), vm(FIELD)],
    )
    ypr, ygr, yrr, ysep, ynet = call(
        lines_kernel, [cy, beyond], (vm(FIELD),) * 3 + (vm(SEPS), vm(PART)), flops=5_000_000
    )
    others = spread_col(own, "col")
    yrd, ysrd, send = call(
        middle_kernel,
        [own] + others + [face, frd, pr, gr, rd, sep, srd, ty, ypr, ygr, yrr, ysep, ynet],
        (vm(FIELD), vm(SEPD), vm((n,) + NET)),
        scratch=[vm(FIELD), vm(FIELD)],
    )
    got = lax.all_to_all(send, "row", 0, 0, tiled=True)
    out = call(
        last_kernel,
        [got, ypr, ygr, yrd, ysep, ysrd, ty],
        jax.ShapeDtypeStruct((Z, N, N), F32),
        scratch=[vm(SPACED), pltpu.SemaphoreType.DMA((4,))],
        out_space=pl.ANY,
    )
    return out


def solution(mesh):
    specs = (P(None, "row", "col"),) * 3 + (P(), P())
    return jax.shard_map(
        local, mesh=mesh, in_specs=specs, out_specs=P(None, "row", "col"), check_vma=False
    )
```
